32 devices in a mesh: groups: 2 (over x), dp: 16 (over z, y, core).
Axes of the slice: x: 2, y: 2, z: 4, core: 2. Of those that a mesh axis runs over, the one named last changes fastest.
Arguments:
- queries: bfloat16 [32, 256, 1536], P(('groups', 'dp')), parts along dimension 0, may hold values from -8 to 8
- key_rows: bfloat16 [32, 256, 1536], P(('groups', 'dp')), parts along dimension 0, may hold values from -8 to 8
- value_rows: bfloat16 [32, 256, 1536], P(('groups', 'dp')), parts along dimension 0, may hold values from -24 to 24
- stream: bfloat16 [32, 256, 1536], P(('groups', 'dp')), parts along dimension 0, may hold values from -3 to 3
- earlier: bfloat16 [32, 256, 1536], P(('groups', 'dp')), parts along dimension 0, may hold values from -6 to 6
- out_weight: bfloat16 [1536, 1536], P('dp'), may hold values from -0.15625 to 0.15625
- pred_weight: bfloat16 [768, 1536], P('dp'), may hold values from -0.21875 to 0.21875
- decoder_hidden: bfloat16 [32, 8, 256, 768], P(('groups', 'dp')), parts along dimension 0, may hold values from -6 to 6
- kept_index: int32 [32, 8, 64], P(('groups', 'dp')), parts along dimension 0, may hold values from 0 to 255, as said below
Outputs:
- targets: float32 [32, 256, 1536], P(('groups', 'dp')), parts along dimension 0
- pred_grad: float32 [1536, 1536], P(('groups', 'dp')), parts along dimension 0
The draws below stay inside these ranges and needn't reach their ends.
There are 2 independent parts, one for each index of `groups`. The reference program is written for one: setup_inputs(seed, part) draws one part's arguments, and reference() takes and returns one part's arrays. A program takes and returns all parts, laid end to end along the dimension named above; an argument that names none is the same for every part. Nothing has to cross between parts.
Inputs may be any that keep to these rules, and one draw needn't show every extreme that they name: `kept_index`: within one clone of one image the 64 entries are distinct patch numbers.
All inputs are finite; a program needn't handle non-finite values.
Results may differ from the reference program's by a relative error of at most 0.002.
Values may be sent and summed in bfloat16 or wider, within the bound.
No kernel may reach another device: no remote copies, remote signals or barrier semaphores. Data moves between devices by JAX's collectives and lax.ppermute only.
A program may use at most 128 MiB of HBM per device.

```python
import math
import jax
import jax.numpy as jnp
from jax import lax

D = 1536
HEADS = 24
DEC = 768
PATCH = 256
CLONES = 8
KEEP = 64
TOP_K = 10
IMAGES = 16


def draw_queries(key, part):
    key = jax.random.fold_in(key, 11)
    base = jnp.clip(jax.random.normal(key, (IMAGES, PATCH, D), jnp.float32), -8.0, 8.0)
    return base.astype(jnp.bfloat16)


def draw_key_rows(key, part):
    key = jax.random.fold_in(key, 23)
    base = jnp.clip(jax.random.normal(key, (IMAGES, PATCH, D), jnp.float32), -8.0, 8.0)
    return base.astype(jnp.bfloat16)


def draw_kept_index(key, part):
    key = jax.random.fold_in(key, 29)
    several = jax.random.split(key, IMAGES * CLONES)
    orders = jax.vmap(lambda single: jax.random.permutation(single, PATCH))(several)
    return orders[:, :KEEP].reshape(IMAGES, CLONES, KEEP).astype(jnp.int32)


def spiked(array, stream_key, source, target, shards_of, factor):
    def block_of(axis_at):
        return (jnp.arange(array.shape[axis_at]) // (array.shape[axis_at] // shards_of)).reshape((-1,) + (1,) * (array.ndim - 1 - axis_at))

    near = jax.random.permutation(stream_key, shards_of)[block_of(target)]
    second = (block_of(target) + shards_of // 2) % shards_of
    return jnp.where((block_of(source) == near) | (block_of(source) == second), factor * array, array)


def level_of(own_key, dims, pieces, low, high):
    def one(dim, parts):
        heights = jax.random.uniform(jax.random.fold_in(jax.random.fold_in(own_key, 6), dim), (parts,), jnp.float32, low / len(pieces), high / len(pieces))
        return jnp.repeat(jnp.exp(heights), dims[dim] // parts).reshape((-1,) + (1,) * (len(dims) - dim - 1))

    loudness = one(*pieces[0])
    for cut in pieces[1:]:
        loudness = loudness * one(*cut)
    return loudness


def centred(stream_key, dims, scale, limit, cuts=(), held_as=jnp.bfloat16):
    drawn = jax.random.normal(stream_key, dims, jnp.float32) * scale
    if len(cuts) > 0:
        drawn = level_of(stream_key, dims, cuts, -0.22, 0.18) * drawn
    return jnp.clip(drawn, min=-limit, max=limit).astype(held_as)


def heavy_noise(rng, shape, scale, bound, pieces, heavy, kind=jnp.bfloat16):
    values = scale * jax.random.normal(rng, shape, jnp.float32)
    if pieces:
        values = values * level_of(rng, shape, pieces, -0.22, 0.18)
    return jnp.clip(spiked(values, jax.random.fold_in(rng, 3), *heavy), -bound, bound).astype(kind)


def setup_inputs(seed: int = 0, part: int = 0) -> dict:
    seeds = jax.random.split(jax.random.key(seed), 10)
    part_splits = jax.random.split(jax.random.fold_in(seeds[9], part), 10)
    queries = draw_queries(jax.random.fold_in(jax.random.fold_in(seeds[9], part), 71), part)
    key_rows = draw_key_rows(jax.random.fold_in(jax.random.fold_in(seeds[9], part), 71), part)
    value_rows = centred(part_splits[2], (IMAGES, PATCH, D), 4.0, 24.0, ((0, 16),))
    stream = centred(part_splits[3], (IMAGES, PATCH, D), 0.5, 3.0, ((0, 16),))
    earlier = centred(part_splits[4], (IMAGES, PATCH, D), 1.0, 6.0, ((0, 16),))
    out_weight = centred(seeds[5], (D, D), D ** -0.5, 0.15625, ((0, 16),))
    pred_weight = centred(seeds[6], (DEC, D), DEC ** -0.5, 0.21875, ((0, 16),))
    decoder_hidden = heavy_noise(part_splits[7], (IMAGES, CLONES, PATCH, DEC), 1.0, 6.0, ((0, 16),), (0, 3, 16, 2.0))
    kept_index = draw_kept_index(jax.random.fold_in(jax.random.fold_in(seeds[9], part), 71), part)
    return dict(queries=queries, key_rows=key_rows, value_rows=value_rows, stream=stream, earlier=earlier, out_weight=out_weight, pred_weight=pred_weight, decoder_hidden=decoder_hidden, kept_index=kept_index)


def teacher_image(queries, key_rows, value_rows, stream, earlier, out_weight):
    head_size = D // HEADS
    query_f = queries.astype(jnp.float32).reshape(PATCH, HEADS, head_size)
    key_f = key_rows.astype(jnp.float32).reshape(PATCH, HEADS, head_size)
    value_f = value_rows.astype(jnp.float32).reshape(PATCH, HEADS, head_size)
    scores = jnp.einsum('phd,khd->hpk', query_f, key_f) / math.sqrt(head_size)
    attn_probs = jax.nn.softmax(scores, axis=-1).astype(jnp.bfloat16)
    mixed = jnp.einsum('hpk,khd->phd', attn_probs.astype(jnp.float32), value_f)
    mixed = mixed.reshape(PATCH, D).astype(jnp.bfloat16)
    layer_out = stream.astype(jnp.float32) + jnp.dot(mixed, out_weight, preferred_element_type=jnp.float32)
    center = lax.optimization_barrier(jnp.mean(layer_out, axis=0, keepdims=True))
    spread = lax.optimization_barrier(jnp.mean((layer_out - center) ** 2, axis=0, keepdims=True))
    normed = (layer_out - center) / jnp.sqrt(spread + 1e-05)
    blend = ((TOP_K - 1) * earlier.astype(jnp.float32) + normed) / TOP_K
    middle = lax.optimization_barrier(jnp.mean(blend, axis=1, keepdims=True))
    breadth = lax.optimization_barrier(jnp.mean((blend - middle) ** 2, axis=1, keepdims=True))
    return (blend - middle) / jnp.sqrt(breadth + 1e-06)

def student_image(decoder_hidden, kept_index, targets, pred_weight):
    dec_rows = decoder_hidden.reshape(CLONES * PATCH, DEC)
    predicted = jnp.dot(dec_rows, pred_weight, preferred_element_type=jnp.float32)
    positions = jnp.arange(PATCH, dtype=jnp.int32)
    covered = jnp.any(kept_index[:, :, None] == positions[None, None, :], axis=1)
    masked = jnp.where(covered, 0.0, 1.0).astype(jnp.float32)
    errors = predicted.reshape(CLONES, PATCH, D) - targets[None]
    scaled = 2.0 / (math.sqrt(D) * CLONES) * masked[:, :, None] * errors
    scaled = scaled.reshape(CLONES * PATCH, D).astype(jnp.bfloat16)
    return lax.dot_general(dec_rows, scaled, (((0,), (0,)), ((), ())), preferred_element_type=jnp.float32)

def reference(queries, key_rows, value_rows, stream, earlier, out_weight, pred_weight, decoder_hidden, kept_index):

    def advance(running, items):
        query_one, key_one, value_one, stream_one, earlier_one, hidden_one, kept_one = items
        target_one = teacher_image(query_one, key_one, value_one, stream_one, earlier_one, out_weight)
        running = running + student_image(hidden_one, kept_one, target_one, pred_weight)
        return (running, target_one)
    start_grad = jnp.zeros((DEC, D), jnp.float32)
    pred_grad, targets = lax.scan(advance, start_grad, (queries, key_rows, value_rows, stream, earlier, decoder_hidden, kept_index))
    return (targets, pred_grad)
```

```python
import functools
import math

import jax
import jax.numpy as jnp
from jax import lax
from jax.experimental import pallas as pl
from jax.experimental.pallas import tpu as pltpu
from jax.sharding import PartitionSpec as P

HEADS = 24
TOP_K = 10
AXES = ("groups", "dp")
VMEM = 48 * 1024 * 1024
CORE, NEXT_Y, NEXT_Z, FAR_Z = 1, 2, 4, 8
TAIL = 16


def call(kernel, out_shape, *, name, grid=(1,), in_specs, out_specs, scratch=(), flops=0, nbytes=0):
    return pl.pallas_call(
        kernel,
        out_shape=out_shape,
        grid_spec=pltpu.PrefetchScalarGridSpec(
            num_scalar_prefetch=1,
            grid=grid,
            in_specs=in_specs,
            out_specs=out_specs,
            scratch_shapes=scratch,
        ),
        compiler_params=pltpu.CompilerParams(vmem_limit_bytes=VMEM),
        cost_estimate=pl.CostEstimate(flops=flops, bytes_accessed=nbytes, transcendentals=0),
        name=name,
    )


def whole(shape):
    return pl.BlockSpec(shape, lambda i, s: (0,) * len(shape))


def contract_rows(a, b):
    return lax.dot_general(a, b, (((0,), (0,)), ((), ())), preferred_element_type=jnp.float32)


def attention_kernel(where_ref, q_ref, k_ref, v_ref, out_ref, *, size):
    mixed = []
    for j in range(q_ref.shape[1] // size):
        cols = slice(j * size, (j + 1) * size)
        q = q_ref[:, cols] * jnp.asarray(1.0 / math.sqrt(size), q_ref.dtype)
        scores = lax.dot_general(
            q, k_ref[:, cols], (((1,), (1,)), ((), ())), preferred_element_type=jnp.float32
        )
        top = jnp.max(scores, axis=1, keepdims=True)
        weights = jnp.exp(scores - top)
        weights = weights / jnp.sum(weights, axis=1, keepdims=True)
        mixed.append(
            jnp.dot(weights.astype(jnp.bfloat16), v_ref[:, cols], preferred_element_type=jnp.float32)
        )
    out_ref[...] = jnp.concatenate(mixed, axis=1).astype(out_ref.dtype)


def attention(where, q, k, v):
    patches, width = q.shape
    size = width // HEADS
    lanes = 2 * size
    spec = pl.BlockSpec((patches, lanes), lambda i, s: (0, i))
    return call(
        functools.partial(attention_kernel, size=size),
        jax.ShapeDtypeStruct((patches, width), jnp.bfloat16),
        name="attention",
        grid=(width // lanes,),
        in_specs=[spec] * 3,
        out_specs=spec,
        flops=4 * patches * patches * width * 4,
        nbytes=8 * patches * width,
    )(where, q, k, v)


def gram_kernel(where_ref, hidden_ref, kept_ref, gram_ref, sum_ref, total):
    step = pl.program_id(0)
    patches = hidden_ref.shape[2]
    kept = kept_ref[pl.ds(step, 1), :]
    positions = lax.broadcasted_iota(jnp.int32, (patches, kept.shape[1]), 0)
    covered = jnp.max(jnp.where(positions == kept, 1.0, 0.0), axis=1, keepdims=True)
    rows = hidden_ref[0, 0]
    rows = jnp.where(covered > 0.5, jnp.zeros_like(rows), rows)

    @pl.when(step == 0)
    def _():
        gram_ref[...] = jnp.zeros_like(gram_ref)
        total[...] = jnp.zeros_like(total)

    gram_ref[...] += contract_rows(rows, rows)
    total[...] += rows.astype(jnp.float32)

    @pl.when(step == pl.num_programs(0) - 1)
    def _():
        sum_ref[...] = total[...].astype(sum_ref.dtype)


def gram(where, hidden, kept):
    _, clones, patches, width = hidden.shape
    return call(
        gram_kernel,
        (
            jax.ShapeDtypeStruct((width, width), jnp.float32),
            jax.ShapeDtypeStruct((patches, width), jnp.bfloat16),
        ),
        name="gram",
        grid=(clones,),
        in_specs=[
            pl.BlockSpec((1, 1, patches, width), lambda i, s: (0, i, 0, 0)),
            whole(kept.shape),
        ],
        out_specs=(whole((width, width)), whole((patches, width))),
        scratch=[pltpu.VMEM((patches, width), jnp.float32)],
        flops=2 * clones * patches * width * width,
        nbytes=2 * clones * patches * width + 4 * width * width,
    )(where, hidden, kept)


def put_in_order(where_ref, pieces, full):
    core, chip = where_ref[0], where_ref[1]
    if len(pieces) == 1:
        full[...] = pieces[0][...]
        return
    for k, piece in enumerate(pieces):
        rows = piece.shape[0] // 2
        base = (chip ^ k) * 2
        for j in range(2):
            at = pl.multiple_of((base + (core ^ j)) * rows, rows)
            full[pl.ds(at, rows), :] = piece[j * rows : (j + 1) * rows, :]


def branch_kernel(
    where_ref, mixed_own, mixed_other, stream_own, earlier_own, others, *rest
):
    *pieces, blend_ref, stats_ref, full = rest
    put_in_order(where_ref, pieces, full)
    patches, half = stream_own.shape
    streams = (stream_own[...], others[0])
    earliers = (earlier_own[...], others[1])
    for i, mixed in enumerate((mixed_own, mixed_other)):
        layer_out = streams[i].astype(jnp.float32) + jnp.dot(
            mixed[...], full[...], preferred_element_type=jnp.float32
        )
        center = jnp.mean(layer_out, axis=0, keepdims=True)
        away = layer_out - center
        spread = jnp.mean(away * away, axis=0, keepdims=True)
        normed = away / jnp.sqrt(spread + 1e-05)
        blend = ((TOP_K - 1) * earliers[i].astype(jnp.float32) + normed) / TOP_K
        rows = slice(i * patches, (i + 1) * patches)
        blend_ref[rows, :] = blend
        middle = jnp.mean(blend, axis=1, keepdims=True)
        off = blend - middle
        squares = jnp.sum(off * off, axis=1, keepdims=True)
        lane = lax.broadcasted_iota(jnp.int32, (patches, 128), 1)
        stats_ref[rows, :] = jnp.where(lane < 64, middle, squares)


def branch(where, mixed_own, mixed_other, stream, earlier, others, pieces):
    patches, width = mixed_own.shape
    half = width // 2
    own_half = pl.BlockSpec((patches, half), lambda i, s: (0, s[0]))
    return call(
        branch_kernel,
        (
            jax.ShapeDtypeStruct((2 * patches, half), jnp.float32),
            jax.ShapeDtypeStruct((2 * patches, 128), jnp.float32),
        ),
        name="branch",
        in_specs=[whole((patches, width))] * 2
        + [own_half] * 2
        + [whole((2, patches, half))]
        + [whole(p.shape) for p in pieces],
        out_specs=(whole((2 * patches, half)), whole((2 * patches, 128))),
        scratch=[pltpu.VMEM((width, half), jnp.bfloat16)],
        flops=4 * patches * width * half,
        nbytes=12 * patches * width + 2 * width * half,
    )(where, mixed_own, mixed_other, stream, earlier, others, *pieces)


def predict_kernel(where_ref, gram_own, gram_other, *rest):
    *pieces, out_ref, full = rest
    put_in_order(where_ref, pieces, full)
    both = gram_own[...] + gram_other[...]
    high = both.astype(jnp.bfloat16)
    low = (both - high.astype(jnp.float32)).astype(jnp.bfloat16)
    out_ref[...] = jnp.dot(high, full[...], preferred_element_type=jnp.float32) + jnp.dot(
        low, full[...], preferred_element_type=jnp.float32
    )


def predict(where, gram_own, gram_other, pieces):
    width, half = gram_own.shape[0], pieces[0].shape[1]
    return call(
        predict_kernel,
        jax.ShapeDtypeStruct((width, half), jnp.float32),
        name="predict",
        in_specs=[whole((width, width))] * 2 + [whole(p.shape) for p in pieces],
        out_specs=whole((width, half)),
        scratch=[pltpu.VMEM((width, half), jnp.bfloat16)],
        flops=4 * width * width * half,
        nbytes=8 * width * width + 6 * width * half,
    )(where, gram_own, gram_other, *pieces)


def encode(values, out_ref):
    rows = values.shape[0]
    top = jnp.max(jnp.abs(values), axis=0, keepdims=True)
    power = jnp.ceil(jnp.log2(jnp.maximum(top, 1e-30))) - 15.0
    codes = jnp.clip(jnp.round(values * jnp.exp2(-power)), -32767.0, 32767.0)
    out_ref[:rows, :] = codes.astype(jnp.int32).astype(jnp.int16)
    out_ref[rows:, :] = jnp.broadcast_to(power, (TAIL, values.shape[1])).astype(jnp.int32).astype(jnp.int16)


def decode(codes):
    rows = codes.shape[0] - TAIL
    power = codes[rows:, :].astype(jnp.int32).astype(jnp.float32)[:1]
    return codes[:rows, :].astype(jnp.int32).astype(jnp.float32) * jnp.exp2(power)


def targets_kernel(where_ref, blend, stats, stats_other, sum_own, sum_other, product, own_ref, other_ref, grad_ref):
    patches, width = blend.shape[0] // 2, 2 * blend.shape[1]
    results = []
    for i, (out, features) in enumerate(((own_ref, sum_own), (other_ref, sum_other))):
        mine = stats[i * patches : (i + 1) * patches, :]
        theirs = stats_other[(1 - i) * patches : (2 - i) * patches, :]
        gap = mine[:, :1] - theirs[:, :1]
        middle = 0.5 * (mine[:, :1] + theirs[:, :1])
        squares = mine[:, 64:65] + theirs[:, 64:65] + (width / 4) * gap * gap
        root = 1.0 / jnp.sqrt(squares / width + 1e-06)
        target = (blend[i * patches : (i + 1) * patches, :] - middle) * root
        out[...] = target
        results.append(contract_rows(features[...], target.astype(jnp.bfloat16)))
    grad = product[...] - (results[0] + results[1])
    if len(grad_ref.shape) == 3:
        chips, rows = grad_ref.shape[0], grad_ref.shape[1] - TAIL
        for k in range(chips):
            encode(grad[k * rows : (k + 1) * rows, :], grad_ref.at[k])
    else:
        grad_ref[...] = grad


def targets_and_term(where, blend, stats, stats_other, sum_own, sum_other, product, grad_shape):
    patches, half = blend.shape[0] // 2, blend.shape[1]
    width = product.shape[0]
    inputs = (blend, stats, stats_other, sum_own, sum_other, product)
    return call(
        targets_kernel,
        (
            jax.ShapeDtypeStruct((patches, half), jnp.float32),
            jax.ShapeDtypeStruct((patches, half), jnp.float32),
            grad_shape,
        ),
        name="targets",
        in_specs=[whole(x.shape) for x in inputs],
        out_specs=(whole((patches, half)), whole((patches, half)), whole(grad_shape.shape)),
        flops=4 * patches * width * half,
        nbytes=16 * patches * half + 6 * width * half,
    )(where, *inputs)


def sum_kernel(where_ref, codes, out_ref, *, scale):
    total = decode(codes[0])
    for k in range(1, codes.shape[0]):
        total = total + decode(codes[k])
    out_ref[...] = (total * scale).reshape(out_ref.shape)


def sum_terms(where, codes, scale):
    chips, rows, half = codes.shape
    shape = (2, (rows - TAIL) // 2, half)
    return call(
        functools.partial(sum_kernel, scale=scale),
        jax.ShapeDtypeStruct(shape, jnp.float32),
        name="sum_terms",
        in_specs=[whole(codes.shape)],
        out_specs=whole(shape),
        flops=chips * rows * half,
        nbytes=2 * chips * rows * half,
    )(where, codes)


def on_device(
    mesh_shape,
    queries,
    key_rows,
    value_rows,
    stream,
    earlier,
    out_weight,
    pred_weight,
    decoder_hidden,
    kept_index,
):
    groups, parts = mesh_shape["groups"], mesh_shape["dp"]
    chips = parts // 2
    _, patches, width = queries.shape
    clones = decoder_hidden.shape[1]
    half = width // 2
    me = lax.axis_index("dp")
    core, chip = me % 2, me // 2
    where = jnp.stack([core, chip]).astype(jnp.int32)
    same_core = [[2 * k + j for k in range(chips)] for j in range(2)]

    def swap(x, bits):
        pairs = [(g * parts + i, g * parts + (i ^ bits)) for g in range(groups) for i in range(parts)]
        return lax.ppermute(x, AXES, pairs)

    def my_half(x):
        return lax.dynamic_slice_in_dim(x, core * half, half, axis=-1)

    def other_half(x):
        return lax.dynamic_slice_in_dim(x, (1 - core) * half, half, axis=-1)

    out_piece = jnp.concatenate([my_half(out_weight), swap(other_half(out_weight), CORE)], axis=0)
    pred_piece = jnp.concatenate([my_half(pred_weight), swap(other_half(pred_weight), CORE)], axis=0)

    def gathered(piece):
        rows = piece.shape[0] // 2
        got = lax.all_gather(piece, "dp", axis_index_groups=same_core).reshape(chips, 2, rows, half)
        got = jnp.where(core == 0, got, got[:, ::-1])
        return [got.reshape(chips * 2 * rows, half)]

    by_pairs = chips == 8
    if by_pairs:
        z1, z2, y0 = swap(out_piece, NEXT_Z), swap(out_piece, FAR_Z), swap(out_piece, NEXT_Y)
        z3 = swap(z2, NEXT_Z)
        y1, y2, y3 = swap(z1, NEXT_Y), swap(z2, NEXT_Y), swap(z3, NEXT_Y)
        out_pieces = [out_piece, y0, z1, y1, z2, y2, z3, y3]
    else:
        out_pieces = gathered(out_piece)
    pred_pieces = gathered(pred_piece)

    mixed_own = attention(where, queries[0], key_rows[0], value_rows[0])
    gram_own, sum_own = gram(where, decoder_hidden, kept_index[0])
    mixed_other = swap(mixed_own, CORE)
    others = swap(jnp.concatenate([other_half(stream), other_half(earlier)], axis=0), CORE)
    sum_other = swap(sum_own, CORE)
    gram_other = swap(gram_own, CORE)

    blend, stats = branch(where, mixed_own, mixed_other, stream[0], earlier[0], others, out_pieces)
    stats_other = swap(stats, CORE)
    product = predict(where, gram_own, gram_other, pred_pieces)

    dec = product.shape[0]
    rows = dec // chips
    if by_pairs:
        grad_shape = jax.ShapeDtypeStruct((chips, rows + TAIL, half), jnp.int16)
    else:
        grad_shape = jax.ShapeDtypeStruct((dec, half), jnp.float32)
    target_own, target_other, term = targets_and_term(
        where, blend, stats, stats_other, sum_own, sum_other, product, grad_shape
    )
    target_rest = swap(target_other, CORE)
    scale = 2.0 / (math.sqrt(width) * clones)
    if by_pairs:
        codes = lax.all_to_all(term, "dp", 0, 0, axis_index_groups=same_core)
        summed = sum_terms(where, codes, scale)
    else:
        summed = lax.psum_scatter(
            term, "dp", scatter_dimension=0, tiled=True, axis_index_groups=same_core
        )
        summed = (summed * scale).reshape(2, rows // 2, half)

    def side_by_side(mine, theirs):
        return jnp.where(
            core == 0,
            jnp.concatenate([mine, theirs], axis=1),
            jnp.concatenate([theirs, mine], axis=1),
        )

    targets = side_by_side(target_own, target_rest)[None]
    keep = lax.dynamic_index_in_dim(summed, core, 0, keepdims=False)
    send = lax.dynamic_index_in_dim(summed, 1 - core, 0, keepdims=False)
    return targets, side_by_side(keep, swap(send, CORE))


def solution(mesh):
    by_image = P(AXES, None, None)
    return jax.shard_map(
        functools.partial(on_device, dict(mesh.shape)),
        mesh=mesh,
        in_specs=(
            by_image,
            by_image,
            by_image,
            by_image,
            by_image,
            P("dp", None),
            P("dp", None),
            P(AXES, None, None, None),
            by_image,
        ),
        out_specs=(by_image, P(AXES, None)),
        check_vma=False,
    )
```

```python
import functools
import math

import jax
import jax.numpy as jnp
from jax import lax
from jax.experimental import pallas as pl
from jax.experimental.pallas import tpu as pltpu
from jax.sharding import PartitionSpec as P

HEADS = 24
TOP_K = 10
AXES = ("groups", "dp")
VMEM = 56 * 1024 * 1024
CORE, NEXT_Y, NEXT_Z, FAR_Z = 1, 2, 4, 8
LINE = 4
CUTS = 2
TAIL = 16


def call(kernel, out_shape, *, name, grid=(1,), in_specs, out_specs, scratch=(), flops=0, nbytes=0):
    return pl.pallas_call(
        kernel,
        out_shape=out_shape,
        grid_spec=pltpu.PrefetchScalarGridSpec(
            num_scalar_prefetch=1,
            grid=grid,
            in_specs=in_specs,
            out_specs=out_specs,
            scratch_shapes=scratch,
        ),
        compiler_params=pltpu.CompilerParams(vmem_limit_bytes=VMEM),
        cost_estimate=pl.CostEstimate(flops=flops, bytes_accessed=nbytes, transcendentals=0),
        name=name,
    )


def whole(shape):
    return pl.BlockSpec(shape, lambda i, s: (0,) * len(shape))


def contract_rows(a, b):
    return lax.dot_general(a, b, (((0,), (0,)), ((), ())), preferred_element_type=jnp.float32)


def attention_kernel(where_ref, q_ref, k_ref, v_ref, out_ref, *, size):
    mixed = []
    for j in range(q_ref.shape[1] // size):
        cols = slice(j * size, (j + 1) * size)
        q = q_ref[:, cols] * jnp.asarray(1.0 / math.sqrt(size), q_ref.dtype)
        scores = lax.dot_general(
            k_ref[:, cols], q, (((1,), (1,)), ((), ())), preferred_element_type=jnp.float32
        )
        weights = jnp.exp(scores - jnp.max(scores, axis=0, keepdims=True))
        weights = weights * (1.0 / jnp.sum(weights, axis=0, keepdims=True))
        mixed.append(contract_rows(weights.astype(jnp.bfloat16), v_ref[:, cols]))
    out_ref[...] = jnp.concatenate(mixed, axis=1).astype(out_ref.dtype)


def attention(where, q, k, v):
    patches, width = q.shape
    return call(
        functools.partial(attention_kernel, size=width // HEADS),
        jax.ShapeDtypeStruct((patches, width), jnp.bfloat16),
        name="attention",
        in_specs=[whole((patches, width))] * 3,
        out_specs=whole((patches, width)),
        flops=4 * patches * patches * width * 4,
        nbytes=8 * patches * width,
    )(where, q, k, v)


def gram_kernel(where_ref, hidden_ref, kept_ref, *rest, parted):
    *gram_refs, sum_ref, rows_all, total = rest
    clones, patches = hidden_ref.shape[1], hidden_ref.shape[2]
    positions = lax.broadcasted_iota(jnp.int32, (patches, kept_ref.shape[1]), 0)
    sums = None
    for i in range(clones):
        kept = kept_ref[i : i + 1, :]
        covered = jnp.max(jnp.where(positions == kept, 1.0, 0.0), axis=1, keepdims=True)
        rows = hidden_ref[0, i]
        rows = jnp.where(covered > 0.5, jnp.zeros_like(rows), rows)
        rows_all[i * patches : (i + 1) * patches, :] = rows
        wide = rows.astype(jnp.float32)
        sums = wide if sums is None else sums + wide
    sum_ref[...] = sums.astype(sum_ref.dtype)
    if not parted:
        gram_refs[0][...] = contract_rows(rows_all[...], rows_all[...])
        return
    total[...] = contract_rows(rows_all[...], rows_all[...])
    mine, theirs = gram_refs
    core = where_ref[0]
    chips, rows = parted
    for k in range(chips):
        for ref, c in ((mine, core), (theirs, 1 - core)):
            at = pl.multiple_of((2 * k + c) * rows, rows)
            ref[k * rows : (k + 1) * rows, :] = total[pl.ds(at, rows), :]


def gram(where, hidden, kept, parted):
    _, clones, patches, width = hidden.shape
    grams = [(width // 2, width)] * 2 if parted else [(width, width)]
    return call(
        functools.partial(gram_kernel, parted=parted),
        tuple(jax.ShapeDtypeStruct(g, jnp.float32) for g in grams)
        + (jax.ShapeDtypeStruct((patches, width), jnp.bfloat16),),
        name="gram",
        in_specs=[whole(hidden.shape), whole(kept.shape)],
        out_specs=tuple(whole(g) for g in grams) + (whole((patches, width)),),
        scratch=[
            pltpu.VMEM((clones * patches, width), jnp.bfloat16),
            pltpu.VMEM((width, width), jnp.float32),
        ],
        flops=2 * clones * patches * width * width,
        nbytes=2 * clones * patches * width + 4 * width * width,
    )(where, hidden, kept)


def put_in_order(where_ref, pieces, full):
    core, chip = where_ref[0], where_ref[1]
    if len(pieces) == 1:
        full[...] = pieces[0][...]
        return
    for k, piece in enumerate(pieces):
        rows = piece.shape[0] // 2
        base = (chip ^ k) * 2
        for j in range(2):
            at = pl.multiple_of((base + (core ^ j)) * rows, rows)
            full[pl.ds(at, rows), :] = piece[j * rows : (j + 1) * rows, :]


def branch_kernel(
    where_ref, mixed_own, mixed_other, stream_own, earlier_own, others, *rest
):
    *pieces, blend_ref, stats_ref, full = rest
    put_in_order(where_ref, pieces, full)
    patches, half = stream_own.shape
    streams = (stream_own[...], others[0])
    earliers = (earlier_own[...], others[1])
    for i, mixed in enumerate((mixed_own, mixed_other)):
        layer_out = streams[i].astype(jnp.float32) + jnp.dot(
            mixed[...], full[...], preferred_element_type=jnp.float32
        )
        center = jnp.mean(layer_out, axis=0, keepdims=True)
        away = layer_out - center
        spread = jnp.mean(away * away, axis=0, keepdims=True)
        normed = away / jnp.sqrt(spread + 1e-05)
        blend = ((TOP_K - 1) * earliers[i].astype(jnp.float32) + normed) / TOP_K
        rows = slice(i * patches, (i + 1) * patches)
        blend_ref[rows, :] = blend
        middle = jnp.mean(blend, axis=1, keepdims=True)
        off = blend - middle
        squares = jnp.sum(off * off, axis=1, keepdims=True)
        lane = lax.broadcasted_iota(jnp.int32, (patches, 128), 1)
        stats_ref[rows, :] = jnp.where(lane < 64, middle, squares)


def branch(where, mixed_own, mixed_other, stream, earlier, others, pieces):
    patches, width = mixed_own.shape
    half = width // 2
    own_half = pl.BlockSpec((patches, half), lambda i, s: (0, s[0]))
    return call(
        branch_kernel,
        (
            jax.ShapeDtypeStruct((2 * patches, half), jnp.float32),
            jax.ShapeDtypeStruct((2 * patches, 128), jnp.float32),
        ),
        name="branch",
        in_specs=[whole((patches, width))] * 2
        + [own_half] * 2
        + [whole((2, patches, half))]
        + [whole(p.shape) for p in pieces],
        out_specs=(whole((2 * patches, half)), whole((2 * patches, 128))),
        scratch=[pltpu.VMEM((width, half), jnp.bfloat16)],
        flops=4 * patches * width * half,
        nbytes=12 * patches * width + 2 * width * half,
    )(where, mixed_own, mixed_other, stream, earlier, others, *pieces)


def encode(values, out_ref):
    rows = values.shape[0]
    top = jnp.max(jnp.abs(values), axis=0, keepdims=True)
    power = jnp.ceil(jnp.log2(jnp.maximum(top, 1e-30))) - 15.0
    codes = jnp.clip(jnp.round(values * jnp.exp2(-power)), -32767.0, 32767.0)
    out_ref[:rows, :] = codes.astype(jnp.int32).astype(jnp.int16)
    out_ref[rows:, :] = jnp.broadcast_to(power, (TAIL, values.shape[1])).astype(jnp.int32).astype(jnp.int16)


def decode(codes):
    rows = codes.shape[0] - TAIL
    power = codes[rows:, :].astype(jnp.int32).astype(jnp.float32)[:1]
    return codes[:rows, :].astype(jnp.int32).astype(jnp.float32) * jnp.exp2(power)


def halve(values, where_ref, send_ref, keep_ref):
    rows = keep_ref.shape[0] // LINE
    y = where_ref[1] % 2

    def blocks(of):
        return [values[pl.ds(pl.multiple_of((2 * z + of) * rows, rows), rows), :] for z in range(LINE)]

    keep_ref[...] = jnp.concatenate(blocks(y), axis=0)
    encode(jnp.concatenate(blocks(1 - y), axis=0), send_ref)


def halved_shapes(rows, width):
    return (
        jax.ShapeDtypeStruct((rows // 2 + TAIL, width), jnp.int16),
        jax.ShapeDtypeStruct((rows // 2, width), jnp.float32),
    )


def first_kernel(where_ref, mine, theirs, send_ref, keep_ref, total):
    total[...] = mine[...] + theirs[...]
    halve(total, where_ref, send_ref, keep_ref)


def first_step(where, mine, theirs):
    shapes = halved_shapes(*mine.shape)
    return call(
        first_kernel,
        shapes,
        name="first_step",
        in_specs=[whole(mine.shape)] * 2,
        out_specs=tuple(whole(x.shape) for x in shapes),
        scratch=[pltpu.VMEM(mine.shape, jnp.float32)],
        flops=mine.size,
        nbytes=11 * mine.size,
    )(where, mine, theirs)


def second_kernel(where_ref, keep, codes, own_ref, *rest):
    *send_refs, total = rest
    rows = own_ref.shape[0]
    z = where_ref[1] // 2
    total[...] = keep[...] + decode(codes[...])

    def block(of):
        return total[pl.ds(pl.multiple_of(of * rows, rows), rows), :]

    own_ref[...] = block(z)
    for m, ref in enumerate(send_refs):
        encode(block(z ^ (m + 1)), ref)


def second_step(where, keep, codes):
    rows, width = keep.shape[0] // LINE, keep.shape[1]
    shapes = (jax.ShapeDtypeStruct((rows, width), jnp.float32),) + (
        jax.ShapeDtypeStruct((rows + TAIL, width), jnp.int16),
    ) * (LINE - 1)
    return call(
        second_kernel,
        shapes,
        name="second_step",
        in_specs=[whole(keep.shape), whole(codes.shape)],
        out_specs=tuple(whole(x.shape) for x in shapes),
        scratch=[pltpu.VMEM(keep.shape, jnp.float32)],
        flops=keep.size,
        nbytes=9 * keep.size,
    )(where, keep, codes)


def last_kernel(where_ref, own, c1, c2, c3, *out_refs, scale):
    total = own[...] + (decode(c1[...]) + (decode(c2[...]) + decode(c3[...])))
    if scale is None:
        (pair,) = out_refs
        rows = total.shape[0]
        high = total.astype(jnp.bfloat16)
        pair[:rows, :] = high
        pair[rows:, :] = (total - high.astype(jnp.float32)).astype(jnp.bfloat16)
        return
    keep, send = out_refs
    rows = keep.shape[0]
    first, second = total[:rows, :] * scale, total[rows:, :] * scale
    mine_first = where_ref[0] == 0
    keep[...] = jnp.where(mine_first, first, second)
    send[...] = jnp.where(mine_first, second, first)


def last_step(where, own, codes, scale=None):
    rows, width = own.shape
    if scale is None:
        shapes = (jax.ShapeDtypeStruct((2 * rows, width), jnp.bfloat16),)
    else:
        shapes = (jax.ShapeDtypeStruct((rows // 2, width), jnp.float32),) * 2
    return call(
        functools.partial(last_kernel, scale=scale),
        shapes,
        name="last_step",
        in_specs=[whole(own.shape)] + [whole(c.shape) for c in codes],
        out_specs=tuple(whole(x.shape) for x in shapes),
        flops=8 * own.size,
        nbytes=14 * own.size,
    )(where, own, *codes)


def targets_kernel(where_ref, blend, stats, stats_other, sum_own, sum_other, grams, weights, own_ref, other_ref, *rest, width):
    patches = own_ref.shape[0]
    grad = contract_rows(grams[...], weights[...])
    for i, (out, features) in enumerate(((own_ref, sum_own), (other_ref, sum_other))):
        mine = stats[i * patches : (i + 1) * patches, :]
        theirs = stats_other[(1 - i) * patches : (2 - i) * patches, :]
        gap = mine[:, :1] - theirs[:, :1]
        middle = 0.5 * (mine[:, :1] + theirs[:, :1])
        squares = mine[:, 64:65] + theirs[:, 64:65] + (width / 4) * gap * gap
        root = 1.0 / jnp.sqrt(squares / width + 1e-06)
        target = (blend[i * patches : (i + 1) * patches, :] - middle) * root
        out[...] = target
        grad = grad - contract_rows(features[...], target.astype(jnp.bfloat16))
    if len(rest) == 1:
        rest[0][...] = grad
        return
    send_ref, keep_ref, total = rest
    total[...] = grad
    halve(total, where_ref, send_ref, keep_ref)


def targets_and_term(where, blend, stats, stats_other, sum_own, sum_other, grams, weights, cut, coded):
    j, n = cut
    patches, columns = blend.shape[0] // 2, blend.shape[1] // n
    dec = grams.shape[1]
    shapes = (jax.ShapeDtypeStruct((patches, columns), jnp.float32),) * 2
    if coded:
        shapes += halved_shapes(dec, columns)
    else:
        shapes += (jax.ShapeDtypeStruct((dec, columns), jnp.float32),)

    def part(x):
        return pl.BlockSpec((x.shape[0], columns), lambda i, s: (0, j))

    inputs = (blend, stats, stats_other, sum_own, sum_other, grams, weights)
    return call(
        functools.partial(targets_kernel, width=2 * blend.shape[1]),
        shapes,
        name="targets",
        in_specs=[part(blend)] + [whole(x.shape) for x in inputs[1:-1]] + [part(weights)],
        out_specs=tuple(whole(x.shape) for x in shapes),
        scratch=[pltpu.VMEM((dec, columns), jnp.float32)] if coded else [],
        flops=4 * patches * dec * columns,
        nbytes=16 * patches * columns + 6 * dec * columns,
    )(where, *inputs)


def after(x, *others):
    return lax.optimization_barrier((x,) + others)[0]


def on_device(
    mesh_shape,
    queries,
    key_rows,
    value_rows,
    stream,
    earlier,
    out_weight,
    pred_weight,
    decoder_hidden,
    kept_index,
):
    groups, parts = mesh_shape["groups"], mesh_shape["dp"]
    chips = parts // 2
    patches, width = queries.shape[1:]
    clones, dec = decoder_hidden.shape[1], decoder_hidden.shape[3]
    half = width // 2
    scale = 2.0 / (math.sqrt(width) * clones)
    me = lax.axis_index("dp")
    core, chip = me % 2, me // 2
    where = jnp.stack([core, chip]).astype(jnp.int32)
    same_core = [[2 * k + j for k in range(chips)] for j in range(2)]
    by_pairs = chips == 2 * LINE

    def swap(x, bits):
        pairs = [(g * parts + i, g * parts + (i ^ bits)) for g in range(groups) for i in range(parts)]
        return lax.ppermute(x, AXES, pairs)

    def my_half(x):
        return lax.dynamic_slice_in_dim(x, core * half, half, axis=-1)

    def other_half(x):
        return lax.dynamic_slice_in_dim(x, (1 - core) * half, half, axis=-1)

    def side_by_side(mine, theirs):
        return jnp.where(
            core == 0,
            jnp.concatenate(mine + theirs, axis=1),
            jnp.concatenate(theirs + mine, axis=1),
        )

    out_piece = jnp.concatenate([my_half(out_weight), swap(other_half(out_weight), CORE)], axis=0)
    if by_pairs:
        z1, z2, y0 = swap(out_piece, NEXT_Z), swap(out_piece, FAR_Z), swap(out_piece, NEXT_Y)
        z3 = swap(z2, NEXT_Z)
        y1, y2, y3 = swap(z1, NEXT_Y), swap(z2, NEXT_Y), swap(z3, NEXT_Y)
        out_pieces = [out_piece, y0, z1, y1, z2, y2, z3, y3]
    else:
        rows = out_weight.shape[0]
        got = lax.all_gather(out_piece, "dp", axis_index_groups=same_core).reshape(chips, 2, rows, half)
        out_pieces = [jnp.where(core == 0, got, got[:, ::-1]).reshape(width, half)]

    hidden = after(decoder_hidden, out_piece)
    if by_pairs:
        gram_mine, gram_theirs, sum_own = gram(where, hidden, kept_index[0], (chips, dec // parts))
        send, keep = first_step(where, gram_mine, swap(gram_theirs, CORE))
        own, *codes = second_step(where, keep, swap(send, NEXT_Y))
        codes = [swap(c, NEXT_Z * (m + 1)) for m, c in enumerate(codes)]
        (gram_rows,) = last_step(where, own, codes)
    else:
        gram_all, sum_own = gram(where, hidden, kept_index[0], None)
        gram_rows = lax.psum_scatter(gram_all, "dp", scatter_dimension=0, tiled=True)
        high = gram_rows.astype(jnp.bfloat16)
        low = (gram_rows - high.astype(jnp.float32)).astype(jnp.bfloat16)
        gram_rows = jnp.concatenate([high, low], axis=0)
    grams = jnp.concatenate([gram_rows, swap(gram_rows, CORE)], axis=0)
    pred = after(pred_weight, out_piece)
    pred_mine, pred_theirs = my_half(pred), swap(other_half(pred), CORE)
    weights = jnp.concatenate([pred_mine, pred_mine, pred_theirs, pred_theirs], axis=0)

    mixed_own = attention(where, after(queries, out_piece)[0], key_rows[0], value_rows[0])
    mixed_other = swap(mixed_own, CORE)
    others = jnp.concatenate([other_half(after(stream, out_piece)), other_half(earlier)], axis=0)
    others = swap(others, CORE)
    sum_other = swap(sum_own, CORE)

    blend, stats = branch(where, mixed_own, mixed_other, stream[0], earlier[0], others, out_pieces)
    stats_other = swap(stats, CORE)

    def term(cut, coded):
        return targets_and_term(
            where, blend, stats, stats_other, sum_own, sum_other, grams, weights, cut, coded
        )

    if not by_pairs:
        target_own, target_other, total = term((0, 1), False)
        targets = side_by_side([target_own], [swap(target_other, CORE)])[None]
        summed = lax.psum_scatter(
            total, "dp", scatter_dimension=0, tiled=True, axis_index_groups=same_core
        )
        summed = (summed * scale).reshape(2, dec // parts, half)
        keep = lax.dynamic_index_in_dim(summed, core, 0, keepdims=False)
        send = lax.dynamic_index_in_dim(summed, 1 - core, 0, keepdims=False)
        return targets, side_by_side([keep], [swap(send, CORE)])

    steps = [term((j, CUTS), True) for j in range(CUTS)]
    received = [swap(send, NEXT_Y) for _, _, send, _ in steps]
    targets = side_by_side([s[0] for s in steps], [swap(s[1], CORE) for s in steps])[None]
    received[-1] = after(received[-1], targets)
    mine, theirs = [], []
    for (_, _, _, keep), codes in zip(steps, received):
        own, *codes = second_step(where, keep, codes)
        codes = [swap(c, NEXT_Z * (m + 1)) for m, c in enumerate(codes)]
        keep, send = last_step(where, own, codes, scale)
        mine.append(keep)
        theirs.append(swap(send, CORE))
    return targets, side_by_side(mine, theirs)


def solution(mesh):
    by_image = P(AXES, None, None)
    return jax.shard_map(
        functools.partial(on_device, dict(mesh.shape)),
        mesh=mesh,
        in_specs=(
            by_image,
            by_image,
            by_image,
            by_image,
            by_image,
            P("dp", None),
            P("dp", None),
            P(AXES, None, None, None),
            by_image,
        ),
        out_specs=(by_image, P(AXES, None)),
        check_vma=False,
    )
```

```python
import functools
import math

import jax
import jax.numpy as jnp
from jax import lax
from jax.experimental import pallas as pl
from jax.experimental.pallas import tpu as pltpu
from jax.sharding import PartitionSpec as P

HEADS = 24
TOP_K = 10
AXES = ("groups", "dp")
VMEM = 24 * 1024 * 1024
COST = 1000
CORE, NEXT_Y, NEXT_Z, FAR_Z = 1, 2, 4, 8
LINE = 4
CUTS = 2
TAIL = 16


def call(kernel, out_shape, name, scratch=()):
    held = pl.BlockSpec(memory_space=pltpu.VMEM)

    def run(where, *arrays):
        return pl.pallas_call(
            kernel,
            out_shape=tuple(out_shape),
            in_specs=[pl.BlockSpec(memory_space=pltpu.SMEM)] + [held] * len(arrays),
            out_specs=(held,) * len(out_shape),
            scratch_shapes=scratch,
            compiler_params=pltpu.CompilerParams(vmem_limit_bytes=VMEM),
            cost_estimate=pl.CostEstimate(flops=COST, bytes_accessed=COST, transcendentals=0),
            name=name,
        )(where, *arrays)

    return run


def f32(*shape):
    return jax.ShapeDtypeStruct(shape, jnp.float32)


def bf16(*shape):
    return jax.ShapeDtypeStruct(shape, jnp.bfloat16)


def contract_rows(a, b):
    return lax.dot_general(a, b, (((0,), (0,)), ((), ())), preferred_element_type=jnp.float32)


def attention_kernel(where_ref, q_ref, k_ref, v_ref, out_ref, *, size):
    mixed = []
    for j in range(q_ref.shape[1] // size):
        cols = slice(j * size, (j + 1) * size)
        q = q_ref[:, cols] * jnp.asarray(1.0 / math.sqrt(size), q_ref.dtype)
        scores = lax.dot_general(
            k_ref[:, cols], q, (((1,), (1,)), ((), ())), preferred_element_type=jnp.float32
        )
        weights = jnp.exp(scores - jnp.max(scores, axis=0, keepdims=True))
        weights = weights * (1.0 / jnp.sum(weights, axis=0, keepdims=True))
        mixed.append(contract_rows(weights.astype(jnp.bfloat16), v_ref[:, cols]))
    out_ref[...] = jnp.concatenate(mixed, axis=1).astype(out_ref.dtype)


def attention(where, q, k, v):
    kernel = functools.partial(attention_kernel, size=q.shape[1] // HEADS)
    return call(kernel, [bf16(*q.shape)], "attention")(where, q, k, v)[0]


def gram_kernel(where_ref, hidden_ref, kept_ref, *rest, parted):
    *gram_refs, sum_ref, rows_all, total = rest
    clones, patches = hidden_ref.shape[1], hidden_ref.shape[2]
    positions = lax.broadcasted_iota(jnp.int32, (patches, kept_ref.shape[1]), 0)
    sums = None
    for i in range(clones):
        kept = kept_ref[i : i + 1, :]
        covered = jnp.max(jnp.where(positions == kept, 1.0, 0.0), axis=1, keepdims=True)
        rows = hidden_ref[0, i]
        rows = jnp.where(covered > 0.5, jnp.zeros_like(rows), rows)
        rows_all[i * patches : (i + 1) * patches, :] = rows
        wide = rows.astype(jnp.float32)
        sums = wide if sums is None else sums + wide
    sum_ref[...] = sums.astype(sum_ref.dtype)
    if not parted:
        gram_refs[0][...] = contract_rows(rows_all[...], rows_all[...])
        return
    total[...] = contract_rows(rows_all[...], rows_all[...])
    mine, theirs = gram_refs
    core = where_ref[0]
    chips, rows = parted
    for k in range(chips):
        for ref, c in ((mine, core), (theirs, 1 - core)):
            at = pl.multiple_of((2 * k + c) * rows, rows)
            ref[k * rows : (k + 1) * rows, :] = total[pl.ds(at, rows), :]


def gram(where, hidden, kept, parted):
    _, clones, patches, width = hidden.shape
    grams = [f32(width // 2, width)] * 2 if parted else [f32(width, width)]
    scratch = [pltpu.VMEM((clones * patches, width), jnp.bfloat16), pltpu.VMEM((width, width), jnp.float32)]
    kernel = functools.partial(gram_kernel, parted=parted)
    return call(kernel, grams + [bf16(patches, width)], "gram", scratch)(where, hidden, kept)


def put_in_order(where_ref, pieces, full):
    core, chip = where_ref[0], where_ref[1]
    if len(pieces) == 1:
        full[...] = pieces[0][...]
        return
    for k, piece in enumerate(pieces):
        rows = piece.shape[0] // 2
        base = (chip ^ k) * 2
        for j in range(2):
            at = pl.multiple_of((base + (core ^ j)) * rows, rows)
            full[pl.ds(at, rows), :] = piece[j * rows : (j + 1) * rows, :]


def branch_kernel(where_ref, mixed_own, mixed_other, stream, earlier, others, *rest):
    *pieces, blend_ref, stats_ref, full = rest
    put_in_order(where_ref, pieces, full)
    patches, half = stream.shape[0], blend_ref.shape[1]
    columns = pl.ds(pl.multiple_of(where_ref[0] * half, half), half)
    streams = (stream[:, columns], others[0])
    earliers = (earlier[:, columns], others[1])
    for i, mixed in enumerate((mixed_own, mixed_other)):
        layer_out = streams[i].astype(jnp.float32) + jnp.dot(
            mixed[...], full[...], preferred_element_type=jnp.float32
        )
        center = jnp.mean(layer_out, axis=0, keepdims=True)
        away = layer_out - center
        spread = jnp.mean(away * away, axis=0, keepdims=True)
        normed = away * (1.0 / jnp.sqrt(spread + 1e-05))
        blend = ((TOP_K - 1) * earliers[i].astype(jnp.float32) + normed) * (1.0 / TOP_K)
        rows = slice(i * patches, (i + 1) * patches)
        blend_ref[rows, :] = blend
        middle = jnp.mean(blend, axis=1, keepdims=True)
        off = blend - middle
        squares = jnp.sum(off * off, axis=1, keepdims=True)
        lane = lax.broadcasted_iota(jnp.int32, (patches, 128), 1)
        stats_ref[rows, :] = jnp.where(lane < 64, middle, squares)


def branch(where, mixed_own, *others):
    patches, width = mixed_own.shape
    half = width // 2
    shapes = [f32(2 * patches, half), f32(2 * patches, 128)]
    scratch = [pltpu.VMEM((width, half), jnp.bfloat16)]
    return call(branch_kernel, shapes, "branch", scratch)(where, mixed_own, *others)


def encode(values, out_ref):
    rows = values.shape[0]
    top = jnp.max(jnp.abs(values), axis=0, keepdims=True)
    power = jnp.ceil(jnp.log2(jnp.maximum(top, 1e-30))) - 15.0
    codes = jnp.clip(jnp.round(values * jnp.exp2(-power)), -32767.0, 32767.0)
    out_ref[:rows, :] = codes.astype(jnp.int32).astype(jnp.int16)
    out_ref[rows:, :] = jnp.broadcast_to(power, (TAIL, values.shape[1])).astype(jnp.int32).astype(jnp.int16)


def decode(codes):
    rows = codes.shape[0] - TAIL
    power = codes[rows:, :].astype(jnp.int32).astype(jnp.float32)[:1]
    return codes[:rows, :].astype(jnp.int32).astype(jnp.float32) * jnp.exp2(power)


def halve(values, where_ref, send_ref, keep_ref):
    rows = keep_ref.shape[0] // LINE
    y = where_ref[1] % 2

    def blocks(of):
        return [values[pl.ds(pl.multiple_of((2 * z + of) * rows, rows), rows), :] for z in range(LINE)]

    keep_ref[...] = jnp.concatenate(blocks(y), axis=0)
    encode(jnp.concatenate(blocks(1 - y), axis=0), send_ref)


def halved_shapes(rows, width):
    return [jax.ShapeDtypeStruct((rows // 2 + TAIL, width), jnp.int16), f32(rows // 2, width)]


def first_kernel(where_ref, mine, theirs, send_ref, keep_ref, total):
    total[...] = mine[...] + theirs[...]
    halve(total, where_ref, send_ref, keep_ref)


def first_step(where, mine, theirs):
    scratch = [pltpu.VMEM(mine.shape, jnp.float32)]
    return call(first_kernel, halved_shapes(*mine.shape), "first_step", scratch)(where, mine, theirs)


def second_kernel(where_ref, keep, codes, own_ref, *rest):
    *send_refs, total = rest
    rows = own_ref.shape[0]
    z = where_ref[1] // 2
    total[...] = keep[...] + decode(codes[...])

    def block(of):
        return total[pl.ds(pl.multiple_of(of * rows, rows), rows), :]

    own_ref[...] = block(z)
    for m, ref in enumerate(send_refs):
        encode(block(z ^ (m + 1)), ref)


def second_step(where, keep, codes):
    rows, width = keep.shape[0] // LINE, keep.shape[1]
    shapes = [f32(rows, width)] + [jax.ShapeDtypeStruct((rows + TAIL, width), jnp.int16)] * (LINE - 1)
    scratch = [pltpu.VMEM(keep.shape, jnp.float32)]
    return call(second_kernel, shapes, "second_step", scratch)(where, keep, codes)


def last_kernel(where_ref, own, c1, c2, c3, *out_refs, scale):
    total = own[...] + (decode(c1[...]) + (decode(c2[...]) + decode(c3[...])))
    if scale is None:
        (pair,) = out_refs
        rows = total.shape[0]
        high = total.astype(jnp.bfloat16)
        pair[:rows, :] = high
        pair[rows:, :] = (total - high.astype(jnp.float32)).astype(jnp.bfloat16)
        return
    keep, send = out_refs
    rows = keep.shape[0]
    first, second = total[:rows, :] * scale, total[rows:, :] * scale
    mine_first = where_ref[0] == 0
    keep[...] = jnp.where(mine_first, first, second)
    send[...] = jnp.where(mine_first, second, first)


def last_step(where, own, codes, scale=None):
    rows, width = own.shape
    shapes = [bf16(2 * rows, width)] if scale is None else [f32(rows // 2, width)] * 2
    return call(functools.partial(last_kernel, scale=scale), shapes, "last_step")(where, own, *codes)


def targets_kernel(where_ref, blend, stats, stats_other, sum_own, sum_other, grams, weights, own_ref, other_ref, *rest, cut, width):
    patches, columns = own_ref.shape
    cols = slice(cut * columns, (cut + 1) * columns)
    grad = contract_rows(grams[...], weights[:, cols])
    for i, (out, features) in enumerate(((own_ref, sum_own), (other_ref, sum_other))):
        mine = stats[i * patches : (i + 1) * patches, :]
        theirs = stats_other[(1 - i) * patches : (2 - i) * patches, :]
        gap = mine[:, :1] - theirs[:, :1]
        middle = 0.5 * (mine[:, :1] + theirs[:, :1])
        squares = mine[:, 64:65] + theirs[:, 64:65] + (width / 4) * gap * gap
        root = 1.0 / jnp.sqrt(squares * (1.0 / width) + 1e-06)
        target = (blend[i * patches : (i + 1) * patches, cols] - middle) * root
        out[...] = target
        grad = grad - contract_rows(features[...], target.astype(jnp.bfloat16))
    if len(rest) == 1:
        rest[0][...] = grad
        return
    send_ref, keep_ref, total = rest
    total[...] = grad
    halve(total, where_ref, send_ref, keep_ref)


def targets_and_term(where, blend, stats, stats_other, sum_own, sum_other, grams, weights, cut, coded):
    j, n = cut
    patches, columns = blend.shape[0] // 2, blend.shape[1] // n
    dec = grams.shape[1]
    shapes = [f32(patches, columns)] * 2
    shapes += halved_shapes(dec, columns) if coded else [f32(dec, columns)]
    kernel = functools.partial(targets_kernel, cut=j, width=2 * blend.shape[1])
    scratch = [pltpu.VMEM((dec, columns), jnp.float32)] if coded else []
    return call(kernel, shapes, "targets", scratch)(
        where, blend, stats, stats_other, sum_own, sum_other, grams, weights
    )


def after(x, *others):
    return lax.optimization_barrier((x,) + others)[0]


def on_device(
    mesh_shape,
    queries,
    key_rows,
    value_rows,
    stream,
    earlier,
    out_weight,
    pred_weight,
    decoder_hidden,
    kept_index,
):
    groups, parts = mesh_shape["groups"], mesh_shape["dp"]
    chips = parts // 2
    patches, width = queries.shape[1:]
    clones, dec = decoder_hidden.shape[1], decoder_hidden.shape[3]
    half = width // 2
    scale = 2.0 / (math.sqrt(width) * clones)
    me = lax.axis_index("dp")
    core, chip = me % 2, me // 2
    where = jnp.stack([core, chip]).astype(jnp.int32)
    same_core = [[2 * k + j for k in range(chips)] for j in range(2)]
    by_pairs = chips == 2 * LINE

    def swap(x, bits):
        pairs = [(g * parts + i, g * parts + (i ^ bits)) for g in range(groups) for i in range(parts)]
        return lax.ppermute(x, AXES, pairs)

    def my_half(x):
        return lax.dynamic_slice_in_dim(x, core * half, half, axis=-1)

    def other_half(x):
        return lax.dynamic_slice_in_dim(x, (1 - core) * half, half, axis=-1)

    def side_by_side(mine, theirs):
        return jnp.where(
            core == 0,
            jnp.concatenate(mine + theirs, axis=1),
            jnp.concatenate(theirs + mine, axis=1),
        )

    out_piece = jnp.concatenate([my_half(out_weight), swap(other_half(out_weight), CORE)], axis=0)
    if by_pairs:
        z1, z2, y0 = swap(out_piece, NEXT_Z), swap(out_piece, FAR_Z), swap(out_piece, NEXT_Y)
        z3 = swap(z2, NEXT_Z)
        y1, y2, y3 = swap(z1, NEXT_Y), swap(z2, NEXT_Y), swap(z3, NEXT_Y)
        out_pieces = [out_piece, y0, z1, y1, z2, y2, z3, y3]
    else:
        rows = out_weight.shape[0]
        got = lax.all_gather(out_piece, "dp", axis_index_groups=same_core).reshape(chips, 2, rows, half)
        out_pieces = [jnp.where(core == 0, got, got[:, ::-1]).reshape(width, half)]

    hidden = after(decoder_hidden, out_piece)
    if by_pairs:
        gram_mine, gram_theirs, sum_own = gram(where, hidden, kept_index[0], (chips, dec // parts))
        send, keep = first_step(where, gram_mine, swap(gram_theirs, CORE))
        own, *codes = second_step(where, keep, swap(send, NEXT_Y))
        codes = [swap(c, NEXT_Z * (m + 1)) for m, c in enumerate(codes)]
        (gram_rows,) = last_step(where, own, codes)
    else:
        gram_all, sum_own = gram(where, hidden, kept_index[0], None)
        gram_rows = lax.psum_scatter(gram_all, "dp", scatter_dimension=0, tiled=True)
        high = gram_rows.astype(jnp.bfloat16)
        low = (gram_rows - high.astype(jnp.float32)).astype(jnp.bfloat16)
        gram_rows = jnp.concatenate([high, low], axis=0)
    grams = jnp.concatenate([gram_rows, swap(gram_rows, CORE)], axis=0)
    pred = after(pred_weight, out_piece)
    pred_mine, pred_theirs = my_half(pred), swap(other_half(pred), CORE)
    weights = jnp.concatenate([pred_mine, pred_mine, pred_theirs, pred_theirs], axis=0)

    mixed_own = attention(where, after(queries, out_piece)[0], key_rows[0], value_rows[0])
    mixed_other = swap(mixed_own, CORE)
    others = jnp.concatenate([other_half(after(stream, out_piece)), other_half(earlier)], axis=0)
    others = swap(others, CORE)
    sum_other = swap(sum_own, CORE)

    blend, stats = branch(where, mixed_own, mixed_other, stream[0], earlier[0], others, *out_pieces)
    stats_other = swap(stats, CORE)

    def term(cut, coded):
        return targets_and_term(
            where, blend, stats, stats_other, sum_own, sum_other, grams, weights, cut, coded
        )

    if not by_pairs:
        target_own, target_other, total = term((0, 1), False)
        targets = side_by_side([target_own], [swap(target_other, CORE)])[None]
        summed = lax.psum_scatter(
            total, "dp", scatter_dimension=0, tiled=True, axis_index_groups=same_core
        )
        summed = (summed * scale).reshape(2, dec // parts, half)
        keep = lax.dynamic_index_in_dim(summed, core, 0, keepdims=False)
        send = lax.dynamic_index_in_dim(summed, 1 - core, 0, keepdims=False)
        return targets, side_by_side([keep], [swap(send, CORE)])

    steps = [term((j, CUTS), True) for j in range(CUTS)]
    received = [swap(send, NEXT_Y) for _, _, send, _ in steps]
    targets = side_by_side([s[0] for s in steps], [swap(s[1], CORE) for s in steps])[None]
    received[-1] = after(received[-1], targets)
    mine, theirs = [], []
    for (_, _, _, keep), codes in zip(steps, received):
        own, *codes = second_step(where, keep, codes)
        codes = [swap(c, NEXT_Z * (m + 1)) for m, c in enumerate(codes)]
        keep, send = last_step(where, own, codes, scale)
        mine.append(keep)
        theirs.append(swap(send, CORE))
    return targets, side_by_side(mine, theirs)


def solution(mesh):
    by_image = P(AXES, None, None)
    return jax.shard_map(
        functools.partial(on_device, dict(mesh.shape)),
        mesh=mesh,
        in_specs=(
            by_image,
            by_image,
            by_image,
            by_image,
            by_image,
            P("dp", None),
            P("dp", None),
            P(AXES, None, None, None),
            by_image,
        ),
        out_specs=(by_image, P(AXES, None)),
        check_vma=False,
    )
```

```python
import functools
import math

import jax
import jax.numpy as jnp
from jax import lax
from jax.experimental import pallas as pl
from jax.experimental.pallas import tpu as pltpu
from jax.sharding import PartitionSpec as P

HEADS = 24
TOP_K = 10
AXES = ("groups", "dp")
VMEM = 24 * 1024 * 1024
COST = 1000
CORE, NEXT_Y, NEXT_Z, FAR_Z = 1, 2, 4, 8
LINE = 4
CUTS = 2
TAIL = 16


def call(kernel, out_shape, name, scratch=(), cost=COST):
    held = pl.BlockSpec(memory_space=pltpu.VMEM)

    def run(where, *arrays):
        return pl.pallas_call(
            kernel,
            out_shape=tuple(out_shape),
            in_specs=[pl.BlockSpec(memory_space=pltpu.SMEM)] + [held] * len(arrays),
            out_specs=(held,) * len(out_shape),
            scratch_shapes=scratch,
            compiler_params=pltpu.CompilerParams(vmem_limit_bytes=VMEM),
            cost_estimate=pl.CostEstimate(flops=0, bytes_accessed=cost, transcendentals=0),
            name=name,
        )(where, *arrays)

    return run


def f32(*shape):
    return jax.ShapeDtypeStruct(shape, jnp.float32)


def bf16(*shape):
    return jax.ShapeDtypeStruct(shape, jnp.bfloat16)


def contract_rows(a, b):
    return lax.dot_general(a, b, (((0,), (0,)), ((), ())), preferred_element_type=jnp.float32)


def attention_kernel(where_ref, q_ref, k_ref, v_ref, stream, earlier, out_ref, *bundle, size):
    mixed = []
    for j in range(q_ref.shape[1] // size):
        cols = slice(j * size, (j + 1) * size)
        q = q_ref[:, cols] * jnp.asarray(1.0 / math.sqrt(size), q_ref.dtype)
        scores = lax.dot_general(
            k_ref[:, cols], q, (((1,), (1,)), ((), ())), preferred_element_type=jnp.float32
        )
        weights = jnp.exp(scores - jnp.max(scores, axis=0, keepdims=True))
        weights = weights * (1.0 / jnp.sum(weights, axis=0, keepdims=True))
        mixed.append(contract_rows(weights.astype(jnp.bfloat16), v_ref[:, cols]))
    half = bundle[0].shape[1]
    mixed = jnp.concatenate(mixed, axis=1).astype(out_ref.dtype)
    out_ref[...] = mixed
    theirs = pl.ds(pl.multiple_of((1 - where_ref[0]) * half, half), half)
    bundle[0][...] = mixed[:, :half]
    bundle[1][...] = mixed[:, half:]
    bundle[2][...] = stream[:, theirs]
    bundle[3][...] = earlier[:, theirs]


def attention(where, q, k, v, stream, earlier):
    patches, width = q.shape
    kernel = functools.partial(attention_kernel, size=width // HEADS)
    shapes = [bf16(patches, width)] + [bf16(patches, width // 2)] * 4
    return call(kernel, shapes, "attention")(where, q, k, v, stream, earlier)


def gram_kernel(where_ref, hidden_ref, kept_ref, *rest, parted):
    *gram_refs, sum_ref, rows_all, total = rest
    clones, patches = hidden_ref.shape[1], hidden_ref.shape[2]
    positions = lax.broadcasted_iota(jnp.int32, (patches, kept_ref.shape[1]), 0)
    sums = None
    for i in range(clones):
        kept = kept_ref[i : i + 1, :]
        covered = jnp.max(jnp.where(positions == kept, 1.0, 0.0), axis=1, keepdims=True)
        rows = hidden_ref[0, i]
        rows = jnp.where(covered > 0.5, jnp.zeros_like(rows), rows)
        rows_all[i * patches : (i + 1) * patches, :] = rows
        wide = rows.astype(jnp.float32)
        sums = wide if sums is None else sums + wide
    sum_ref[...] = sums.astype(sum_ref.dtype)
    if not parted:
        gram_refs[0][...] = contract_rows(rows_all[...], rows_all[...])
        return
    total[...] = contract_rows(rows_all[...], rows_all[...])
    mine, theirs = gram_refs
    core = where_ref[0]
    chips, rows = parted
    for k in range(chips):
        for ref, c in ((mine, core), (theirs, 1 - core)):
            at = pl.multiple_of((2 * k + c) * rows, rows)
            ref[k * rows : (k + 1) * rows, :] = total[pl.ds(at, rows), :]


def gram(where, hidden, kept, parted):
    _, clones, patches, width = hidden.shape
    grams = [f32(width // 2, width)] * 2 if parted else [f32(width, width)]
    scratch = [pltpu.VMEM((clones * patches, width), jnp.bfloat16), pltpu.VMEM((width, width), jnp.float32)]
    kernel = functools.partial(gram_kernel, parted=parted)
    return call(kernel, grams + [bf16(patches, width)], "gram", scratch)(where, hidden, kept)


def put_in_order(where_ref, pieces, full):
    core, chip = where_ref[0], where_ref[1]
    if len(pieces) == 1:
        full[...] = pieces[0][...]
        return
    for k, piece in enumerate(pieces):
        rows = piece.shape[0] // 2
        base = (chip ^ k) * 2
        for j in range(2):
            at = pl.multiple_of((base + (core ^ j)) * rows, rows)
            full[pl.ds(at, rows), :] = piece[j * rows : (j + 1) * rows, :]


def branch_kernel(where_ref, mixed_own, stream, earlier, *rest):
    others, rest = rest[:4], rest[4:]
    *pieces, blend_ref, stats_ref, full = rest
    put_in_order(where_ref, pieces, full)
    patches, half = stream.shape[0], blend_ref.shape[1]
    columns = pl.ds(pl.multiple_of(where_ref[0] * half, half), half)
    mixeds = (mixed_own[...], jnp.concatenate([others[0][...], others[1][...]], axis=1))
    streams = (stream[:, columns], others[2][...])
    earliers = (earlier[:, columns], others[3][...])
    for i in range(2):
        layer_out = streams[i].astype(jnp.float32) + jnp.dot(
            mixeds[i], full[...], preferred_element_type=jnp.float32
        )
        center = jnp.mean(layer_out, axis=0, keepdims=True)
        away = layer_out - center
        spread = jnp.mean(away * away, axis=0, keepdims=True)
        normed = away * (1.0 / jnp.sqrt(spread + 1e-05))
        blend = ((TOP_K - 1) * earliers[i].astype(jnp.float32) + normed) * (1.0 / TOP_K)
        rows = slice(i * patches, (i + 1) * patches)
        blend_ref[rows, :] = blend
        middle = jnp.mean(blend, axis=1, keepdims=True)
        off = blend - middle
        squares = jnp.sum(off * off, axis=1, keepdims=True)
        lane = lax.broadcasted_iota(jnp.int32, (patches, 128), 1)
        stats_ref[rows, :] = jnp.where(lane < 64, middle, squares)


def branch(where, mixed_own, *others):
    patches, width = mixed_own.shape
    half = width // 2
    shapes = [f32(2 * patches, half), f32(2 * patches, 128)]
    scratch = [pltpu.VMEM((width, half), jnp.bfloat16)]
    return call(branch_kernel, shapes, "branch", scratch)(where, mixed_own, *others)


def encode(values, out_ref):
    rows = values.shape[0]
    top = jnp.max(jnp.abs(values), axis=0, keepdims=True)
    power = jnp.ceil(jnp.log2(jnp.maximum(top, 1e-30))) - 15.0
    codes = jnp.clip(jnp.round(values * jnp.exp2(-power)), -32767.0, 32767.0)
    out_ref[:rows, :] = codes.astype(jnp.int32).astype(jnp.int16)
    out_ref[rows:, :] = jnp.broadcast_to(power, (TAIL, values.shape[1])).astype(jnp.int32).astype(jnp.int16)


def decode(codes):
    rows = codes.shape[0] - TAIL
    power = codes[rows:, :].astype(jnp.int32).astype(jnp.float32)[:1]
    return codes[:rows, :].astype(jnp.int32).astype(jnp.float32) * jnp.exp2(power)


def halve(values, where_ref, send_ref, keep_ref):
    rows = keep_ref.shape[0] // LINE
    y = where_ref[1] % 2

    def blocks(of):
        return [values[pl.ds(pl.multiple_of((2 * z + of) * rows, rows), rows), :] for z in range(LINE)]

    keep_ref[...] = jnp.concatenate(blocks(y), axis=0)
    encode(jnp.concatenate(blocks(1 - y), axis=0), send_ref)


def halved_shapes(rows, width):
    return [jax.ShapeDtypeStruct((rows // 2 + TAIL, width), jnp.int16), f32(rows // 2, width)]


def first_kernel(where_ref, mine, t0, t1, send_ref, keep_ref, total):
    total[...] = mine[...] + jnp.concatenate([t0[...], t1[...]], axis=0)
    halve(total, where_ref, send_ref, keep_ref)


def first_step(where, mine, theirs):
    scratch = [pltpu.VMEM(mine.shape, jnp.float32)]
    return call(first_kernel, halved_shapes(*mine.shape), "first_step", scratch)(where, mine, *theirs)


def second_kernel(where_ref, keep, codes, own_ref, *rest):
    *send_refs, total = rest
    rows = own_ref.shape[0]
    z = where_ref[1] // 2
    total[...] = keep[...] + decode(codes[...])

    def block(of):
        return total[pl.ds(pl.multiple_of(of * rows, rows), rows), :]

    own_ref[...] = block(z)
    for m, ref in enumerate(send_refs):
        encode(block(z ^ (m + 1)), ref)


def second_step(where, keep, codes):
    rows, width = keep.shape[0] // LINE, keep.shape[1]
    shapes = [f32(rows, width)] + [jax.ShapeDtypeStruct((rows + TAIL, width), jnp.int16)] * (LINE - 1)
    scratch = [pltpu.VMEM(keep.shape, jnp.float32)]
    return call(second_kernel, shapes, "second_step", scratch)(where, keep, codes)


def last_kernel(where_ref, own, c1, c2, c3, *out_refs, scale):
    total = own[...] + (decode(c1[...]) + (decode(c2[...]) + decode(c3[...])))
    if scale is None:
        (pair,) = out_refs
        rows = total.shape[0]
        high = total.astype(jnp.bfloat16)
        pair[:rows, :] = high
        pair[rows:, :] = (total - high.astype(jnp.float32)).astype(jnp.bfloat16)
        return
    keep, send = out_refs
    rows = keep.shape[0]
    first, second = total[:rows, :] * scale, total[rows:, :] * scale
    mine_first = where_ref[0] == 0
    keep[...] = jnp.where(mine_first, first, second)
    send[...] = jnp.where(mine_first, second, first)


def last_step(where, own, codes, scale=None):
    rows, width = own.shape
    shapes = [bf16(2 * rows, width)] if scale is None else [f32(rows // 2, width)] * 2
    return call(functools.partial(last_kernel, scale=scale), shapes, "last_step")(where, own, *codes)


def targets_kernel(where_ref, blend, stats, stats_other, sum_own, sum_other, grams, weights, own_ref, other_ref, *rest, cut, width):
    patches, columns = own_ref.shape
    cols = slice(cut * columns, (cut + 1) * columns)
    grad = contract_rows(grams[...], weights[:, cols])
    for i, (out, features) in enumerate(((own_ref, sum_own), (other_ref, sum_other))):
        mine = stats[i * patches : (i + 1) * patches, :]
        theirs = stats_other[(1 - i) * patches : (2 - i) * patches, :]
        gap = mine[:, :1] - theirs[:, :1]
        middle = 0.5 * (mine[:, :1] + theirs[:, :1])
        squares = mine[:, 64:65] + theirs[:, 64:65] + (width / 4) * gap * gap
        root = 1.0 / jnp.sqrt(squares * (1.0 / width) + 1e-06)
        target = (blend[i * patches : (i + 1) * patches, cols] - middle) * root
        out[...] = target
        grad = grad - contract_rows(features[...], target.astype(jnp.bfloat16))
    if len(rest) == 1:
        rest[0][...] = grad
        return
    send_ref, keep_ref, total = rest
    total[...] = grad
    halve(total, where_ref, send_ref, keep_ref)


def targets_and_term(where, blend, stats, stats_other, sum_own, sum_other, grams, weights, cut, coded):
    j, n = cut
    patches, columns = blend.shape[0] // 2, blend.shape[1] // n
    dec = grams.shape[1]
    shapes = [f32(patches, columns)] * 2
    shapes += halved_shapes(dec, columns) if coded else [f32(dec, columns)]
    kernel = functools.partial(targets_kernel, cut=j, width=2 * blend.shape[1])
    scratch = [pltpu.VMEM((dec, columns), jnp.float32)] if coded else []
    return call(kernel, shapes, "targets", scratch)(
        where, blend, stats, stats_other, sum_own, sum_other, grams, weights
    )


def after(x, *others):
    return lax.optimization_barrier((x,) + others)[0]


def on_device(
    mesh_shape,
    queries,
    key_rows,
    value_rows,
    stream,
    earlier,
    out_weight,
    pred_weight,
    decoder_hidden,
    kept_index,
):
    groups, parts = mesh_shape["groups"], mesh_shape["dp"]
    chips = parts // 2
    patches, width = queries.shape[1:]
    clones, dec = decoder_hidden.shape[1], decoder_hidden.shape[3]
    half = width // 2
    scale = 2.0 / (math.sqrt(width) * clones)
    me = lax.axis_index("dp")
    core, chip = me % 2, me // 2
    where = jnp.stack([core, chip]).astype(jnp.int32)
    same_core = [[2 * k + j for k in range(chips)] for j in range(2)]
    by_pairs = chips == 2 * LINE

    def swap(x, bits):
        pairs = [(g * parts + i, g * parts + (i ^ bits)) for g in range(groups) for i in range(parts)]
        return lax.ppermute(x, AXES, pairs)

    def my_half(x):
        return lax.dynamic_slice_in_dim(x, core * half, half, axis=-1)

    def other_half(x):
        return lax.dynamic_slice_in_dim(x, (1 - core) * half, half, axis=-1)

    def side_by_side(mine, theirs):
        return jnp.where(
            core == 0,
            jnp.concatenate(mine + theirs, axis=1),
            jnp.concatenate(theirs + mine, axis=1),
        )

    rows = out_weight.shape[0]
    got = swap(jnp.concatenate([other_half(out_weight), other_half(pred_weight)], axis=0), CORE)
    out_piece = jnp.concatenate([my_half(out_weight), got[:rows]], axis=0)
    pred_mine, pred_theirs = my_half(pred_weight), got[rows:]
    weights = jnp.concatenate([pred_mine, pred_mine, pred_theirs, pred_theirs], axis=0)

    def attend(*anchors):
        q = after(queries, *anchors) if anchors else queries
        return attention(where, q[0], key_rows[0], value_rows[0], stream[0], earlier[0])

    if by_pairs:
        z2, z1, y0 = swap(out_piece, FAR_Z), swap(out_piece, NEXT_Z), swap(out_piece, NEXT_Y)
        y1, y2 = swap(z1, NEXT_Y), swap(after(z2, y0), NEXT_Y)
        z3 = swap(z2, NEXT_Z)
        y3 = swap(after(z3, y1), NEXT_Y)
        out_pieces = [out_piece, y0, z1, y1, z2, y2, z3, y3]
        hidden = decoder_hidden
        gram_mine, gram_theirs, sum_own = gram(where, hidden, kept_index[0], (chips, dec // parts))
        sum_other = swap(sum_own, CORE)
        gram_theirs = [swap(g, CORE) for g in jnp.split(gram_theirs, 2)]
        mixed_own, *bundle = attend(z3)
        others = [swap(b, CORE) for b in bundle]
        send, keep = first_step(where, after(gram_mine, y0), gram_theirs)
        own, *codes = second_step(where, after(keep, z3,y1), swap(send, NEXT_Y))
        codes = [swap(c, NEXT_Z * (m + 1)) for m, c in enumerate(codes)]
        (gram_rows,) = last_step(where, after(own, y2), codes)
    else:
        got = lax.all_gather(out_piece, "dp", axis_index_groups=same_core).reshape(chips, 2, rows, half)
        out_pieces = [jnp.where(core == 0, got, got[:, ::-1]).reshape(width, half)]
        gram_all, sum_own = gram(where, decoder_hidden, kept_index[0], None)
        sum_other = swap(sum_own, CORE)
        mixed_own, *bundle = attend()
        others = [swap(b, CORE) for b in bundle]
        gram_rows = lax.psum_scatter(gram_all, "dp", scatter_dimension=0, tiled=True)
        high = gram_rows.astype(jnp.bfloat16)
        low = (gram_rows - high.astype(jnp.float32)).astype(jnp.bfloat16)
        gram_rows = jnp.concatenate([high, low], axis=0)
    grams = jnp.concatenate([gram_rows, swap(gram_rows, CORE)], axis=0)

    blend, stats = branch(where, mixed_own, stream[0], earlier[0], *others, *out_pieces)
    stats_other = swap(stats, CORE)

    def term(cut, coded, *before):
        return targets_and_term(
            where, blend, stats, after(stats_other, *before), sum_own, sum_other, grams, weights, cut, coded
        )

    if not by_pairs:
        target_own, target_other, total = term((0, 1), False)
        targets = side_by_side([target_own], [swap(target_other, CORE)])[None]
        summed = lax.psum_scatter(
            total, "dp", scatter_dimension=0, tiled=True, axis_index_groups=same_core
        )
        summed = (summed * scale).reshape(2, dec // parts, half)
        keep = lax.dynamic_index_in_dim(summed, core, 0, keepdims=False)
        send = lax.dynamic_index_in_dim(summed, 1 - core, 0, keepdims=False)
        return targets, side_by_side([keep], [swap(send, CORE)])

    steps, rest, received = [], [], []
    for j in range(CUTS):
        steps.append(term((j, CUTS), True, *rest))
        rest.append(swap(steps[j][1], CORE))
        received.append(swap(steps[j][2], NEXT_Y))
    targets = side_by_side([s[0] for s in steps], rest)[None]
    mine, theirs = [], []
    for j in range(CUTS):
        own, *codes = second_step(where, steps[j][3], received[j])
        codes = [swap(c, NEXT_Z * (m + 1)) for m, c in enumerate(codes)]
        if j == 0:
            own = after(own, targets)
        keep, send = last_step(where, own, codes, scale)
        mine.append(keep)
        theirs.append(swap(send, CORE))
    return targets, side_by_side(mine, theirs)


def solution(mesh):
    by_image = P(AXES, None, None)
    return jax.shard_map(
        functools.partial(on_device, dict(mesh.shape)),
        mesh=mesh,
        in_specs=(
            by_image,
            by_image,
            by_image,
            by_image,
            by_image,
            P("dp", None),
            P("dp", None),
            P(AXES, None, None, None),
            by_image,
        ),
        out_specs=(by_image, P(AXES, None)),
        check_vma=False,
    )
```

```python
import functools
import math

import jax
import jax.numpy as jnp
from jax import lax
from jax.experimental import pallas as pl
from jax.experimental.pallas import tpu as pltpu
from jax.sharding import PartitionSpec as P

HEADS = 24
TOP_K = 10
AXES = ("groups", "dp")
VMEM = 24 * 1024 * 1024
COST = 1000
CORE, NEXT_Y, NEXT_Z, FAR_Z = 1, 2, 4, 8
LINE = 4
CUTS = 2
TAIL = 16


def call(kernel, out_shape, name, scratch=()):
    held = pl.BlockSpec(memory_space=pltpu.VMEM)

    def run(where, *arrays):
        return pl.pallas_call(
            kernel,
            out_shape=tuple(out_shape),
            in_specs=[pl.BlockSpec(memory_space=pltpu.SMEM)] + [held] * len(arrays),
            out_specs=(held,) * len(out_shape),
            scratch_shapes=scratch,
            compiler_params=pltpu.CompilerParams(vmem_limit_bytes=VMEM),
            cost_estimate=pl.CostEstimate(flops=COST, bytes_accessed=COST, transcendentals=0),
            name=name,
        )(where, *arrays)

    return run


def f32(*shape):
    return jax.ShapeDtypeStruct(shape, jnp.float32)


def bf16(*shape):
    return jax.ShapeDtypeStruct(shape, jnp.bfloat16)


def contract_rows(a, b):
    return lax.dot_general(a, b, (((0,), (0,)), ((), ())), preferred_element_type=jnp.float32)


def attention_kernel(where_ref, q_ref, k_ref, v_ref, stream, earlier, out_ref, *bundle, size):
    mixed = []
    for j in range(q_ref.shape[1] // size):
        cols = slice(j * size, (j + 1) * size)
        q = q_ref[:, cols] * jnp.asarray(1.0 / math.sqrt(size), q_ref.dtype)
        scores = lax.dot_general(
            k_ref[:, cols], q, (((1,), (1,)), ((), ())), preferred_element_type=jnp.float32
        )
        weights = jnp.exp(scores - jnp.max(scores, axis=0, keepdims=True))
        weights = weights * (1.0 / jnp.sum(weights, axis=0, keepdims=True))
        mixed.append(contract_rows(weights.astype(jnp.bfloat16), v_ref[:, cols]))
    half = bundle[0].shape[1]
    mixed = jnp.concatenate(mixed, axis=1).astype(out_ref.dtype)
    out_ref[...] = mixed
    theirs = pl.ds(pl.multiple_of((1 - where_ref[0]) * half, half), half)
    bundle[0][...] = mixed[:, :half]
    bundle[1][...] = mixed[:, half:]
    bundle[2][...] = stream[:, theirs]
    bundle[3][...] = earlier[:, theirs]


def attention(where, q, k, v, stream, earlier):
    patches, width = q.shape
    kernel = functools.partial(attention_kernel, size=width // HEADS)
    shapes = [bf16(patches, width)] + [bf16(patches, width // 2)] * 4
    return call(kernel, shapes, "attention")(where, q, k, v, stream, earlier)


def gram_kernel(where_ref, hidden_ref, kept_ref, *rest, parted):
    *gram_refs, sum_ref, rows_all, total = rest
    clones, patches = hidden_ref.shape[1:3]
    positions = lax.broadcasted_iota(jnp.int32, (patches, kept_ref.shape[1]), 0)
    sums = None
    for i in range(clones):
        kept = kept_ref[i : i + 1, :]
        covered = jnp.max(jnp.where(positions == kept, 1.0, 0.0), axis=1, keepdims=True)
        rows = hidden_ref[0, i]
        rows = jnp.where(covered > 0.5, jnp.zeros_like(rows), rows)
        rows_all[i * patches : (i + 1) * patches, :] = rows
        wide = rows.astype(jnp.float32)
        sums = wide if sums is None else sums + wide
    sum_ref[...] = sums.astype(sum_ref.dtype)
    if not parted:
        gram_refs[0][...] = contract_rows(rows_all[...], rows_all[...])
        return
    total[...] = contract_rows(rows_all[...], rows_all[...])
    mine, *theirs = gram_refs
    core = where_ref[0]
    chips, rows = parted
    for k in range(chips):
        at = pl.multiple_of((2 * k + core) * rows, rows)
        mine[k * rows : (k + 1) * rows, :] = total[pl.ds(at, rows), :]
        at = pl.multiple_of((2 * k + 1 - core) * rows, rows)
        part = k // (chips // len(theirs))
        here = (k % (chips // len(theirs))) * rows
        theirs[part][here : here + rows, :] = total[pl.ds(at, rows), :]


def gram(where, hidden, kept, parted):
    _, clones, patches, width = hidden.shape
    grams = [f32(width // 2, width)] + [f32(width // 4, width)] * 2 if parted else [f32(width, width)]
    scratch = [
        pltpu.VMEM((clones * patches, width), jnp.bfloat16),
        pltpu.VMEM((width, width), jnp.float32),
    ]
    kernel = functools.partial(gram_kernel, parted=parted)
    shapes = grams + [bf16(patches, width)]
    return call(kernel, shapes, "gram", scratch)(where, hidden, kept)


def cut_kernel(where_ref, own, other, out_ref):
    rows, half = own.shape[0], out_ref.shape[1]
    columns = pl.ds(pl.multiple_of(where_ref[0] * half, half), half)
    out_ref[:rows, :] = own[:, columns]
    out_ref[rows:, :] = other[:, columns]


def cut(where, own, other):
    rows, width = own.shape
    return call(cut_kernel, [bf16(2 * rows, width // 2)], "cut")(where, own, other)[0]


def put_in_order(where_ref, pieces, full):
    core, chip = where_ref[0], where_ref[1]
    if len(pieces) == 1:
        full[...] = pieces[0][...]
        return
    for k, piece in enumerate(pieces):
        rows = piece.shape[0] // 2
        base = (chip ^ k) * 2
        for j in range(2):
            at = pl.multiple_of((base + (core ^ j)) * rows, rows)
            full[pl.ds(at, rows), :] = piece[j * rows : (j + 1) * rows, :]


def branch_kernel(where_ref, mixed_own, stream, earlier, *rest):
    others, rest = rest[:4], rest[4:]
    *pieces, blend_ref, stats_ref, full = rest
    put_in_order(where_ref, pieces, full)
    patches, half = stream.shape[0], blend_ref.shape[1]
    columns = pl.ds(pl.multiple_of(where_ref[0] * half, half), half)
    mixeds = (mixed_own[...], jnp.concatenate([others[0][...], others[1][...]], axis=1))
    streams = (stream[:, columns], others[2][...])
    earliers = (earlier[:, columns], others[3][...])
    for i in range(2):
        layer_out = streams[i].astype(jnp.float32) + jnp.dot(
            mixeds[i], full[...], preferred_element_type=jnp.float32
        )
        center = jnp.mean(layer_out, axis=0, keepdims=True)
        away = layer_out - center
        spread = jnp.mean(away * away, axis=0, keepdims=True)
        normed = away * (1.0 / jnp.sqrt(spread + 1e-05))
        blend = ((TOP_K - 1) * earliers[i].astype(jnp.float32) + normed) * (1.0 / TOP_K)
        rows = slice(i * patches, (i + 1) * patches)
        blend_ref[rows, :] = blend
        middle = jnp.mean(blend, axis=1, keepdims=True)
        off = blend - middle
        squares = jnp.sum(off * off, axis=1, keepdims=True)
        lane = lax.broadcasted_iota(jnp.int32, (patches, 128), 1)
        stats_ref[rows, :] = jnp.where(lane < 64, middle, squares)


def branch(where, mixed_own, *others):
    patches, width = mixed_own.shape
    half = width // 2
    shapes = [f32(2 * patches, half), f32(2 * patches, 128)]
    scratch = [pltpu.VMEM((width, half), jnp.bfloat16)]
    return call(branch_kernel, shapes, "branch", scratch)(where, mixed_own, *others)


def encode(values, out_ref):
    rows = values.shape[0]
    top = jnp.max(jnp.abs(values), axis=0, keepdims=True)
    power = jnp.ceil(jnp.log2(jnp.maximum(top, 1e-30))) - 15.0
    codes = jnp.clip(jnp.round(values * jnp.exp2(-power)), -32767.0, 32767.0)
    out_ref[:rows, :] = codes.astype(jnp.int32).astype(jnp.int16)
    out_ref[rows:, :] = jnp.broadcast_to(power, (TAIL, values.shape[1])).astype(jnp.int32).astype(jnp.int16)


def decode(codes):
    rows = codes.shape[0] - TAIL
    power = codes[rows:, :].astype(jnp.int32).astype(jnp.float32)[:1]
    return codes[:rows, :].astype(jnp.int32).astype(jnp.float32) * jnp.exp2(power)


def halve(values, where_ref, send_ref, keep_ref):
    rows = keep_ref.shape[0] // LINE
    y = where_ref[1] % 2

    def blocks(of):
        return [values[pl.ds(pl.multiple_of((2 * z + of) * rows, rows), rows), :] for z in range(LINE)]

    keep_ref[...] = jnp.concatenate(blocks(y), axis=0)
    encode(jnp.concatenate(blocks(1 - y), axis=0), send_ref)


def halved_shapes(rows, width):
    return [jax.ShapeDtypeStruct((rows // 2 + TAIL, width), jnp.int16), f32(rows // 2, width)]


def first_kernel(where_ref, mine, t0, t1, send_ref, keep_ref, total):
    total[...] = mine[...] + jnp.concatenate([t0[...], t1[...]], axis=0)
    halve(total, where_ref, send_ref, keep_ref)


def first_step(where, mine, theirs):
    scratch = [pltpu.VMEM(mine.shape, jnp.float32)]
    return call(first_kernel, halved_shapes(*mine.shape), "first_step", scratch)(where, mine, *theirs)


def second_kernel(where_ref, keep, codes, own_ref, *rest):
    *send_refs, total = rest
    rows = own_ref.shape[0]
    z = where_ref[1] // 2
    total[...] = keep[...] + decode(codes[...])

    def block(of):
        return total[pl.ds(pl.multiple_of(of * rows, rows), rows), :]

    own_ref[...] = block(z)
    for m, ref in enumerate(send_refs):
        encode(block(z ^ (m + 1)), ref)


def second_step(where, keep, codes):
    rows, width = keep.shape[0] // LINE, keep.shape[1]
    shapes = [f32(rows, width)] + [jax.ShapeDtypeStruct((rows + TAIL, width), jnp.int16)] * (LINE - 1)
    scratch = [pltpu.VMEM(keep.shape, jnp.float32)]
    return call(second_kernel, shapes, "second_step", scratch)(where, keep, codes)


def last_kernel(where_ref, own, c1, c2, c3, *out_refs, scale):
    total = own[...] + (decode(c1[...]) + (decode(c2[...]) + decode(c3[...])))
    if scale is None:
        (pair,) = out_refs
        rows = total.shape[0]
        high = total.astype(jnp.bfloat16)
        pair[:rows, :] = high
        pair[rows:, :] = (total - high.astype(jnp.float32)).astype(jnp.bfloat16)
        return
    keep, send = out_refs
    rows = keep.shape[0]
    first, second = total[:rows, :] * scale, total[rows:, :] * scale
    mine_first = where_ref[0] == 0
    keep[...] = jnp.where(mine_first, first, second)
    send[...] = jnp.where(mine_first, second, first)


def last_step(where, own, codes, scale=None):
    rows, width = own.shape
    shapes = [bf16(2 * rows, width)] if scale is None else [f32(rows // 2, width)] * 2
    return call(functools.partial(last_kernel, scale=scale), shapes, "last_step")(where, own, *codes)


def targets_kernel(where_ref, blend, stats, stats_other, sum_own, sum_other, gram_own, gram_other, weights, own_ref, other_ref, *rest, cut, width):
    patches, columns = own_ref.shape
    cols = slice(cut * columns, (cut + 1) * columns)
    rows = weights.shape[0] // 2
    mine, theirs = weights[:rows, cols], weights[rows:, cols]
    grad = contract_rows(
        jnp.concatenate([gram_own[...], gram_other[...]], axis=0),
        jnp.concatenate([mine, mine, theirs, theirs], axis=0),
    )
    for i, (out, features) in enumerate(((own_ref, sum_own), (other_ref, sum_other))):
        mine = stats[i * patches : (i + 1) * patches, :]
        theirs = stats_other[(1 - i) * patches : (2 - i) * patches, :]
        gap = mine[:, :1] - theirs[:, :1]
        middle = 0.5 * (mine[:, :1] + theirs[:, :1])
        squares = mine[:, 64:65] + theirs[:, 64:65] + (width / 4) * gap * gap
        root = 1.0 / jnp.sqrt(squares * (1.0 / width) + 1e-06)
        target = (blend[i * patches : (i + 1) * patches, cols] - middle) * root
        out[...] = target
        grad = grad - contract_rows(features[...], target.astype(jnp.bfloat16))
    if len(rest) == 1:
        rest[0][...] = grad
        return
    send_ref, keep_ref, total = rest
    total[...] = grad
    halve(total, where_ref, send_ref, keep_ref)


def targets_and_term(where, blend, stats, stats_other, sum_own, sum_other, grams, weights, part, coded):
    j, n = part
    patches, columns = blend.shape[0] // 2, blend.shape[1] // n
    dec = grams[0].shape[1]
    shapes = [f32(patches, columns)] * 2
    shapes += halved_shapes(dec, columns) if coded else [f32(dec, columns)]
    kernel = functools.partial(targets_kernel, cut=j, width=2 * blend.shape[1])
    scratch = [pltpu.VMEM((dec, columns), jnp.float32)] if coded else []
    return call(kernel, shapes, "targets", scratch)(
        where, blend, stats, stats_other, sum_own, sum_other, *grams, weights
    )


def after(x, *others):
    return lax.optimization_barrier((x,) + others)[0]


def on_device(
    mesh_shape,
    queries,
    key_rows,
    value_rows,
    stream,
    earlier,
    out_weight,
    pred_weight,
    decoder_hidden,
    kept_index,
):
    groups, parts = mesh_shape["groups"], mesh_shape["dp"]
    chips = parts // 2
    patches, width = queries.shape[1:]
    clones, dec = decoder_hidden.shape[1], decoder_hidden.shape[3]
    half = width // 2
    scale = 2.0 / (math.sqrt(width) * clones)
    me = lax.axis_index("dp")
    core, chip = me % 2, me // 2
    where = jnp.stack([core, chip]).astype(jnp.int32)
    same_core = [[2 * k + j for k in range(chips)] for j in range(2)]
    by_pairs = chips == 2 * LINE

    def swap(x, bits):
        pairs = [(g * parts + i, g * parts + (i ^ bits)) for g in range(groups) for i in range(parts)]
        return lax.ppermute(x, AXES, pairs)

    def side_by_side(mine, theirs):
        return jnp.where(
            core == 0,
            jnp.concatenate(mine + theirs, axis=1),
            jnp.concatenate(theirs + mine, axis=1),
        )

    rows = out_weight.shape[0]
    if by_pairs:
        gram_mine, *gram_theirs, sum_own = gram(where, decoder_hidden, kept_index[0], (chips, dec // parts))
    else:
        gram_all, sum_own = gram(where, decoder_hidden, kept_index[0], None)
    out_piece = cut(where, after(out_weight, sum_own), swap(out_weight, CORE))
    pred_piece = cut(where, pred_weight, swap(pred_weight, CORE))

    def attend(*anchors):
        q = after(queries, *anchors) if anchors else queries
        return attention(where, q[0], key_rows[0], value_rows[0], stream[0], earlier[0])

    if by_pairs:
        z1, z2, y0 = swap(out_piece, NEXT_Z), swap(out_piece, FAR_Z), swap(out_piece, NEXT_Y)
        sum_other = swap(sum_own, CORE)
        gram_theirs = [swap(g, CORE) for g in gram_theirs]
        send, keep = first_step(where, after(gram_mine, y0), gram_theirs)
        y1 = swap(z1, NEXT_Y)
        z3 = swap(after(z2, send), NEXT_Z)
        y2 = swap(after(z2, y0), NEXT_Y)
        own, *codes = second_step(where, after(keep, z2), swap(send, NEXT_Y))
        y3 = swap(after(z3, y1, own), NEXT_Y)
        out_pieces = [out_piece, y0, z1, y1, z2, y2, z3, y3]
        mixed_own, *bundle = attend(z3, pred_piece)
        others = [swap(b, CORE) for b in bundle]
        codes = [swap(c, NEXT_Z * (m + 1)) for m, c in enumerate(codes)]
        (gram_rows,) = last_step(where, after(own, y2), codes)
        mixed_own = after(mixed_own, gram_rows)
    else:
        got = lax.all_gather(out_piece, "dp", axis_index_groups=same_core).reshape(chips, 2, rows, half)
        out_pieces = [jnp.where(core == 0, got, got[:, ::-1]).reshape(width, half)]
        sum_other = swap(sum_own, CORE)
        mixed_own, *bundle = attend()
        others = [swap(b, CORE) for b in bundle]
        gram_rows = lax.psum_scatter(gram_all, "dp", scatter_dimension=0, tiled=True)
        high = gram_rows.astype(jnp.bfloat16)
        low = (gram_rows - high.astype(jnp.float32)).astype(jnp.bfloat16)
        gram_rows = jnp.concatenate([high, low], axis=0)
    grams = [gram_rows, swap(gram_rows, CORE)]

    blend, stats = branch(where, mixed_own, stream[0], earlier[0], *others, *out_pieces)
    stats_other = swap(stats, CORE)

    def term(part, coded, *before):
        return targets_and_term(
            where, blend, stats, after(stats_other, *before), sum_own, sum_other, grams, pred_piece, part, coded
        )

    if not by_pairs:
        target_own, target_other, total = term((0, 1), False)
        targets = side_by_side([target_own], [swap(target_other, CORE)])[None]
        summed = lax.psum_scatter(
            total, "dp", scatter_dimension=0, tiled=True, axis_index_groups=same_core
        )
        summed = (summed * scale).reshape(2, dec // parts, half)
        keep = lax.dynamic_index_in_dim(summed, core, 0, keepdims=False)
        send = lax.dynamic_index_in_dim(summed, 1 - core, 0, keepdims=False)
        return targets, side_by_side([keep], [swap(send, CORE)])

    steps, rest, received = [], [], []
    for j in range(CUTS):
        steps.append(term((j, CUTS), True, *rest))
        rest.append(swap(steps[j][1], CORE))
        received.append(swap(steps[j][2], NEXT_Y))
    targets = side_by_side([s[0] for s in steps], rest)[None]
    mine, theirs = [], []
    for j in range(CUTS):
        own, *codes = second_step(where, steps[j][3], received[j])
        codes = [swap(c, NEXT_Z * (m + 1)) for m, c in enumerate(codes)]
        if j == 0:
            own = after(own, targets)
        keep, send = last_step(where, own, codes, scale)
        mine.append(keep)
        theirs.append(swap(send, CORE))
    return targets, side_by_side(mine, theirs)


def solution(mesh):
    by_image = P(AXES, None, None)
    return jax.shard_map(
        functools.partial(on_device, dict(mesh.shape)),
        mesh=mesh,
        in_specs=(
            by_image,
            by_image,
            by_image,
            by_image,
            by_image,
            P("dp", None),
            P("dp", None),
            P(AXES, None, None, None),
            by_image,
        ),
        out_specs=(by_image, P(AXES, None)),
        check_vma=False,
    )
```

```python
import functools
import math

import jax
import jax.numpy as jnp
from jax import lax
from jax.experimental import pallas as pl
from jax.experimental.pallas import tpu as pltpu
from jax.sharding import PartitionSpec as P

HEADS = 24
TOP_K = 10
AXES = ("groups", "dp")
VMEM = 24 * 1024 * 1024
COST = 1000
CORE, NEXT_Y, NEXT_Z, FAR_Z = 1, 2, 4, 8
LINE = 4
TAIL = 16


def call(kernel, out_shape, name, scratch=()):
    held = pl.BlockSpec(memory_space=pltpu.VMEM)

    def run(where, *arrays):
        return pl.pallas_call(
            kernel,
            out_shape=tuple(out_shape),
            in_specs=[pl.BlockSpec(memory_space=pltpu.SMEM)] + [held] * len(arrays),
            out_specs=(held,) * len(out_shape),
            scratch_shapes=scratch,
            compiler_params=pltpu.CompilerParams(vmem_limit_bytes=VMEM),
            cost_estimate=pl.CostEstimate(flops=COST, bytes_accessed=COST, transcendentals=0),
            name=name,
        )(where, *arrays)

    return run


def f32(*shape):
    return jax.ShapeDtypeStruct(shape, jnp.float32)


def bf16(*shape):
    return jax.ShapeDtypeStruct(shape, jnp.bfloat16)


def contract_rows(a, b):
    return lax.dot_general(a, b, (((0,), (0,)), ((), ())), preferred_element_type=jnp.float32)


def attention_kernel(where_ref, q_ref, k_ref, v_ref, stream, earlier, out_ref, *bundle, size):
    mixed = []
    for j in range(q_ref.shape[1] // size):
        cols = slice(j * size, (j + 1) * size)
        q = q_ref[:, cols] * jnp.asarray(1.0 / math.sqrt(size), q_ref.dtype)
        scores = lax.dot_general(
            k_ref[:, cols], q, (((1,), (1,)), ((), ())), preferred_element_type=jnp.float32
        )
        weights = jnp.exp(scores - jnp.max(scores, axis=0, keepdims=True))
        weights = weights * (1.0 / jnp.sum(weights, axis=0, keepdims=True))
        mixed.append(contract_rows(weights.astype(jnp.bfloat16), v_ref[:, cols]))
    half = bundle[0].shape[1]
    mixed = jnp.concatenate(mixed, axis=1).astype(out_ref.dtype)
    out_ref[...] = mixed
    theirs = pl.ds(pl.multiple_of((1 - where_ref[0]) * half, half), half)
    bundle[0][...] = mixed[:, :half]
    bundle[1][...] = mixed[:, half:]
    bundle[2][...] = stream[:, theirs]
    bundle[3][...] = earlier[:, theirs]


def attention(where, q, k, v, stream, earlier):
    patches, width = q.shape
    kernel = functools.partial(attention_kernel, size=width // HEADS)
    shapes = [bf16(patches, width)] + [bf16(patches, width // 2)] * 4
    return call(kernel, shapes, "attention")(where, q, k, v, stream, earlier)


def gram_kernel(where_ref, hidden_ref, kept_ref, *rest, parted):
    *gram_refs, sum_ref, rows_all, total = rest
    clones, patches = hidden_ref.shape[1:3]
    positions = lax.broadcasted_iota(jnp.int32, (patches, kept_ref.shape[1]), 0)
    sums = None
    for i in range(clones):
        kept = kept_ref[i : i + 1, :]
        covered = jnp.max(jnp.where(positions == kept, 1.0, 0.0), axis=1, keepdims=True)
        rows = hidden_ref[0, i]
        rows = jnp.where(covered > 0.5, jnp.zeros_like(rows), rows)
        rows_all[i * patches : (i + 1) * patches, :] = rows
        wide = rows.astype(jnp.float32)
        sums = wide if sums is None else sums + wide
    sum_ref[...] = sums.astype(sum_ref.dtype)
    if not parted:
        gram_refs[0][...] = contract_rows(rows_all[...], rows_all[...])
        return
    total[...] = contract_rows(rows_all[...], rows_all[...])
    mine, *theirs = gram_refs
    core = where_ref[0]
    chips, rows = parted
    for k in range(chips):
        at = pl.multiple_of((2 * k + core) * rows, rows)
        mine[k * rows : (k + 1) * rows, :] = total[pl.ds(at, rows), :]
        at = pl.multiple_of((2 * k + 1 - core) * rows, rows)
        part = k // (chips // len(theirs))
        here = (k % (chips // len(theirs))) * rows
        theirs[part][here : here + rows, :] = total[pl.ds(at, rows), :]


def gram(where, hidden, kept, parted):
    _, clones, patches, width = hidden.shape
    grams = [f32(width // 2, width)] + [f32(width // 4, width)] * 2 if parted else [f32(width, width)]
    scratch = [
        pltpu.VMEM((clones * patches, width), jnp.bfloat16),
        pltpu.VMEM((width, width), jnp.float32),
    ]
    kernel = functools.partial(gram_kernel, parted=parted)
    shapes = grams + [bf16(patches, width)]
    return call(kernel, shapes, "gram", scratch)(where, hidden, kept)


def cut_kernel(where_ref, own, other, out_ref):
    rows, half = own.shape[0], out_ref.shape[1]
    columns = pl.ds(pl.multiple_of(where_ref[0] * half, half), half)
    out_ref[:rows, :] = own[:, columns]
    out_ref[rows:, :] = other[:, columns]


def cut(where, own, other):
    rows, width = own.shape
    return call(cut_kernel, [bf16(2 * rows, width // 2)], "cut")(where, own, other)[0]


def put_in_order(where_ref, pieces, full):
    core, chip = where_ref[0], where_ref[1]
    if len(pieces) == 1:
        full[...] = pieces[0][...]
        return
    for k, piece in enumerate(pieces):
        rows = piece.shape[0] // 2
        base = (chip ^ k) * 2
        for j in range(2):
            at = pl.multiple_of((base + (core ^ j)) * rows, rows)
            full[pl.ds(at, rows), :] = piece[j * rows : (j + 1) * rows, :]


def branch_kernel(where_ref, mixed_own, stream, earlier, *rest):
    others, rest = rest[:4], rest[4:]
    *pieces, blend_ref, stats_ref, full = rest
    put_in_order(where_ref, pieces, full)
    patches, half = stream.shape[0], blend_ref.shape[1]
    columns = pl.ds(pl.multiple_of(where_ref[0] * half, half), half)
    mixeds = (mixed_own[...], jnp.concatenate([others[0][...], others[1][...]], axis=1))
    streams = (stream[:, columns], others[2][...])
    earliers = (earlier[:, columns], others[3][...])
    for i in range(2):
        layer_out = streams[i].astype(jnp.float32) + jnp.dot(
            mixeds[i], full[...], preferred_element_type=jnp.float32
        )
        center = jnp.mean(layer_out, axis=0, keepdims=True)
        away = layer_out - center
        spread = jnp.mean(away * away, axis=0, keepdims=True)
        normed = away * (1.0 / jnp.sqrt(spread + 1e-05))
        blend = ((TOP_K - 1) * earliers[i].astype(jnp.float32) + normed) * (1.0 / TOP_K)
        rows = slice(i * patches, (i + 1) * patches)
        blend_ref[rows, :] = blend
        middle = jnp.mean(blend, axis=1, keepdims=True)
        off = blend - middle
        squares = jnp.sum(off * off, axis=1, keepdims=True)
        lane = lax.broadcasted_iota(jnp.int32, (patches, 128), 1)
        stats_ref[rows, :] = jnp.where(lane < 64, middle, squares)


def branch(where, mixed_own, *others):
    patches, width = mixed_own.shape
    half = width // 2
    shapes = [f32(2 * patches, half), f32(2 * patches, 128)]
    scratch = [pltpu.VMEM((width, half), jnp.bfloat16)]
    return call(branch_kernel, shapes, "branch", scratch)(where, mixed_own, *others)


def encode(values, out_ref):
    rows = values.shape[0]
    top = jnp.max(jnp.abs(values), axis=0, keepdims=True)
    power = jnp.ceil(jnp.log2(jnp.maximum(top, 1e-30))) - 15.0
    codes = jnp.clip(jnp.round(values * jnp.exp2(-power)), -32767.0, 32767.0)
    out_ref[:rows, :] = codes.astype(jnp.int32).astype(jnp.int16)
    out_ref[rows:, :] = jnp.broadcast_to(power, (TAIL, values.shape[1])).astype(jnp.int32).astype(jnp.int16)


def decode(codes):
    rows = codes.shape[0] - TAIL
    power = codes[rows:, :].astype(jnp.int32).astype(jnp.float32)[:1]
    return codes[:rows, :].astype(jnp.int32).astype(jnp.float32) * jnp.exp2(power)


def halve(values, where_ref, send_ref, keep_ref):
    rows = keep_ref.shape[0] // LINE
    y = where_ref[1] % 2

    def blocks(of):
        return [values[pl.ds(pl.multiple_of((2 * z + of) * rows, rows), rows), :] for z in range(LINE)]

    keep_ref[...] = jnp.concatenate(blocks(y), axis=0)
    encode(jnp.concatenate(blocks(1 - y), axis=0), send_ref)


def halve_z(values, where_ref, send_ref, keep_ref):
    rows = keep_ref.shape[0] // 2
    z = where_ref[1] // 2

    def block(of):
        return values[pl.ds(pl.multiple_of(of * rows, rows), rows), :]

    keep_ref[...] = jnp.concatenate([block(z), block(z ^ 2)], axis=0)
    encode(jnp.concatenate([block(z ^ 1), block(z ^ 3)], axis=0), send_ref)


def halve_pairs(values, where_ref, send_ref, keep_ref):
    rows = keep_ref.shape[0] // 2
    y = where_ref[1] % 2

    def blocks(of):
        return [values[pl.ds(pl.multiple_of((2 * z + of) * rows, rows), rows), :] for z in range(2)]

    keep_ref[...] = jnp.concatenate(blocks(y), axis=0)
    encode(jnp.concatenate(blocks(1 - y), axis=0), send_ref)


def halve_far(values, where_ref, send_ref, keep_ref):
    rows = keep_ref.shape[0]
    keep_ref[...] = values[:rows, :]
    encode(values[rows:, :], send_ref)


def halved_shapes(rows, width):
    return [jax.ShapeDtypeStruct((rows // 2 + TAIL, width), jnp.int16), f32(rows // 2, width)]


def first_kernel(where_ref, mine, t0, t1, send_ref, keep_ref, total):
    total[...] = mine[...] + jnp.concatenate([t0[...], t1[...]], axis=0)
    halve(total, where_ref, send_ref, keep_ref)


def first_step(where, mine, theirs):
    scratch = [pltpu.VMEM(mine.shape, jnp.float32)]
    return call(first_kernel, halved_shapes(*mine.shape), "first_step", scratch)(where, mine, *theirs)


def second_kernel(where_ref, keep, codes, own_ref, *rest):
    *send_refs, total = rest
    rows = own_ref.shape[0]
    z = where_ref[1] // 2
    total[...] = keep[...] + decode(codes[...])

    def block(of):
        return total[pl.ds(pl.multiple_of(of * rows, rows), rows), :]

    own_ref[...] = block(z)
    for m, ref in enumerate(send_refs):
        encode(block(z ^ (m + 1)), ref)


def second_step(where, keep, codes):
    rows, width = keep.shape[0] // LINE, keep.shape[1]
    shapes = [f32(rows, width)] + [jax.ShapeDtypeStruct((rows + TAIL, width), jnp.int16)] * (LINE - 1)
    scratch = [pltpu.VMEM(keep.shape, jnp.float32)]
    return call(second_kernel, shapes, "second_step", scratch)(where, keep, codes)


def next_kernel(where_ref, keep, codes, send_ref, keep_ref, total, *, halving):
    total[...] = keep[...] + decode(codes[...])
    halving(total, where_ref, send_ref, keep_ref)


def next_step(where, keep, codes, halving):
    scratch = [pltpu.VMEM(keep.shape, jnp.float32)]
    kernel = functools.partial(next_kernel, halving=halving)
    return call(kernel, halved_shapes(*keep.shape), "next_step", scratch)(where, keep, codes)


def last_kernel(where_ref, own, *rest, scale, count):
    codes, out_refs = rest[:count], rest[count:]
    total = own[...]
    for ref in codes:
        total = total + decode(ref[...])
    if scale is None:
        (pair,) = out_refs
        rows = total.shape[0]
        high = total.astype(jnp.bfloat16)
        pair[:rows, :] = high
        pair[rows:, :] = (total - high.astype(jnp.float32)).astype(jnp.bfloat16)
        return
    keep, send = out_refs
    rows = keep.shape[0]
    first, second = total[:rows, :] * scale, total[rows:, :] * scale
    mine_first = where_ref[0] == 0
    keep[...] = jnp.where(mine_first, first, second)
    send[...] = jnp.where(mine_first, second, first)


def last_step(where, own, codes, scale=None):
    rows, width = own.shape
    shapes = [bf16(2 * rows, width)] if scale is None else [f32(rows // 2, width)] * 2
    return call(functools.partial(last_kernel, scale=scale, count=len(codes)), shapes, "last_step")(where, own, *codes)


def targets_kernel(where_ref, blend, stats, stats_other, sum_own, sum_other, gram_own, gram_other, weights, own_ref, other_ref, *rest, cut, width):
    patches, columns = own_ref.shape
    cols = slice(cut * columns, (cut + 1) * columns)
    rows = weights.shape[0] // 2
    mine, theirs = weights[:rows, cols], weights[rows:, cols]
    grad = contract_rows(
        jnp.concatenate([gram_own[...], gram_other[...]], axis=0),
        jnp.concatenate([mine, mine, theirs, theirs], axis=0),
    )
    for i, (out, features) in enumerate(((own_ref, sum_own), (other_ref, sum_other))):
        mine = stats[i * patches : (i + 1) * patches, :]
        theirs = stats_other[(1 - i) * patches : (2 - i) * patches, :]
        gap = mine[:, :1] - theirs[:, :1]
        middle = 0.5 * (mine[:, :1] + theirs[:, :1])
        squares = mine[:, 64:65] + theirs[:, 64:65] + (width / 4) * gap * gap
        root = 1.0 / jnp.sqrt(squares * (1.0 / width) + 1e-06)
        target = (blend[i * patches : (i + 1) * patches, cols] - middle) * root
        out[...] = target
        grad = grad - contract_rows(features[...], target.astype(jnp.bfloat16))
    if len(rest) == 1:
        rest[0][...] = grad
        return
    send_ref, keep_ref, total = rest
    total[...] = grad
    if cut == 0:
        halve(total, where_ref, send_ref, keep_ref)
    else:
        halve_z(total, where_ref, send_ref, keep_ref)


def targets_and_term(where, blend, stats, stats_other, sum_own, sum_other, grams, weights, part, coded):
    j, n = part
    patches, columns = blend.shape[0] // 2, blend.shape[1] // n
    dec = grams[0].shape[1]
    shapes = [f32(patches, columns)] * 2
    shapes += halved_shapes(dec, columns) if coded else [f32(dec, columns)]
    kernel = functools.partial(targets_kernel, cut=j, width=2 * blend.shape[1])
    scratch = [pltpu.VMEM((dec, columns), jnp.float32)] if coded else []
    return call(kernel, shapes, "targets", scratch)(
        where, blend, stats, stats_other, sum_own, sum_other, *grams, weights
    )


def after(x, *others):
    return lax.optimization_barrier((x,) + others)[0]


def on_device(
    mesh_shape,
    queries,
    key_rows,
    value_rows,
    stream,
    earlier,
    out_weight,
    pred_weight,
    decoder_hidden,
    kept_index,
):
    groups, parts = mesh_shape["groups"], mesh_shape["dp"]
    chips = parts // 2
    patches, width = queries.shape[1:]
    clones, dec = decoder_hidden.shape[1], decoder_hidden.shape[3]
    half = width // 2
    scale = 2.0 / (math.sqrt(width) * clones)
    me = lax.axis_index("dp")
    core, chip = me % 2, me // 2
    where = jnp.stack([core, chip]).astype(jnp.int32)
    same_core = [[2 * k + j for k in range(chips)] for j in range(2)]
    by_pairs = chips == 2 * LINE

    def swap(x, bits):
        pairs = [(g * parts + i, g * parts + (i ^ bits)) for g in range(groups) for i in range(parts)]
        return lax.ppermute(x, AXES, pairs)

    def side_by_side(mine, theirs):
        return jnp.where(
            core == 0,
            jnp.concatenate(mine + theirs, axis=1),
            jnp.concatenate(theirs + mine, axis=1),
        )

    rows = out_weight.shape[0]
    if by_pairs:
        gram_mine, *gram_theirs, sum_own = gram(where, decoder_hidden, kept_index[0], (chips, dec // parts))
    else:
        gram_all, sum_own = gram(where, decoder_hidden, kept_index[0], None)
    out_piece = cut(where, after(out_weight, sum_own), swap(out_weight, CORE))
    pred_piece = cut(where, pred_weight, swap(pred_weight, CORE))

    def attend(*anchors):
        q = after(queries, *anchors) if anchors else queries
        return attention(where, q[0], key_rows[0], value_rows[0], stream[0], earlier[0])

    if by_pairs:
        z1, z2, y0 = swap(out_piece, NEXT_Z), swap(out_piece, FAR_Z), swap(out_piece, NEXT_Y)
        sum_other = swap(sum_own, CORE)
        gram_theirs = [swap(g, CORE) for g in gram_theirs]
        send, keep = first_step(where, after(gram_mine, y0), gram_theirs)
        y1 = swap(z1, NEXT_Y)
        z3 = swap(after(z2, send), NEXT_Z)
        y2 = swap(after(z2, y0), NEXT_Y)
        own, *codes = second_step(where, after(keep, z2), swap(send, NEXT_Y))
        y3 = swap(after(z3, y1, own), NEXT_Y)
        out_pieces = [out_piece, y0, z1, y1, z2, y2, z3, y3]
        mixed_own, *bundle = attend(z3, pred_piece)
        others = [swap(b, CORE) for b in bundle]
        codes = [swap(c, NEXT_Z * (m + 1)) for m, c in enumerate(codes)]
        (gram_rows,) = last_step(where, after(own, y2), codes)
        mixed_own = after(mixed_own, gram_rows)
    else:
        got = lax.all_gather(out_piece, "dp", axis_index_groups=same_core).reshape(chips, 2, rows, half)
        out_pieces = [jnp.where(core == 0, got, got[:, ::-1]).reshape(width, half)]
        sum_other = swap(sum_own, CORE)
        mixed_own, *bundle = attend()
        others = [swap(b, CORE) for b in bundle]
        gram_rows = lax.psum_scatter(gram_all, "dp", scatter_dimension=0, tiled=True)
        high = gram_rows.astype(jnp.bfloat16)
        low = (gram_rows - high.astype(jnp.float32)).astype(jnp.bfloat16)
        gram_rows = jnp.concatenate([high, low], axis=0)
    grams = [gram_rows, swap(gram_rows, CORE)]

    blend, stats = branch(where, mixed_own, stream[0], earlier[0], *others, *out_pieces)
    stats_other = swap(stats, CORE)

    def term(part, coded, *before):
        return targets_and_term(
            where, blend, stats, after(stats_other, *before), sum_own, sum_other, grams, pred_piece, part, coded
        )

    if not by_pairs:
        target_own, target_other, total = term((0, 1), False)
        targets = side_by_side([target_own], [swap(target_other, CORE)])[None]
        summed = lax.psum_scatter(
            total, "dp", scatter_dimension=0, tiled=True, axis_index_groups=same_core
        )
        summed = (summed * scale).reshape(2, dec // parts, half)
        keep = lax.dynamic_index_in_dim(summed, core, 0, keepdims=False)
        send = lax.dynamic_index_in_dim(summed, 1 - core, 0, keepdims=False)
        return targets, side_by_side([keep], [swap(send, CORE)])

    steps, rest = [], []
    for j, axis in enumerate((NEXT_Y, NEXT_Z)):
        target_own, target_other, send, keep = term((j, 2), True, *rest)
        rest.append(swap(target_other, CORE))
        steps.append((target_own, keep, swap(send, axis)))
    targets = side_by_side([x[0] for x in steps], rest)[None]
    mine, theirs = [], []
    for (_, keep, codes), halving, axis in zip(steps, (halve_z, halve_pairs), (NEXT_Z, NEXT_Y)):
        send, keep = next_step(where, keep, codes, halving)
        codes = swap(send, axis)
        send, keep = next_step(where, keep, codes, halve_far)
        codes = swap(send, FAR_Z)
        if not mine:
            keep = after(keep, targets)
        keep, send = last_step(where, keep, [codes], scale)
        mine.append(keep)
        theirs.append(swap(send, CORE))
    return targets, side_by_side(mine, theirs)


def solution(mesh):
    by_image = P(AXES, None, None)
    return jax.shard_map(
        functools.partial(on_device, dict(mesh.shape)),
        mesh=mesh,
        in_specs=(
            by_image,
            by_image,
            by_image,
            by_image,
            by_image,
            P("dp", None),
            P("dp", None),
            P(AXES, None, None, None),
            by_image,
        ),
        out_specs=(by_image, P(AXES, None)),
        check_vma=False,
    )
```

```python
import functools
import math

import jax
import jax.numpy as jnp
from jax import lax
from jax.experimental import pallas as pl
from jax.experimental.pallas import tpu as pltpu
from jax.sharding import PartitionSpec as P

HEADS = 24
TOP_K = 10
AXES = ("groups", "dp")
VMEM = 24 * 1024 * 1024
COST = 1000
CORE, NEXT_Y, NEXT_Z, FAR_Z = 1, 2, 4, 8
LINE = 4
TAIL = 16


def call(kernel, out_shape, name, scratch=()):
    held = pl.BlockSpec(memory_space=pltpu.VMEM)

    def run(where, *arrays):
        return pl.pallas_call(
            kernel,
            out_shape=tuple(out_shape),
            in_specs=[pl.BlockSpec(memory_space=pltpu.SMEM)] + [held] * len(arrays),
            out_specs=(held,) * len(out_shape),
            scratch_shapes=scratch,
            compiler_params=pltpu.CompilerParams(vmem_limit_bytes=VMEM),
            cost_estimate=pl.CostEstimate(flops=COST, bytes_accessed=COST, transcendentals=0),
            name=name,
        )(where, *arrays)

    return run


def f32(*shape):
    return jax.ShapeDtypeStruct(shape, jnp.float32)


def bf16(*shape):
    return jax.ShapeDtypeStruct(shape, jnp.bfloat16)


def contract_rows(a, b):
    return lax.dot_general(a, b, (((0,), (0,)), ((), ())), preferred_element_type=jnp.float32)


def attention_kernel(where_ref, q_ref, k_ref, v_ref, stream, earlier, out_ref, *bundle, size):
    mixed = []
    for j in range(q_ref.shape[1] // size):
        cols = slice(j * size, (j + 1) * size)
        q = q_ref[:, cols] * jnp.asarray(1.0 / math.sqrt(size), q_ref.dtype)
        scores = lax.dot_general(
            k_ref[:, cols], q, (((1,), (1,)), ((), ())), preferred_element_type=jnp.float32
        )
        weights = jnp.exp(scores - jnp.max(scores, axis=0, keepdims=True))
        weights = weights * (1.0 / jnp.sum(weights, axis=0, keepdims=True))
        mixed.append(contract_rows(weights.astype(jnp.bfloat16), v_ref[:, cols]))
    half = bundle[0].shape[1]
    mixed = jnp.concatenate(mixed, axis=1).astype(out_ref.dtype)
    out_ref[...] = mixed
    theirs = pl.ds(pl.multiple_of((1 - where_ref[0]) * half, half), half)
    bundle[0][...] = mixed[:, :half]
    bundle[1][...] = mixed[:, half:]
    bundle[2][...] = stream[:, theirs]
    bundle[3][...] = earlier[:, theirs]


def attention(where, q, k, v, stream, earlier):
    patches, width = q.shape
    kernel = functools.partial(attention_kernel, size=width // HEADS)
    shapes = [bf16(patches, width)] + [bf16(patches, width // 2)] * 4
    return call(kernel, shapes, "attention")(where, q, k, v, stream, earlier)


def symmetric_product(x, out):
    width = x.shape[1]
    block = 256 if width % 256 == 0 else width
    for at in range(0, width, block):
        here = slice(at, at + block)
        strip = contract_rows(x[:, here], x[:, at:])
        out[here, at:] = strip
        for later in range(at + block, width, block):
            out[later : later + block, here] = strip[:, later - at : later - at + block].T


def gram_kernel(where_ref, hidden_ref, kept_ref, *rest, parted):
    *gram_refs, sum_ref, rows_all, total = rest
    clones, patches = hidden_ref.shape[1:3]
    positions = lax.broadcasted_iota(jnp.int32, (patches, kept_ref.shape[1]), 0)
    sums = None
    for i in range(clones):
        kept = kept_ref[i : i + 1, :]
        covered = jnp.max(jnp.where(positions == kept, 1.0, 0.0), axis=1, keepdims=True)
        rows = hidden_ref[0, i]
        rows = jnp.where(covered > 0.5, jnp.zeros_like(rows), rows)
        rows_all[i * patches : (i + 1) * patches, :] = rows
        wide = rows.astype(jnp.float32)
        sums = wide if sums is None else sums + wide
    sum_ref[...] = sums.astype(sum_ref.dtype)
    if not parted:
        symmetric_product(rows_all, gram_refs[0])
        return
    symmetric_product(rows_all, total)
    mine, *theirs = gram_refs
    core = where_ref[0]
    chips, rows = parted
    for k in range(chips):
        at = pl.multiple_of((2 * k + core) * rows, rows)
        mine[k * rows : (k + 1) * rows, :] = total[pl.ds(at, rows), :]
        at = pl.multiple_of((2 * k + 1 - core) * rows, rows)
        part = k // (chips // len(theirs))
        here = (k % (chips // len(theirs))) * rows
        theirs[part][here : here + rows, :] = total[pl.ds(at, rows), :]


def gram(where, hidden, kept, parted):
    _, clones, patches, width = hidden.shape
    grams = [f32(width // 2, width)] + [f32(width // 4, width)] * 2 if parted else [f32(width, width)]
    scratch = [
        pltpu.VMEM((clones * patches, width), jnp.bfloat16),
        pltpu.VMEM((width, width), jnp.float32),
    ]
    kernel = functools.partial(gram_kernel, parted=parted)
    shapes = grams + [bf16(patches, width)]
    return call(kernel, shapes, "gram", scratch)(where, hidden, kept)


def cut_kernel(where_ref, own, other, out_ref):
    rows, half = own.shape[0], out_ref.shape[1]
    columns = pl.ds(pl.multiple_of(where_ref[0] * half, half), half)
    out_ref[:rows, :] = own[:, columns]
    out_ref[rows:, :] = other[:, columns]


def cut(where, own, other):
    rows, width = own.shape
    return call(cut_kernel, [bf16(2 * rows, width // 2)], "cut")(where, own, other)[0]


def put_in_order(where_ref, pieces, full):
    core, chip = where_ref[0], where_ref[1]
    if len(pieces) == 1:
        full[...] = pieces[0][...]
        return
    for k, piece in enumerate(pieces):
        rows = piece.shape[0] // 2
        base = (chip ^ k) * 2
        for j in range(2):
            at = pl.multiple_of((base + (core ^ j)) * rows, rows)
            full[pl.ds(at, rows), :] = piece[j * rows : (j + 1) * rows, :]


def branch_kernel(where_ref, mixed_own, stream, earlier, *rest):
    others, rest = rest[:4], rest[4:]
    *pieces, blend_ref, stats_ref, full = rest
    put_in_order(where_ref, pieces, full)
    patches, half = stream.shape[0], blend_ref.shape[1]
    columns = pl.ds(pl.multiple_of(where_ref[0] * half, half), half)
    mixeds = (mixed_own[...], jnp.concatenate([others[0][...], others[1][...]], axis=1))
    streams = (stream[:, columns], others[2][...])
    earliers = (earlier[:, columns], others[3][...])
    for i in range(2):
        layer_out = streams[i].astype(jnp.float32) + jnp.dot(
            mixeds[i], full[...], preferred_element_type=jnp.float32
        )
        center = jnp.mean(layer_out, axis=0, keepdims=True)
        away = layer_out - center
        spread = jnp.mean(away * away, axis=0, keepdims=True)
        normed = away * (1.0 / jnp.sqrt(spread + 1e-05))
        blend = ((TOP_K - 1) * earliers[i].astype(jnp.float32) + normed) * (1.0 / TOP_K)
        rows = slice(i * patches, (i + 1) * patches)
        blend_ref[rows, :] = blend
        middle = jnp.mean(blend, axis=1, keepdims=True)
        off = blend - middle
        squares = jnp.sum(off * off, axis=1, keepdims=True)
        lane = lax.broadcasted_iota(jnp.int32, (patches, 128), 1)
        stats_ref[rows, :] = jnp.where(lane < 64, middle, squares)


def branch(where, mixed_own, *others):
    patches, width = mixed_own.shape
    half = width // 2
    shapes = [f32(2 * patches, half), f32(2 * patches, 128)]
    scratch = [pltpu.VMEM((width, half), jnp.bfloat16)]
    return call(branch_kernel, shapes, "branch", scratch)(where, mixed_own, *others)


def encode(values, out_ref):
    rows = values.shape[0]
    top = jnp.max(jnp.abs(values), axis=0, keepdims=True)
    power = jnp.ceil(jnp.log2(jnp.maximum(top, 1e-30))) - 15.0
    codes = jnp.clip(jnp.round(values * jnp.exp2(-power)), -32767.0, 32767.0)
    out_ref[:rows, :] = codes.astype(jnp.int32).astype(jnp.int16)
    out_ref[rows:, :] = jnp.broadcast_to(power, (TAIL, values.shape[1])).astype(jnp.int32).astype(jnp.int16)


def decode(codes):
    rows = codes.shape[0] - TAIL
    power = codes[rows:, :].astype(jnp.int32).astype(jnp.float32)[:1]
    return codes[:rows, :].astype(jnp.int32).astype(jnp.float32) * jnp.exp2(power)


def halve(values, where_ref, send_ref, keep_ref):
    rows = keep_ref.shape[0] // LINE
    y = where_ref[1] % 2

    def blocks(of):
        return [values[pl.ds(pl.multiple_of((2 * z + of) * rows, rows), rows), :] for z in range(LINE)]

    keep_ref[...] = jnp.concatenate(blocks(y), axis=0)
    encode(jnp.concatenate(blocks(1 - y), axis=0), send_ref)


def halve_z(values, where_ref, send_ref, keep_ref):
    rows = keep_ref.shape[0] // 2
    z = where_ref[1] // 2

    def block(of):
        return values[pl.ds(pl.multiple_of(of * rows, rows), rows), :]

    keep_ref[...] = jnp.concatenate([block(z), block(z ^ 2)], axis=0)
    encode(jnp.concatenate([block(z ^ 1), block(z ^ 3)], axis=0), send_ref)


def halve_pairs(values, where_ref, send_ref, keep_ref):
    rows = keep_ref.shape[0] // 2
    y = where_ref[1] % 2

    def blocks(of):
        return [values[pl.ds(pl.multiple_of((2 * z + of) * rows, rows), rows), :] for z in range(2)]

    keep_ref[...] = jnp.concatenate(blocks(y), axis=0)
    encode(jnp.concatenate(blocks(1 - y), axis=0), send_ref)


def halve_far(values, where_ref, send_ref, keep_ref):
    rows = keep_ref.shape[0]
    keep_ref[...] = values[:rows, :]
    encode(values[rows:, :], send_ref)


def halved_shapes(rows, width):
    return [jax.ShapeDtypeStruct((rows // 2 + TAIL, width), jnp.int16), f32(rows // 2, width)]


def first_kernel(where_ref, mine, t0, t1, send_ref, keep_ref, total):
    total[...] = mine[...] + jnp.concatenate([t0[...], t1[...]], axis=0)
    halve(total, where_ref, send_ref, keep_ref)


def first_step(where, mine, theirs):
    scratch = [pltpu.VMEM(mine.shape, jnp.float32)]
    return call(first_kernel, halved_shapes(*mine.shape), "first_step", scratch)(where, mine, *theirs)


def second_kernel(where_ref, keep, codes, own_ref, *rest):
    *send_refs, total = rest
    rows = own_ref.shape[0]
    z = where_ref[1] // 2
    total[...] = keep[...] + decode(codes[...])

    def block(of):
        return total[pl.ds(pl.multiple_of(of * rows, rows), rows), :]

    own_ref[...] = block(z)
    for m, ref in enumerate(send_refs):
        encode(block(z ^ (m + 1)), ref)


def second_step(where, keep, codes):
    rows, width = keep.shape[0] // LINE, keep.shape[1]
    shapes = [f32(rows, width)] + [jax.ShapeDtypeStruct((rows + TAIL, width), jnp.int16)] * (LINE - 1)
    scratch = [pltpu.VMEM(keep.shape, jnp.float32)]
    return call(second_kernel, shapes, "second_step", scratch)(where, keep, codes)


def next_kernel(where_ref, keep, codes, send_ref, keep_ref, total, *, halving):
    total[...] = keep[...] + decode(codes[...])
    halving(total, where_ref, send_ref, keep_ref)


def next_step(where, keep, codes, halving):
    scratch = [pltpu.VMEM(keep.shape, jnp.float32)]
    kernel = functools.partial(next_kernel, halving=halving)
    return call(kernel, halved_shapes(*keep.shape), "next_step", scratch)(where, keep, codes)


def last_kernel(where_ref, own, *rest, scale, count):
    codes, out_refs = rest[:count], rest[count:]
    total = own[...]
    for ref in codes:
        total = total + decode(ref[...])
    if scale is None:
        (pair,) = out_refs
        rows = total.shape[0]
        high = total.astype(jnp.bfloat16)
        pair[:rows, :] = high
        pair[rows:, :] = (total - high.astype(jnp.float32)).astype(jnp.bfloat16)
        return
    keep, send = out_refs
    rows = keep.shape[0]
    first, second = total[:rows, :] * scale, total[rows:, :] * scale
    mine_first = where_ref[0] == 0
    keep[...] = jnp.where(mine_first, first, second)
    send[...] = jnp.where(mine_first, second, first)


def last_step(where, own, codes, scale=None):
    rows, width = own.shape
    shapes = [bf16(2 * rows, width)] if scale is None else [f32(rows // 2, width)] * 2
    return call(functools.partial(last_kernel, scale=scale, count=len(codes)), shapes, "last_step")(where, own, *codes)


def targets_kernel(where_ref, blend, stats, stats_other, sum_own, sum_other, gram_own, gram_other, weights, own_ref, other_ref, *rest, cut, width):
    patches, columns = own_ref.shape
    cols = slice(cut * columns, (cut + 1) * columns)
    rows = weights.shape[0] // 2
    mine, theirs = weights[:rows, cols], weights[rows:, cols]
    grad = contract_rows(
        jnp.concatenate([gram_own[...], gram_other[...]], axis=0),
        jnp.concatenate([mine, mine, theirs, theirs], axis=0),
    )
    for i, (out, features) in enumerate(((own_ref, sum_own), (other_ref, sum_other))):
        mine = stats[i * patches : (i + 1) * patches, :]
        theirs = stats_other[(1 - i) * patches : (2 - i) * patches, :]
        gap = mine[:, :1] - theirs[:, :1]
        middle = 0.5 * (mine[:, :1] + theirs[:, :1])
        squares = mine[:, 64:65] + theirs[:, 64:65] + (width / 4) * gap * gap
        root = 1.0 / jnp.sqrt(squares * (1.0 / width) + 1e-06)
        target = (blend[i * patches : (i + 1) * patches, cols] - middle) * root
        out[...] = target
        grad = grad - contract_rows(features[...], target.astype(jnp.bfloat16))
    if len(rest) == 1:
        rest[0][...] = grad
        return
    send_ref, keep_ref, total = rest
    total[...] = grad
    if cut == 0:
        halve(total, where_ref, send_ref, keep_ref)
    else:
        halve_z(total, where_ref, send_ref, keep_ref)


def targets_and_term(where, blend, stats, stats_other, sum_own, sum_other, grams, weights, part, coded):
    j, n = part
    patches, columns = blend.shape[0] // 2, blend.shape[1] // n
    dec = grams[0].shape[1]
    shapes = [f32(patches, columns)] * 2
    shapes += halved_shapes(dec, columns) if coded else [f32(dec, columns)]
    kernel = functools.partial(targets_kernel, cut=j, width=2 * blend.shape[1])
    scratch = [pltpu.VMEM((dec, columns), jnp.float32)] if coded else []
    return call(kernel, shapes, "targets", scratch)(
        where, blend, stats, stats_other, sum_own, sum_other, *grams, weights
    )


def after(x, *others):
    return lax.optimization_barrier((x,) + others)[0]


def on_device(
    mesh_shape,
    queries,
    key_rows,
    value_rows,
    stream,
    earlier,
    out_weight,
    pred_weight,
    decoder_hidden,
    kept_index,
):
    groups, parts = mesh_shape["groups"], mesh_shape["dp"]
    chips = parts // 2
    patches, width = queries.shape[1:]
    clones, dec = decoder_hidden.shape[1], decoder_hidden.shape[3]
    half = width // 2
    scale = 2.0 / (math.sqrt(width) * clones)
    me = lax.axis_index("dp")
    core, chip = me % 2, me // 2
    where = jnp.stack([core, chip]).astype(jnp.int32)
    same_core = [[2 * k + j for k in range(chips)] for j in range(2)]
    by_pairs = chips == 2 * LINE

    def swap(x, bits):
        pairs = [(g * parts + i, g * parts + (i ^ bits)) for g in range(groups) for i in range(parts)]
        return lax.ppermute(x, AXES, pairs)

    def side_by_side(mine, theirs):
        return jnp.where(
            core == 0,
            jnp.concatenate(mine + theirs, axis=1),
            jnp.concatenate(theirs + mine, axis=1),
        )

    rows = out_weight.shape[0]
    if by_pairs:
        gram_mine, *gram_theirs, sum_own = gram(where, decoder_hidden, kept_index[0], (chips, dec // parts))
    else:
        gram_all, sum_own = gram(where, decoder_hidden, kept_index[0], None)
    out_piece = cut(where, after(out_weight, sum_own), swap(out_weight, CORE))
    pred_piece = cut(where, pred_weight, swap(pred_weight, CORE))

    def attend(*anchors):
        q = after(queries, *anchors) if anchors else queries
        return attention(where, q[0], key_rows[0], value_rows[0], stream[0], earlier[0])

    if by_pairs:
        z1, z2, y0 = swap(out_piece, NEXT_Z), swap(out_piece, FAR_Z), swap(out_piece, NEXT_Y)
        sum_other = swap(sum_own, CORE)
        gram_theirs = [swap(g, CORE) for g in gram_theirs]
        send, keep = first_step(where, after(gram_mine, y0), gram_theirs)
        y1 = swap(z1, NEXT_Y)
        z3 = swap(after(z2, send), NEXT_Z)
        y2 = swap(after(z2, y0), NEXT_Y)
        own, *codes = second_step(where, after(keep, z2), swap(send, NEXT_Y))
        y3 = swap(after(z3, y1, own), NEXT_Y)
        out_pieces = [out_piece, y0, z1, y1, z2, y2, z3, y3]
        mixed_own, *bundle = attend(z3, pred_piece)
        others = [swap(b, CORE) for b in bundle]
        codes = [swap(c, NEXT_Z * (m + 1)) for m, c in enumerate(codes)]
        (gram_rows,) = last_step(where, after(own, y2), codes)
        mixed_own = after(mixed_own, gram_rows)
    else:
        got = lax.all_gather(out_piece, "dp", axis_index_groups=same_core).reshape(chips, 2, rows, half)
        out_pieces = [jnp.where(core == 0, got, got[:, ::-1]).reshape(width, half)]
        sum_other = swap(sum_own, CORE)
        mixed_own, *bundle = attend()
        others = [swap(b, CORE) for b in bundle]
        gram_rows = lax.psum_scatter(gram_all, "dp", scatter_dimension=0, tiled=True)
        high = gram_rows.astype(jnp.bfloat16)
        low = (gram_rows - high.astype(jnp.float32)).astype(jnp.bfloat16)
        gram_rows = jnp.concatenate([high, low], axis=0)
    grams = [gram_rows, swap(gram_rows, CORE)]

    blend, stats = branch(where, mixed_own, stream[0], earlier[0], *others, *out_pieces)
    stats_other = swap(stats, CORE)

    def term(part, coded, *before):
        return targets_and_term(
            where, blend, stats, after(stats_other, *before), sum_own, sum_other, grams, pred_piece, part, coded
        )

    if not by_pairs:
        target_own, target_other, total = term((0, 1), False)
        targets = side_by_side([target_own], [swap(target_other, CORE)])[None]
        summed = lax.psum_scatter(
            total, "dp", scatter_dimension=0, tiled=True, axis_index_groups=same_core
        )
        summed = (summed * scale).reshape(2, dec // parts, half)
        keep = lax.dynamic_index_in_dim(summed, core, 0, keepdims=False)
        send = lax.dynamic_index_in_dim(summed, 1 - core, 0, keepdims=False)
        return targets, side_by_side([keep], [swap(send, CORE)])

    steps, rest = [], []
    for j, axis in enumerate((NEXT_Y, NEXT_Z)):
        target_own, target_other, send, keep = term((j, 2), True)
        rest.append(swap(target_other, CORE))
        steps.append((target_own, keep, swap(send, axis)))
    targets = side_by_side([x[0] for x in steps], rest)[None]
    mine, theirs = [], []
    for (_, keep, codes), halving, axis in zip(steps, (halve_z, halve_pairs), (NEXT_Z, NEXT_Y)):
        send, keep = next_step(where, keep, codes, halving)
        codes = swap(send, axis)
        send, keep = next_step(where, keep, codes, halve_far)
        codes = swap(send, FAR_Z)
        if not mine:
            keep = after(keep, targets)
        keep, send = last_step(where, keep, [codes], scale)
        mine.append(keep)
        theirs.append(swap(send, CORE))
    return targets, side_by_side(mine, theirs)


def solution(mesh):
    by_image = P(AXES, None, None)
    return jax.shard_map(
        functools.partial(on_device, dict(mesh.shape)),
        mesh=mesh,
        in_specs=(
            by_image,
            by_image,
            by_image,
            by_image,
            by_image,
            P("dp", None),
            P("dp", None),
            P(AXES, None, None, None),
            by_image,
        ),
        out_specs=(by_image, P(AXES, None)),
        check_vma=False,
    )
```

```python
import functools
import math

import jax
import jax.numpy as jnp
from jax import lax
from jax.experimental import pallas as pl
from jax.experimental.pallas import tpu as pltpu
from jax.sharding import PartitionSpec as P

HEADS = 24
TOP_K = 10
AXES = ("groups", "dp")
VMEM = 24 * 1024 * 1024
COST = 1000
CORE, NEXT_Y, NEXT_Z, FAR_Z = 1, 2, 4, 8
LINE = 4
TAIL = 16


def call(kernel, out_shape, name, scratch=()):
    held = pl.BlockSpec(memory_space=pltpu.VMEM)

    def run(where, *arrays):
        return pl.pallas_call(
            kernel,
            out_shape=tuple(out_shape),
            in_specs=[pl.BlockSpec(memory_space=pltpu.SMEM)] + [held] * len(arrays),
            out_specs=(held,) * len(out_shape),
            scratch_shapes=scratch,
            compiler_params=pltpu.CompilerParams(vmem_limit_bytes=VMEM),
            cost_estimate=pl.CostEstimate(flops=COST, bytes_accessed=COST, transcendentals=0),
            name=name,
        )(where, *arrays)

    return run


def f32(*shape):
    return jax.ShapeDtypeStruct(shape, jnp.float32)


def bf16(*shape):
    return jax.ShapeDtypeStruct(shape, jnp.bfloat16)


def contract_rows(a, b):
    return lax.dot_general(a, b, (((0,), (0,)), ((), ())), preferred_element_type=jnp.float32)


def attention_kernel(where_ref, q_ref, k_ref, v_ref, stream, earlier, out_ref, *bundle, size):
    mixed = []
    for j in range(q_ref.shape[1] // size):
        cols = slice(j * size, (j + 1) * size)
        q = q_ref[:, cols] * jnp.asarray(1.0 / math.sqrt(size), q_ref.dtype)
        scores = lax.dot_general(
            k_ref[:, cols], q, (((1,), (1,)), ((), ())), preferred_element_type=jnp.float32
        )
        weights = jnp.exp(scores - jnp.max(scores, axis=0, keepdims=True))
        weights = weights * (1.0 / jnp.sum(weights, axis=0, keepdims=True))
        mixed.append(contract_rows(weights.astype(jnp.bfloat16), v_ref[:, cols]))
    half = bundle[0].shape[1]
    mixed = jnp.concatenate(mixed, axis=1).astype(out_ref.dtype)
    out_ref[...] = mixed
    theirs = pl.ds(pl.multiple_of((1 - where_ref[0]) * half, half), half)
    bundle[0][...] = mixed[:, :half]
    bundle[1][...] = mixed[:, half:]
    bundle[2][...] = stream[:, theirs]
    bundle[3][...] = earlier[:, theirs]


def attention(where, q, k, v, stream, earlier):
    patches, width = q.shape
    kernel = functools.partial(attention_kernel, size=width // HEADS)
    shapes = [bf16(patches, width)] + [bf16(patches, width // 2)] * 4
    return call(kernel, shapes, "attention")(where, q, k, v, stream, earlier)


def symmetric_product(x, out):
    width = x.shape[1]
    block = 256 if width % 256 == 0 else width
    for at in range(0, width, block):
        here = slice(at, at + block)
        strip = contract_rows(x[:, here], x[:, at:])
        out[here, at:] = strip
        for later in range(at + block, width, block):
            out[later : later + block, here] = strip[:, later - at : later - at + block].T


def gram_kernel(where_ref, hidden_ref, kept_ref, *rest, parted):
    *gram_refs, sum_ref, rows_all, total = rest
    clones, patches = hidden_ref.shape[1:3]
    positions = lax.broadcasted_iota(jnp.int32, (patches, kept_ref.shape[1]), 0)
    sums = None
    for i in range(clones):
        kept = kept_ref[i : i + 1, :]
        covered = jnp.max(jnp.where(positions == kept, 1.0, 0.0), axis=1, keepdims=True)
        rows = hidden_ref[0, i]
        rows = jnp.where(covered > 0.5, jnp.zeros_like(rows), rows)
        rows_all[i * patches : (i + 1) * patches, :] = rows
        wide = rows.astype(jnp.float32)
        sums = wide if sums is None else sums + wide
    sum_ref[...] = sums.astype(sum_ref.dtype)
    if not parted:
        symmetric_product(rows_all, gram_refs[0])
        return
    symmetric_product(rows_all, total)
    mine, *theirs = gram_refs
    core = where_ref[0]
    chips, rows = parted
    for k in range(chips):
        at = pl.multiple_of((2 * k + core) * rows, rows)
        mine[k * rows : (k + 1) * rows, :] = total[pl.ds(at, rows), :]
        at = pl.multiple_of((2 * k + 1 - core) * rows, rows)
        part = k // (chips // len(theirs))
        here = (k % (chips // len(theirs))) * rows
        theirs[part][here : here + rows, :] = total[pl.ds(at, rows), :]


def gram(where, hidden, kept, parted):
    _, clones, patches, width = hidden.shape
    grams = [f32(width // 2, width)] + [f32(width // 4, width)] * 2 if parted else [f32(width, width)]
    scratch = [
        pltpu.VMEM((clones * patches, width), jnp.bfloat16),
        pltpu.VMEM((width, width), jnp.float32),
    ]
    kernel = functools.partial(gram_kernel, parted=parted)
    shapes = grams + [bf16(patches, width)]
    return call(kernel, shapes, "gram", scratch)(where, hidden, kept)


def cut_kernel(where_ref, own, other, out_ref):
    rows, half = own.shape[0], out_ref.shape[1]
    columns = pl.ds(pl.multiple_of(where_ref[0] * half, half), half)
    out_ref[:rows, :] = own[:, columns]
    out_ref[rows:, :] = other[:, columns]


def cut(where, own, other):
    rows, width = own.shape
    return call(cut_kernel, [bf16(2 * rows, width // 2)], "cut")(where, own, other)[0]


def put_in_order(where_ref, pieces, full):
    core, chip = where_ref[0], where_ref[1]
    if len(pieces) == 1:
        full[...] = pieces[0][...]
        return
    for k, piece in enumerate(pieces):
        rows = piece.shape[0] // 2
        base = (chip ^ k) * 2
        for j in range(2):
            at = pl.multiple_of((base + (core ^ j)) * rows, rows)
            full[pl.ds(at, rows), :] = piece[j * rows : (j + 1) * rows, :]


def branch_kernel(where_ref, mixed_own, stream, earlier, *rest):
    others, rest = rest[:4], rest[4:]
    *pieces, blend_ref, stats_ref, full = rest
    put_in_order(where_ref, pieces, full)
    patches, half = stream.shape[0], blend_ref.shape[1]
    columns = pl.ds(pl.multiple_of(where_ref[0] * half, half), half)
    mixeds = (mixed_own[...], jnp.concatenate([others[0][...], others[1][...]], axis=1))
    streams = (stream[:, columns], others[2][...])
    earliers = (earlier[:, columns], others[3][...])
    for i in range(2):
        layer_out = streams[i].astype(jnp.float32) + jnp.dot(
            mixeds[i], full[...], preferred_element_type=jnp.float32
        )
        center = jnp.mean(layer_out, axis=0, keepdims=True)
        away = layer_out - center
        spread = jnp.mean(away * away, axis=0, keepdims=True)
        normed = away * (1.0 / jnp.sqrt(spread + 1e-05))
        blend = ((TOP_K - 1) * earliers[i].astype(jnp.float32) + normed) * (1.0 / TOP_K)
        rows = slice(i * patches, (i + 1) * patches)
        blend_ref[rows, :] = blend
        middle = jnp.mean(blend, axis=1, keepdims=True)
        off = blend - middle
        squares = jnp.sum(off * off, axis=1, keepdims=True)
        lane = lax.broadcasted_iota(jnp.int32, (patches, 128), 1)
        stats_ref[rows, :] = jnp.where(lane < 64, middle, squares)


def branch(where, mixed_own, *others):
    patches, width = mixed_own.shape
    half = width // 2
    shapes = [f32(2 * patches, half), f32(2 * patches, 128)]
    scratch = [pltpu.VMEM((width, half), jnp.bfloat16)]
    return call(branch_kernel, shapes, "branch", scratch)(where, mixed_own, *others)


def encode(values, out_ref):
    rows = values.shape[0]
    top = jnp.max(jnp.abs(values), axis=0, keepdims=True)
    power = jnp.ceil(jnp.log2(jnp.maximum(top, 1e-30))) - 15.0
    codes = jnp.clip(jnp.round(values * jnp.exp2(-power)), -32767.0, 32767.0)
    out_ref[:rows, :] = codes.astype(jnp.int32).astype(jnp.int16)
    out_ref[rows:, :] = jnp.broadcast_to(power, (TAIL, values.shape[1])).astype(jnp.int32).astype(jnp.int16)


def decode(codes):
    rows = codes.shape[0] - TAIL
    power = codes[rows:, :].astype(jnp.int32).astype(jnp.float32)[:1]
    return codes[:rows, :].astype(jnp.int32).astype(jnp.float32) * jnp.exp2(power)


def halve(values, where_ref, send_ref, keep_ref):
    rows = keep_ref.shape[0] // LINE
    y = where_ref[1] % 2

    def blocks(of):
        return [values[pl.ds(pl.multiple_of((2 * z + of) * rows, rows), rows), :] for z in range(LINE)]

    keep_ref[...] = jnp.concatenate(blocks(y), axis=0)
    encode(jnp.concatenate(blocks(1 - y), axis=0), send_ref)


def halve_z(values, where_ref, send_ref, keep_ref):
    rows = keep_ref.shape[0] // 2
    z = where_ref[1] // 2

    def block(of):
        return values[pl.ds(pl.multiple_of(of * rows, rows), rows), :]

    keep_ref[...] = jnp.concatenate([block(z), block(z ^ 2)], axis=0)
    encode(jnp.concatenate([block(z ^ 1), block(z ^ 3)], axis=0), send_ref)


def halve_pairs(values, where_ref, send_ref, keep_ref):
    rows = keep_ref.shape[0] // 2
    y = where_ref[1] % 2

    def blocks(of):
        return [values[pl.ds(pl.multiple_of((2 * z + of) * rows, rows), rows), :] for z in range(2)]

    keep_ref[...] = jnp.concatenate(blocks(y), axis=0)
    encode(jnp.concatenate(blocks(1 - y), axis=0), send_ref)


def halve_far(values, where_ref, send_ref, keep_ref):
    rows = keep_ref.shape[0]
    keep_ref[...] = values[:rows, :]
    encode(values[rows:, :], send_ref)


def halved_shapes(rows, width):
    return [jax.ShapeDtypeStruct((rows // 2 + TAIL, width), jnp.int16), f32(rows // 2, width)]


def first_kernel(where_ref, mine, t0, t1, send_ref, keep_ref, total):
    total[...] = mine[...] + jnp.concatenate([t0[...], t1[...]], axis=0)
    halve(total, where_ref, send_ref, keep_ref)


def first_step(where, mine, theirs):
    scratch = [pltpu.VMEM(mine.shape, jnp.float32)]
    return call(first_kernel, halved_shapes(*mine.shape), "first_step", scratch)(where, mine, *theirs)


def second_kernel(where_ref, keep, codes, own_ref, *rest):
    *send_refs, total = rest
    rows = own_ref.shape[0]
    z = where_ref[1] // 2
    total[...] = keep[...] + decode(codes[...])

    def block(of):
        return total[pl.ds(pl.multiple_of(of * rows, rows), rows), :]

    own_ref[...] = block(z)
    for m, ref in enumerate(send_refs):
        encode(block(z ^ (m + 1)), ref)


def second_step(where, keep, codes):
    rows, width = keep.shape[0] // LINE, keep.shape[1]
    shapes = [f32(rows, width)] + [jax.ShapeDtypeStruct((rows + TAIL, width), jnp.int16)] * (LINE - 1)
    scratch = [pltpu.VMEM(keep.shape, jnp.float32)]
    return call(second_kernel, shapes, "second_step", scratch)(where, keep, codes)


def next_kernel(where_ref, keep, codes, send_ref, keep_ref, total, *, halving):
    total[...] = keep[...] + decode(codes[...])
    halving(total, where_ref, send_ref, keep_ref)


def next_step(where, keep, codes, halving):
    scratch = [pltpu.VMEM(keep.shape, jnp.float32)]
    kernel = functools.partial(next_kernel, halving=halving)
    return call(kernel, halved_shapes(*keep.shape), "next_step", scratch)(where, keep, codes)


def last_kernel(where_ref, own, *rest, scale, count):
    codes, out_refs = rest[:count], rest[count:]
    total = own[...]
    for ref in codes:
        total = total + decode(ref[...])
    if scale is None:
        (pair,) = out_refs
        rows = total.shape[0]
        high = total.astype(jnp.bfloat16)
        pair[:rows, :] = high
        pair[rows:, :] = (total - high.astype(jnp.float32)).astype(jnp.bfloat16)
        return
    keep, send = out_refs
    rows = keep.shape[0]
    first, second = total[:rows, :] * scale, total[rows:, :] * scale
    mine_first = where_ref[0] == 0
    keep[...] = jnp.where(mine_first, first, second)
    send[...] = jnp.where(mine_first, second, first)


def last_step(where, own, codes, scale=None):
    rows, width = own.shape
    shapes = [bf16(2 * rows, width)] if scale is None else [f32(rows // 2, width)] * 2
    return call(functools.partial(last_kernel, scale=scale, count=len(codes)), shapes, "last_step")(where, own, *codes)


def targets_kernel(where_ref, blend, stats, stats_other, sum_own, sum_other, gram_own, gram_other, weights, own_ref, other_ref, *rest, cut, width):
    patches, columns = own_ref.shape
    cols = slice(cut * columns, (cut + 1) * columns)
    rows = weights.shape[0] // 2
    mine, theirs = weights[:rows, cols], weights[rows:, cols]
    grad = contract_rows(
        jnp.concatenate([gram_own[...], gram_other[...]], axis=0),
        jnp.concatenate([mine, mine, theirs, theirs], axis=0),
    )
    for i, (out, features) in enumerate(((own_ref, sum_own), (other_ref, sum_other))):
        mine = stats[i * patches : (i + 1) * patches, :]
        theirs = stats_other[(1 - i) * patches : (2 - i) * patches, :]
        gap = mine[:, :1] - theirs[:, :1]
        middle = 0.5 * (mine[:, :1] + theirs[:, :1])
        squares = mine[:, 64:65] + theirs[:, 64:65] + (width / 4) * gap * gap
        root = 1.0 / jnp.sqrt(squares * (1.0 / width) + 1e-06)
        target = (blend[i * patches : (i + 1) * patches, cols] - middle) * root
        out[...] = target
        grad = grad - contract_rows(features[...], target.astype(jnp.bfloat16))
    if len(rest) == 1:
        rest[0][...] = grad
        return
    send_ref, keep_ref, total = rest
    total[...] = grad
    if cut == 0:
        halve(total, where_ref, send_ref, keep_ref)
    else:
        halve_z(total, where_ref, send_ref, keep_ref)


def targets_and_term(where, blend, stats, stats_other, sum_own, sum_other, grams, weights, part, coded):
    j, n = part
    patches, columns = blend.shape[0] // 2, blend.shape[1] // n
    dec = grams[0].shape[1]
    shapes = [f32(patches, columns)] * 2
    shapes += halved_shapes(dec, columns) if coded else [f32(dec, columns)]
    kernel = functools.partial(targets_kernel, cut=j, width=2 * blend.shape[1])
    scratch = [pltpu.VMEM((dec, columns), jnp.float32)] if coded else []
    return call(kernel, shapes, "targets", scratch)(
        where, blend, stats, stats_other, sum_own, sum_other, *grams, weights
    )


def after(x, *others):
    return lax.optimization_barrier((x,) + others)[0]


def on_device(
    mesh_shape,
    queries,
    key_rows,
    value_rows,
    stream,
    earlier,
    out_weight,
    pred_weight,
    decoder_hidden,
    kept_index,
):
    groups, parts = mesh_shape["groups"], mesh_shape["dp"]
    chips = parts // 2
    patches, width = queries.shape[1:]
    clones, dec = decoder_hidden.shape[1], decoder_hidden.shape[3]
    half = width // 2
    scale = 2.0 / (math.sqrt(width) * clones)
    me = lax.axis_index("dp")
    core, chip = me % 2, me // 2
    where = jnp.stack([core, chip]).astype(jnp.int32)
    same_core = [[2 * k + j for k in range(chips)] for j in range(2)]
    by_pairs = chips == 2 * LINE

    def swap(x, bits):
        pairs = [(g * parts + i, g * parts + (i ^ bits)) for g in range(groups) for i in range(parts)]
        return lax.ppermute(x, AXES, pairs)

    def side_by_side(mine, theirs):
        return jnp.where(
            core == 0,
            jnp.concatenate(mine + theirs, axis=1),
            jnp.concatenate(theirs + mine, axis=1),
        )

    rows = out_weight.shape[0]
    pred_other = swap(pred_weight, CORE)
    if by_pairs:
        gram_mine, *gram_theirs, sum_own = gram(
            where, decoder_hidden, after(kept_index, pred_other)[0], (chips, dec // parts)
        )
    else:
        gram_all, sum_own = gram(where, decoder_hidden, kept_index[0], None)
    out_piece = cut(where, after(out_weight, sum_own), swap(out_weight, CORE))
    pred_piece = cut(where, pred_weight, pred_other)

    def attend(*anchors):
        q = after(queries, *anchors) if anchors else queries
        return attention(where, q[0], key_rows[0], value_rows[0], stream[0], earlier[0])

    if by_pairs:
        z1, z2, y0 = swap(out_piece, NEXT_Z), swap(out_piece, FAR_Z), swap(out_piece, NEXT_Y)
        sum_other = swap(sum_own, CORE)
        gram_theirs = [swap(g, CORE) for g in gram_theirs]
        send, keep = first_step(where, after(gram_mine, y0), gram_theirs)
        y1 = swap(z1, NEXT_Y)
        z3 = swap(after(z2, send), NEXT_Z)
        y2 = swap(after(z2, y0), NEXT_Y)
        own, *codes = second_step(where, after(keep, z2), swap(send, NEXT_Y))
        y3 = swap(after(z3, y1, own), NEXT_Y)
        out_pieces = [out_piece, y0, z1, y1, z2, y2, z3, y3]
        mixed_own, *bundle = attend(z3, pred_piece)
        others = [swap(b, CORE) for b in bundle]
        codes = [swap(c, NEXT_Z * (m + 1)) for m, c in enumerate(codes)]
        (gram_rows,) = last_step(where, after(own, y2), codes)
        mixed_own = after(mixed_own, gram_rows)
    else:
        got = lax.all_gather(out_piece, "dp", axis_index_groups=same_core).reshape(chips, 2, rows, half)
        out_pieces = [jnp.where(core == 0, got, got[:, ::-1]).reshape(width, half)]
        sum_other = swap(sum_own, CORE)
        mixed_own, *bundle = attend()
        others = [swap(b, CORE) for b in bundle]
        gram_rows = lax.psum_scatter(gram_all, "dp", scatter_dimension=0, tiled=True)
        high = gram_rows.astype(jnp.bfloat16)
        low = (gram_rows - high.astype(jnp.float32)).astype(jnp.bfloat16)
        gram_rows = jnp.concatenate([high, low], axis=0)
    grams = [gram_rows, swap(gram_rows, CORE)]

    blend, stats = branch(where, mixed_own, stream[0], earlier[0], *others, *out_pieces)
    stats_other = swap(stats, CORE)

    def term(part, coded, *before):
        return targets_and_term(
            where, blend, stats, after(stats_other, *before), sum_own, sum_other, grams, pred_piece, part, coded
        )

    if not by_pairs:
        target_own, target_other, total = term((0, 1), False)
        targets = side_by_side([target_own], [swap(target_other, CORE)])[None]
        summed = lax.psum_scatter(
            total, "dp", scatter_dimension=0, tiled=True, axis_index_groups=same_core
        )
        summed = (summed * scale).reshape(2, dec // parts, half)
        keep = lax.dynamic_index_in_dim(summed, core, 0, keepdims=False)
        send = lax.dynamic_index_in_dim(summed, 1 - core, 0, keepdims=False)
        return targets, side_by_side([keep], [swap(send, CORE)])

    steps, rest = [], []
    for j, axis in enumerate((NEXT_Y, NEXT_Z)):
        target_own, target_other, send, keep = term((j, 2), True)
        rest.append(swap(target_other, CORE))
        steps.append((target_own, keep, swap(send, axis)))
    targets = side_by_side([x[0] for x in steps], rest)[None]
    mine, theirs = [], []
    for (_, keep, codes), halving, axis in zip(steps, (halve_z, halve_pairs), (NEXT_Z, NEXT_Y)):
        send, keep = next_step(where, keep, codes, halving)
        codes = swap(send, axis)
        send, keep = next_step(where, keep, codes, halve_far)
        codes = swap(send, FAR_Z)
        if not mine:
            keep = after(keep, targets)
        keep, send = last_step(where, keep, [codes], scale)
        mine.append(keep)
        theirs.append(swap(send, CORE))
    return targets, side_by_side(mine, theirs)


def solution(mesh):
    by_image = P(AXES, None, None)
    return jax.shard_map(
        functools.partial(on_device, dict(mesh.shape)),
        mesh=mesh,
        in_specs=(
            by_image,
            by_image,
            by_image,
            by_image,
            by_image,
            P("dp", None),
            P("dp", None),
            P(AXES, None, None, None),
            by_image,
        ),
        out_specs=(by_image, P(AXES, None)),
        check_vma=False,
    )
```

```python
import functools
import math

import jax
import jax.numpy as jnp
from jax import lax
from jax.experimental import pallas as pl
from jax.experimental.pallas import tpu as pltpu
from jax.sharding import PartitionSpec as P

HEADS = 24
TOP_K = 10
AXES = ("groups", "dp")
VMEM = 24 * 1024 * 1024
COST = 1000
CORE, NEXT_Y, NEXT_Z, FAR_Z = 1, 2, 4, 8
LINE = 4
TAIL = 16


def call(kernel, out_shape, name, scratch=()):
    held = pl.BlockSpec(memory_space=pltpu.VMEM)

    def run(where, *arrays):
        return pl.pallas_call(
            kernel,
            out_shape=tuple(out_shape),
            in_specs=[pl.BlockSpec(memory_space=pltpu.SMEM)] + [held] * len(arrays),
            out_specs=(held,) * len(out_shape),
            scratch_shapes=scratch,
            compiler_params=pltpu.CompilerParams(vmem_limit_bytes=VMEM),
            cost_estimate=pl.CostEstimate(flops=COST, bytes_accessed=COST, transcendentals=0),
            name=name,
        )(where, *arrays)

    return run


def f32(*shape):
    return jax.ShapeDtypeStruct(shape, jnp.float32)


def bf16(*shape):
    return jax.ShapeDtypeStruct(shape, jnp.bfloat16)


def contract_rows(a, b):
    return lax.dot_general(a, b, (((0,), (0,)), ((), ())), preferred_element_type=jnp.float32)


def attention_kernel(where_ref, q_ref, k_ref, v_ref, stream, earlier, out_ref, *bundle, size):
    mixed = []
    for j in range(q_ref.shape[1] // size):
        cols = slice(j * size, (j + 1) * size)
        q = q_ref[:, cols] * jnp.asarray(1.0 / math.sqrt(size), q_ref.dtype)
        scores = lax.dot_general(
            k_ref[:, cols], q, (((1,), (1,)), ((), ())), preferred_element_type=jnp.float32
        )
        weights = jnp.exp(scores - jnp.max(scores, axis=0, keepdims=True))
        weights = weights * (1.0 / jnp.sum(weights, axis=0, keepdims=True))
        mixed.append(contract_rows(weights.astype(jnp.bfloat16), v_ref[:, cols]))
    half = bundle[0].shape[1]
    mixed = jnp.concatenate(mixed, axis=1).astype(out_ref.dtype)
    out_ref[...] = mixed
    theirs = pl.ds(pl.multiple_of((1 - where_ref[0]) * half, half), half)
    bundle[0][...] = mixed[:, :half]
    bundle[1][...] = mixed[:, half:]
    bundle[2][...] = stream[:, theirs]
    bundle[3][...] = earlier[:, theirs]


def attention(where, q, k, v, stream, earlier):
    patches, width = q.shape
    kernel = functools.partial(attention_kernel, size=width // HEADS)
    shapes = [bf16(patches, width)] + [bf16(patches, width // 2)] * 4
    return call(kernel, shapes, "attention")(where, q, k, v, stream, earlier)


def symmetric_product(x, out):
    width = x.shape[1]
    block = 256 if width % 256 == 0 else width
    for at in range(0, width, block):
        here = slice(at, at + block)
        strip = contract_rows(x[:, here], x[:, at:])
        out[here, at:] = strip
        for later in range(at + block, width, block):
            out[later : later + block, here] = strip[:, later - at : later - at + block].T


def gram_kernel(where_ref, hidden_ref, kept_ref, *rest, parted):
    *gram_refs, sum_ref, rows_all, total = rest
    clones, patches = hidden_ref.shape[1:3]
    positions = lax.broadcasted_iota(jnp.int32, (patches, kept_ref.shape[1]), 0)
    sums = None
    for i in range(clones):
        kept = kept_ref[i : i + 1, :]
        covered = jnp.max(jnp.where(positions == kept, 1.0, 0.0), axis=1, keepdims=True)
        rows = hidden_ref[0, i]
        rows = jnp.where(covered > 0.5, jnp.zeros_like(rows), rows)
        rows_all[i * patches : (i + 1) * patches, :] = rows
        wide = rows.astype(jnp.float32)
        sums = wide if sums is None else sums + wide
    sum_ref[...] = sums.astype(sum_ref.dtype)
    if not parted:
        symmetric_product(rows_all, gram_refs[0])
        return
    symmetric_product(rows_all, total)
    mine, *theirs = gram_refs
    core = where_ref[0]
    chips, rows = parted
    for k in range(chips):
        at = pl.multiple_of((2 * k + core) * rows, rows)
        mine[k * rows : (k + 1) * rows, :] = total[pl.ds(at, rows), :]
        at = pl.multiple_of((2 * k + 1 - core) * rows, rows)
        part = k // (chips // len(theirs))
        here = (k % (chips // len(theirs))) * rows
        theirs[part][here : here + rows, :] = total[pl.ds(at, rows), :]


def gram(where, hidden, kept, parted):
    _, clones, patches, width = hidden.shape
    grams = [f32(width // 2, width)] + [f32(width // 4, width)] * 2 if parted else [f32(width, width)]
    scratch = [
        pltpu.VMEM((clones * patches, width), jnp.bfloat16),
        pltpu.VMEM((width, width), jnp.float32),
    ]
    kernel = functools.partial(gram_kernel, parted=parted)
    shapes = grams + [bf16(patches, width)]
    return call(kernel, shapes, "gram", scratch)(where, hidden, kept)


def cut_kernel(where_ref, own, other, out_ref):
    rows, half = own.shape[0], out_ref.shape[1]
    columns = pl.ds(pl.multiple_of(where_ref[0] * half, half), half)
    out_ref[:rows, :] = own[:, columns]
    out_ref[rows:, :] = other[:, columns]


def cut(where, own, other):
    rows, width = own.shape
    return call(cut_kernel, [bf16(2 * rows, width // 2)], "cut")(where, own, other)[0]


def put_in_order(where_ref, pieces, full):
    core, chip = where_ref[0], where_ref[1]
    if len(pieces) == 1:
        full[...] = pieces[0][...]
        return
    for k, piece in enumerate(pieces):
        rows = piece.shape[0] // 2
        base = (chip ^ k) * 2
        for j in range(2):
            at = pl.multiple_of((base + (core ^ j)) * rows, rows)
            full[pl.ds(at, rows), :] = piece[j * rows : (j + 1) * rows, :]


def branch_kernel(where_ref, mixed_own, stream, earlier, *rest):
    others, rest = rest[:4], rest[4:]
    *pieces, blend_ref, stats_ref, full = rest
    put_in_order(where_ref, pieces, full)
    patches, half = stream.shape[0], blend_ref.shape[1]
    columns = pl.ds(pl.multiple_of(where_ref[0] * half, half), half)
    mixeds = (mixed_own[...], jnp.concatenate([others[0][...], others[1][...]], axis=1))
    streams = (stream[:, columns], others[2][...])
    earliers = (earlier[:, columns], others[3][...])
    for i in range(2):
        layer_out = streams[i].astype(jnp.float32) + jnp.dot(
            mixeds[i], full[...], preferred_element_type=jnp.float32
        )
        center = jnp.mean(layer_out, axis=0, keepdims=True)
        away = layer_out - center
        spread = jnp.mean(away * away, axis=0, keepdims=True)
        normed = away * (1.0 / jnp.sqrt(spread + 1e-05))
        blend = ((TOP_K - 1) * earliers[i].astype(jnp.float32) + normed) * (1.0 / TOP_K)
        rows = slice(i * patches, (i + 1) * patches)
        blend_ref[rows, :] = blend
        middle = jnp.mean(blend, axis=1, keepdims=True)
        off = blend - middle
        squares = jnp.sum(off * off, axis=1, keepdims=True)
        lane = lax.broadcasted_iota(jnp.int32, (patches, 128), 1)
        stats_ref[rows, :] = jnp.where(lane < 64, middle, squares)


def branch(where, mixed_own, *others):
    patches, width = mixed_own.shape
    half = width // 2
    shapes = [f32(2 * patches, half), f32(2 * patches, 128)]
    scratch = [pltpu.VMEM((width, half), jnp.bfloat16)]
    return call(branch_kernel, shapes, "branch", scratch)(where, mixed_own, *others)


def encode(values, out_ref):
    rows = values.shape[0]
    top = jnp.max(jnp.abs(values), axis=0, keepdims=True)
    power = jnp.ceil(jnp.log2(jnp.maximum(top, 1e-30))) - 15.0
    codes = jnp.clip(jnp.round(values * jnp.exp2(-power)), -32767.0, 32767.0)
    out_ref[:rows, :] = codes.astype(jnp.int32).astype(jnp.int16)
    out_ref[rows:, :] = jnp.broadcast_to(power, (TAIL, values.shape[1])).astype(jnp.int32).astype(jnp.int16)


def decode(codes):
    rows = codes.shape[0] - TAIL
    power = codes[rows:, :].astype(jnp.int32).astype(jnp.float32)[:1]
    return codes[:rows, :].astype(jnp.int32).astype(jnp.float32) * jnp.exp2(power)


def halve(values, where_ref, send_ref, keep_ref):
    rows = keep_ref.shape[0] // LINE
    y = where_ref[1] % 2

    def blocks(of):
        return [values[pl.ds(pl.multiple_of((2 * z + of) * rows, rows), rows), :] for z in range(LINE)]

    keep_ref[...] = jnp.concatenate(blocks(y), axis=0)
    encode(jnp.concatenate(blocks(1 - y), axis=0), send_ref)


def halve_z(values, where_ref, send_ref, keep_ref):
    rows = keep_ref.shape[0] // 2
    z = where_ref[1] // 2

    def block(of):
        return values[pl.ds(pl.multiple_of(of * rows, rows), rows), :]

    keep_ref[...] = jnp.concatenate([block(z), block(z ^ 2)], axis=0)
    encode(jnp.concatenate([block(z ^ 1), block(z ^ 3)], axis=0), send_ref)


def halve_pairs(values, where_ref, send_ref, keep_ref):
    rows = keep_ref.shape[0] // 2
    y = where_ref[1] % 2

    def blocks(of):
        return [values[pl.ds(pl.multiple_of((2 * z + of) * rows, rows), rows), :] for z in range(2)]

    keep_ref[...] = jnp.concatenate(blocks(y), axis=0)
    encode(jnp.concatenate(blocks(1 - y), axis=0), send_ref)


def halve_far(values, where_ref, send_ref, keep_ref):
    rows = keep_ref.shape[0]
    keep_ref[...] = values[:rows, :]
    encode(values[rows:, :], send_ref)


def halved_shapes(rows, width):
    return [jax.ShapeDtypeStruct((rows // 2 + TAIL, width), jnp.int16), f32(rows // 2, width)]


def first_kernel(where_ref, mine, t0, t1, send_ref, keep_ref, total):
    total[...] = mine[...] + jnp.concatenate([t0[...], t1[...]], axis=0)
    halve(total, where_ref, send_ref, keep_ref)


def first_step(where, mine, theirs):
    scratch = [pltpu.VMEM(mine.shape, jnp.float32)]
    return call(first_kernel, halved_shapes(*mine.shape), "first_step", scratch)(where, mine, *theirs)


def second_kernel(where_ref, keep, codes, own_ref, *rest):
    *send_refs, total = rest
    rows = own_ref.shape[0]
    z = where_ref[1] // 2
    total[...] = keep[...] + decode(codes[...])

    def block(of):
        return total[pl.ds(pl.multiple_of(of * rows, rows), rows), :]

    own_ref[...] = block(z)
    for m, ref in enumerate(send_refs):
        encode(block(z ^ (m + 1)), ref)


def second_step(where, keep, codes):
    rows, width = keep.shape[0] // LINE, keep.shape[1]
    shapes = [f32(rows, width)] + [jax.ShapeDtypeStruct((rows + TAIL, width), jnp.int16)] * (LINE - 1)
    scratch = [pltpu.VMEM(keep.shape, jnp.float32)]
    return call(second_kernel, shapes, "second_step", scratch)(where, keep, codes)


def next_kernel(where_ref, keep, codes, send_ref, keep_ref, total, *, halving):
    total[...] = keep[...] + decode(codes[...])
    halving(total, where_ref, send_ref, keep_ref)


def next_step(where, keep, codes, halving):
    scratch = [pltpu.VMEM(keep.shape, jnp.float32)]
    kernel = functools.partial(next_kernel, halving=halving)
    return call(kernel, halved_shapes(*keep.shape), "next_step", scratch)(where, keep, codes)


def last_kernel(where_ref, own, *rest, scale, count):
    codes, out_refs = rest[:count], rest[count:]
    total = own[...]
    for ref in codes:
        total = total + decode(ref[...])
    if scale is None:
        (pair,) = out_refs
        rows = total.shape[0]
        high = total.astype(jnp.bfloat16)
        pair[:rows, :] = high
        pair[rows:, :] = (total - high.astype(jnp.float32)).astype(jnp.bfloat16)
        return
    keep, send = out_refs
    rows = keep.shape[0]
    first, second = total[:rows, :] * scale, total[rows:, :] * scale
    mine_first = where_ref[0] == 0
    keep[...] = jnp.where(mine_first, first, second)
    send[...] = jnp.where(mine_first, second, first)


def last_step(where, own, codes, scale=None):
    rows, width = own.shape
    shapes = [bf16(2 * rows, width)] if scale is None else [f32(rows // 2, width)] * 2
    return call(functools.partial(last_kernel, scale=scale, count=len(codes)), shapes, "last_step")(where, own, *codes)


def targets_kernel(where_ref, blend, stats, stats_other, sum_own, sum_other, gram_own, gram_other, weights, own_ref, other_ref, *rest, cut, width):
    patches, columns = own_ref.shape
    cols = slice(cut * columns, (cut + 1) * columns)
    rows = weights.shape[0] // 2
    mine, theirs = weights[:rows, cols], weights[rows:, cols]
    grad = contract_rows(
        jnp.concatenate([gram_own[...], gram_other[...]], axis=0),
        jnp.concatenate([mine, mine, theirs, theirs], axis=0),
    )
    for i, (out, features) in enumerate(((own_ref, sum_own), (other_ref, sum_other))):
        mine = stats[i * patches : (i + 1) * patches, :]
        theirs = stats_other[(1 - i) * patches : (2 - i) * patches, :]
        gap = mine[:, :1] - theirs[:, :1]
        middle = 0.5 * (mine[:, :1] + theirs[:, :1])
        squares = mine[:, 64:65] + theirs[:, 64:65] + (width / 4) * gap * gap
        root = 1.0 / jnp.sqrt(squares * (1.0 / width) + 1e-06)
        target = (blend[i * patches : (i + 1) * patches, cols] - middle) * root
        out[...] = target
        grad = grad - contract_rows(features[...], target.astype(jnp.bfloat16))
    if len(rest) == 1:
        rest[0][...] = grad
        return
    send_ref, keep_ref, total = rest
    total[...] = grad
    if cut == 0:
        halve(total, where_ref, send_ref, keep_ref)
    else:
        halve_z(total, where_ref, send_ref, keep_ref)


def targets_and_term(where, blend, stats, stats_other, sum_own, sum_other, grams, weights, part, coded):
    j, n = part
    patches, columns = blend.shape[0] // 2, blend.shape[1] // n
    dec = grams[0].shape[1]
    shapes = [f32(patches, columns)] * 2
    shapes += halved_shapes(dec, columns) if coded else [f32(dec, columns)]
    kernel = functools.partial(targets_kernel, cut=j, width=2 * blend.shape[1])
    scratch = [pltpu.VMEM((dec, columns), jnp.float32)] if coded else []
    return call(kernel, shapes, "targets", scratch)(
        where, blend, stats, stats_other, sum_own, sum_other, *grams, weights
    )


def after(x, *others):
    return lax.optimization_barrier((x,) + others)[0]


def on_device(
    mesh_shape,
    queries,
    key_rows,
    value_rows,
    stream,
    earlier,
    out_weight,
    pred_weight,
    decoder_hidden,
    kept_index,
):
    groups, parts = mesh_shape["groups"], mesh_shape["dp"]
    chips = parts // 2
    patches, width = queries.shape[1:]
    clones, dec = decoder_hidden.shape[1], decoder_hidden.shape[3]
    half = width // 2
    scale = 2.0 / (math.sqrt(width) * clones)
    me = lax.axis_index("dp")
    core, chip = me % 2, me // 2
    where = jnp.stack([core, chip]).astype(jnp.int32)
    same_core = [[2 * k + j for k in range(chips)] for j in range(2)]
    by_pairs = chips == 2 * LINE

    def swap(x, bits):
        pairs = [(g * parts + i, g * parts + (i ^ bits)) for g in range(groups) for i in range(parts)]
        return lax.ppermute(x, AXES, pairs)

    def side_by_side(mine, theirs):
        return jnp.where(
            core == 0,
            jnp.concatenate(mine + theirs, axis=1),
            jnp.concatenate(theirs + mine, axis=1),
        )

    rows = out_weight.shape[0]
    pred_other = swap(pred_weight, CORE)
    if by_pairs:
        gram_mine, *gram_theirs, sum_own = gram(
            where, decoder_hidden, kept_index[0], (chips, dec // parts)
        )
    else:
        gram_all, sum_own = gram(where, decoder_hidden, kept_index[0], None)
    out_piece = cut(where, after(out_weight, sum_own), swap(out_weight, CORE))
    pred_piece = cut(where, pred_weight, pred_other)

    def attend(*anchors):
        q = after(queries, *anchors) if anchors else queries
        return attention(where, q[0], key_rows[0], value_rows[0], stream[0], earlier[0])

    if by_pairs:
        z1, z2, y0 = swap(out_piece, NEXT_Z), swap(out_piece, FAR_Z), swap(out_piece, NEXT_Y)
        sum_other = swap(sum_own, CORE)
        gram_theirs = [swap(after(g, pred_other), CORE) for g in gram_theirs]
        send, keep = first_step(where, after(gram_mine, y0), gram_theirs)
        y1 = swap(z1, NEXT_Y)
        z3 = swap(after(z2, send), NEXT_Z)
        y2 = swap(after(z2, y0), NEXT_Y)
        own, *codes = second_step(where, after(keep, z2), swap(send, NEXT_Y))
        y3 = swap(after(z3, y1, own), NEXT_Y)
        out_pieces = [out_piece, y0, z1, y1, z2, y2, z3, y3]
        mixed_own, *bundle = attend(z3, pred_piece)
        others = [swap(b, CORE) for b in bundle]
        codes = [swap(c, NEXT_Z * (m + 1)) for m, c in enumerate(codes)]
        (gram_rows,) = last_step(where, after(own, y2), codes)
        mixed_own = after(mixed_own, gram_rows)
    else:
        got = lax.all_gather(out_piece, "dp", axis_index_groups=same_core).reshape(chips, 2, rows, half)
        out_pieces = [jnp.where(core == 0, got, got[:, ::-1]).reshape(width, half)]
        sum_other = swap(sum_own, CORE)
        mixed_own, *bundle = attend()
        others = [swap(b, CORE) for b in bundle]
        gram_rows = lax.psum_scatter(gram_all, "dp", scatter_dimension=0, tiled=True)
        high = gram_rows.astype(jnp.bfloat16)
        low = (gram_rows - high.astype(jnp.float32)).astype(jnp.bfloat16)
        gram_rows = jnp.concatenate([high, low], axis=0)
    grams = [gram_rows, swap(gram_rows, CORE)]

    blend, stats = branch(where, mixed_own, stream[0], earlier[0], *others, *out_pieces)
    stats_other = swap(stats, CORE)

    def term(part, coded, *before):
        return targets_and_term(
            where, blend, stats, after(stats_other, *before), sum_own, sum_other, grams, pred_piece, part, coded
        )

    if not by_pairs:
        target_own, target_other, total = term((0, 1), False)
        targets = side_by_side([target_own], [swap(target_other, CORE)])[None]
        summed = lax.psum_scatter(
            total, "dp", scatter_dimension=0, tiled=True, axis_index_groups=same_core
        )
        summed = (summed * scale).reshape(2, dec // parts, half)
        keep = lax.dynamic_index_in_dim(summed, core, 0, keepdims=False)
        send = lax.dynamic_index_in_dim(summed, 1 - core, 0, keepdims=False)
        return targets, side_by_side([keep], [swap(send, CORE)])

    steps, rest = [], []
    for j, axis in enumerate((NEXT_Y, NEXT_Z)):
        target_own, target_other, send, keep = term((j, 2), True)
        rest.append(swap(target_other, CORE))
        steps.append((target_own, keep, swap(send, axis)))
    targets = side_by_side([x[0] for x in steps], rest)[None]
    mine, theirs = [], []
    for (_, keep, codes), halving, axis in zip(steps, (halve_z, halve_pairs), (NEXT_Z, NEXT_Y)):
        send, keep = next_step(where, keep, codes, halving)
        codes = swap(send, axis)
        send, keep = next_step(where, keep, codes, halve_far)
        codes = swap(send, FAR_Z)
        if not mine:
            keep = after(keep, targets)
        keep, send = last_step(where, keep, [codes], scale)
        mine.append(keep)
        theirs.append(swap(send, CORE))
    return targets, side_by_side(mine, theirs)


def solution(mesh):
    by_image = P(AXES, None, None)
    return jax.shard_map(
        functools.partial(on_device, dict(mesh.shape)),
        mesh=mesh,
        in_specs=(
            by_image,
            by_image,
            by_image,
            by_image,
            by_image,
            P("dp", None),
            P("dp", None),
            P(AXES, None, None, None),
            by_image,
        ),
        out_specs=(by_image, P(AXES, None)),
        check_vma=False,
    )
```

```python
import functools
import math

import jax
import jax.numpy as jnp
from jax import lax
from jax.experimental import pallas as pl
from jax.experimental.pallas import tpu as pltpu
from jax.sharding import PartitionSpec as P

HEADS = 24
TOP_K = 10
AXES = ("groups", "dp")
VMEM = 24 * 1024 * 1024
COST = 1000
CORE, NEXT_Y, NEXT_Z, FAR_Z = 1, 2, 4, 8
LINE = 4
TAIL = 16


def call(kernel, out_shape, name, scratch=()):
    held = pl.BlockSpec(memory_space=pltpu.VMEM)

    def run(where, *arrays):
        return pl.pallas_call(
            kernel,
            out_shape=tuple(out_shape),
            in_specs=[pl.BlockSpec(memory_space=pltpu.SMEM)] + [held] * len(arrays),
            out_specs=(held,) * len(out_shape),
            scratch_shapes=scratch,
            compiler_params=pltpu.CompilerParams(vmem_limit_bytes=VMEM),
            cost_estimate=pl.CostEstimate(flops=COST, bytes_accessed=COST, transcendentals=0),
            name=name,
        )(where, *arrays)

    return run


def f32(*shape):
    return jax.ShapeDtypeStruct(shape, jnp.float32)


def bf16(*shape):
    return jax.ShapeDtypeStruct(shape, jnp.bfloat16)


def contract_rows(a, b):
    return lax.dot_general(a, b, (((0,), (0,)), ((), ())), preferred_element_type=jnp.float32)


def attention_kernel(where_ref, q_ref, k_ref, v_ref, stream, earlier, out_ref, *bundle, size):
    mixed = []
    for j in range(q_ref.shape[1] // size):
        cols = slice(j * size, (j + 1) * size)
        q = q_ref[:, cols] * jnp.asarray(1.0 / math.sqrt(size), q_ref.dtype)
        scores = lax.dot_general(
            k_ref[:, cols], q, (((1,), (1,)), ((), ())), preferred_element_type=jnp.float32
        )
        weights = jnp.exp(scores - jnp.max(scores, axis=0, keepdims=True))
        weights = weights * (1.0 / jnp.sum(weights, axis=0, keepdims=True))
        mixed.append(contract_rows(weights.astype(jnp.bfloat16), v_ref[:, cols]))
    half = bundle[0].shape[1]
    mixed = jnp.concatenate(mixed, axis=1).astype(out_ref.dtype)
    out_ref[...] = mixed
    theirs = pl.ds(pl.multiple_of((1 - where_ref[0]) * half, half), half)
    bundle[0][...] = mixed[:, :half]
    bundle[1][...] = mixed[:, half:]
    bundle[2][...] = stream[:, theirs]
    bundle[3][...] = earlier[:, theirs]


def attention(where, q, k, v, stream, earlier):
    patches, width = q.shape
    kernel = functools.partial(attention_kernel, size=width // HEADS)
    shapes = [bf16(patches, width)] + [bf16(patches, width // 2)] * 4
    return call(kernel, shapes, "attention")(where, q, k, v, stream, earlier)


def symmetric_product(x, out):
    width = x.shape[1]
    block = 256 if width % 256 == 0 else width
    for at in range(0, width, block):
        here = slice(at, at + block)
        strip = contract_rows(x[:, here], x[:, at:])
        out[here, at:] = strip
        for later in range(at + block, width, block):
            out[later : later + block, here] = strip[:, later - at : later - at + block].T


def gram_kernel(where_ref, hidden_ref, kept_ref, *rest, parted):
    *gram_refs, sum_ref, rows_all, total = rest
    clones, patches = hidden_ref.shape[1:3]
    positions = lax.broadcasted_iota(jnp.int32, (patches, kept_ref.shape[1]), 0)
    sums = None
    for i in range(clones):
        kept = kept_ref[i : i + 1, :]
        covered = jnp.max(jnp.where(positions == kept, 1.0, 0.0), axis=1, keepdims=True)
        rows = hidden_ref[0, i]
        rows = jnp.where(covered > 0.5, jnp.zeros_like(rows), rows)
        rows_all[i * patches : (i + 1) * patches, :] = rows
        wide = rows.astype(jnp.float32)
        sums = wide if sums is None else sums + wide
    sum_ref[...] = sums.astype(sum_ref.dtype)
    if not parted:
        symmetric_product(rows_all, gram_refs[0])
        return
    symmetric_product(rows_all, total)
    mine, *theirs = gram_refs
    core = where_ref[0]
    chips, rows = parted
    for k in range(chips):
        at = pl.multiple_of((2 * k + core) * rows, rows)
        mine[k * rows : (k + 1) * rows, :] = total[pl.ds(at, rows), :]
        at = pl.multiple_of((2 * k + 1 - core) * rows, rows)
        part = k // (chips // len(theirs))
        here = (k % (chips // len(theirs))) * rows
        theirs[part][here : here + rows, :] = total[pl.ds(at, rows), :]


def gram(where, hidden, kept, parted):
    _, clones, patches, width = hidden.shape
    grams = [f32(width // 2, width)] + [f32(width // 4, width)] * 2 if parted else [f32(width, width)]
    scratch = [
        pltpu.VMEM((clones * patches, width), jnp.bfloat16),
        pltpu.VMEM((width, width), jnp.float32),
    ]
    kernel = functools.partial(gram_kernel, parted=parted)
    shapes = grams + [bf16(patches, width)]
    return call(kernel, shapes, "gram", scratch)(where, hidden, kept)


def cut_kernel(where_ref, own, other, out_ref):
    rows, half = own.shape[0], out_ref.shape[1]
    columns = pl.ds(pl.multiple_of(where_ref[0] * half, half), half)
    out_ref[:rows, :] = own[:, columns]
    out_ref[rows:, :] = other[:, columns]


def cut(where, own, other):
    rows, width = own.shape
    return call(cut_kernel, [bf16(2 * rows, width // 2)], "cut")(where, own, other)[0]


def put_in_order(where_ref, pieces, full):
    core, chip = where_ref[0], where_ref[1]
    if len(pieces) == 1:
        full[...] = pieces[0][...]
        return
    for k, piece in enumerate(pieces):
        rows = piece.shape[0] // 2
        base = (chip ^ k) * 2
        for j in range(2):
            at = pl.multiple_of((base + (core ^ j)) * rows, rows)
            full[pl.ds(at, rows), :] = piece[j * rows : (j + 1) * rows, :]


def branch_kernel(where_ref, mixed_own, stream, earlier, *rest):
    others, rest = rest[:4], rest[4:]
    *pieces, blend_ref, stats_ref, full = rest
    put_in_order(where_ref, pieces, full)
    patches, half = stream.shape[0], blend_ref.shape[1]
    columns = pl.ds(pl.multiple_of(where_ref[0] * half, half), half)
    mixeds = (mixed_own[...], jnp.concatenate([others[0][...], others[1][...]], axis=1))
    streams = (stream[:, columns], others[2][...])
    earliers = (earlier[:, columns], others[3][...])
    for i in range(2):
        layer_out = streams[i].astype(jnp.float32) + jnp.dot(
            mixeds[i], full[...], preferred_element_type=jnp.float32
        )
        center = jnp.mean(layer_out, axis=0, keepdims=True)
        away = layer_out - center
        spread = jnp.mean(away * away, axis=0, keepdims=True)
        normed = away * (1.0 / jnp.sqrt(spread + 1e-05))
        blend = ((TOP_K - 1) * earliers[i].astype(jnp.float32) + normed) * (1.0 / TOP_K)
        rows = slice(i * patches, (i + 1) * patches)
        blend_ref[rows, :] = blend
        middle = jnp.mean(blend, axis=1, keepdims=True)
        off = blend - middle
        squares = jnp.sum(off * off, axis=1, keepdims=True)
        lane = lax.broadcasted_iota(jnp.int32, (patches, 128), 1)
        stats_ref[rows, :] = jnp.where(lane < 64, middle, squares)


def branch(where, mixed_own, *others):
    patches, width = mixed_own.shape
    half = width // 2
    shapes = [f32(2 * patches, half), f32(2 * patches, 128)]
    scratch = [pltpu.VMEM((width, half), jnp.bfloat16)]
    return call(branch_kernel, shapes, "branch", scratch)(where, mixed_own, *others)


def encode(values, out_ref):
    rows = values.shape[0]
    top = jnp.max(jnp.abs(values), axis=0, keepdims=True)
    power = jnp.ceil(jnp.log2(jnp.maximum(top, 1e-30))) - 15.0
    codes = jnp.clip(jnp.round(values * jnp.exp2(-power)), -32767.0, 32767.0)
    out_ref[:rows, :] = codes.astype(jnp.int32).astype(jnp.int16)
    out_ref[rows:, :] = jnp.broadcast_to(power, (TAIL, values.shape[1])).astype(jnp.int32).astype(jnp.int16)


def decode(codes):
    rows = codes.shape[0] - TAIL
    power = codes[rows:, :].astype(jnp.int32).astype(jnp.float32)[:1]
    return codes[:rows, :].astype(jnp.int32).astype(jnp.float32) * jnp.exp2(power)


def halve(values, where_ref, send_ref, keep_ref):
    rows = keep_ref.shape[0] // LINE
    y = where_ref[1] % 2

    def blocks(of):
        return [values[pl.ds(pl.multiple_of((2 * z + of) * rows, rows), rows), :] for z in range(LINE)]

    keep_ref[...] = jnp.concatenate(blocks(y), axis=0)
    encode(jnp.concatenate(blocks(1 - y), axis=0), send_ref)


def halve_z(values, where_ref, send_ref, keep_ref):
    rows = keep_ref.shape[0] // 2
    z = where_ref[1] // 2

    def block(of):
        return values[pl.ds(pl.multiple_of(of * rows, rows), rows), :]

    keep_ref[...] = jnp.concatenate([block(z), block(z ^ 2)], axis=0)
    encode(jnp.concatenate([block(z ^ 1), block(z ^ 3)], axis=0), send_ref)


def halve_pairs(values, where_ref, send_ref, keep_ref):
    rows = keep_ref.shape[0] // 2
    y = where_ref[1] % 2

    def blocks(of):
        return [values[pl.ds(pl.multiple_of((2 * z + of) * rows, rows), rows), :] for z in range(2)]

    keep_ref[...] = jnp.concatenate(blocks(y), axis=0)
    encode(jnp.concatenate(blocks(1 - y), axis=0), send_ref)


def halve_far(values, where_ref, send_ref, keep_ref):
    rows = keep_ref.shape[0]
    keep_ref[...] = values[:rows, :]
    encode(values[rows:, :], send_ref)


def halved_shapes(rows, width):
    return [jax.ShapeDtypeStruct((rows // 2 + TAIL, width), jnp.int16), f32(rows // 2, width)]


def first_kernel(where_ref, mine, t0, t1, send_ref, keep_ref, total):
    total[...] = mine[...] + jnp.concatenate([t0[...], t1[...]], axis=0)
    halve(total, where_ref, send_ref, keep_ref)


def first_step(where, mine, theirs):
    scratch = [pltpu.VMEM(mine.shape, jnp.float32)]
    return call(first_kernel, halved_shapes(*mine.shape), "first_step", scratch)(where, mine, *theirs)


def second_kernel(where_ref, keep, codes, own_ref, *rest):
    *send_refs, total = rest
    rows = own_ref.shape[0]
    z = where_ref[1] // 2
    total[...] = keep[...] + decode(codes[...])

    def block(of):
        return total[pl.ds(pl.multiple_of(of * rows, rows), rows), :]

    own_ref[...] = block(z)
    for m, ref in enumerate(send_refs):
        encode(block(z ^ (m + 1)), ref)


def second_step(where, keep, codes):
    rows, width = keep.shape[0] // LINE, keep.shape[1]
    shapes = [f32(rows, width)] + [jax.ShapeDtypeStruct((rows + TAIL, width), jnp.int16)] * (LINE - 1)
    scratch = [pltpu.VMEM(keep.shape, jnp.float32)]
    return call(second_kernel, shapes, "second_step", scratch)(where, keep, codes)


def next_kernel(where_ref, keep, codes, send_ref, keep_ref, total, *, halving):
    total[...] = keep[...] + decode(codes[...])
    halving(total, where_ref, send_ref, keep_ref)


def next_step(where, keep, codes, halving):
    scratch = [pltpu.VMEM(keep.shape, jnp.float32)]
    kernel = functools.partial(next_kernel, halving=halving)
    return call(kernel, halved_shapes(*keep.shape), "next_step", scratch)(where, keep, codes)


def last_kernel(where_ref, own, *rest, scale, count):
    codes, out_refs = rest[:count], rest[count:]
    total = own[...]
    for ref in codes:
        total = total + decode(ref[...])
    if scale is None:
        (pair,) = out_refs
        rows = total.shape[0]
        high = total.astype(jnp.bfloat16)
        pair[:rows, :] = high
        pair[rows:, :] = (total - high.astype(jnp.float32)).astype(jnp.bfloat16)
        return
    keep, send = out_refs
    rows = keep.shape[0]
    first, second = total[:rows, :] * scale, total[rows:, :] * scale
    mine_first = where_ref[0] == 0
    keep[...] = jnp.where(mine_first, first, second)
    send[...] = jnp.where(mine_first, second, first)


def last_step(where, own, codes, scale=None):
    rows, width = own.shape
    shapes = [bf16(2 * rows, width)] if scale is None else [f32(rows // 2, width)] * 2
    return call(functools.partial(last_kernel, scale=scale, count=len(codes)), shapes, "last_step")(where, own, *codes)


def targets_kernel(where_ref, blend, stats, stats_other, sum_own, sum_other, gram_own, gram_other, weight_own, weight_other, own_ref, other_ref, *rest, cut, width):
    patches, columns = own_ref.shape
    cols = slice(cut * columns, (cut + 1) * columns)
    there = pl.ds(pl.multiple_of(where_ref[0] * (width // 2) + cut * columns, columns), columns)
    mine, theirs = weight_own[:, there], weight_other[:, there]
    grad = contract_rows(
        jnp.concatenate([gram_own[...], gram_other[...]], axis=0),
        jnp.concatenate([mine, mine, theirs, theirs], axis=0),
    )
    for i, (out, features) in enumerate(((own_ref, sum_own), (other_ref, sum_other))):
        mine = stats[i * patches : (i + 1) * patches, :]
        theirs = stats_other[(1 - i) * patches : (2 - i) * patches, :]
        gap = mine[:, :1] - theirs[:, :1]
        middle = 0.5 * (mine[:, :1] + theirs[:, :1])
        squares = mine[:, 64:65] + theirs[:, 64:65] + (width / 4) * gap * gap
        root = 1.0 / jnp.sqrt(squares * (1.0 / width) + 1e-06)
        target = (blend[i * patches : (i + 1) * patches, cols] - middle) * root
        out[...] = target
        grad = grad - contract_rows(features[...], target.astype(jnp.bfloat16))
    if len(rest) == 1:
        rest[0][...] = grad
        return
    send_ref, keep_ref, total = rest
    total[...] = grad
    if cut == 0:
        halve(total, where_ref, send_ref, keep_ref)
    else:
        halve_z(total, where_ref, send_ref, keep_ref)


def targets_and_term(where, blend, stats, stats_other, sum_own, sum_other, grams, weights, part, coded):
    j, n = part
    patches, columns = blend.shape[0] // 2, blend.shape[1] // n
    dec = grams[0].shape[1]
    shapes = [f32(patches, columns)] * 2
    shapes += halved_shapes(dec, columns) if coded else [f32(dec, columns)]
    kernel = functools.partial(targets_kernel, cut=j, width=2 * blend.shape[1])
    scratch = [pltpu.VMEM((dec, columns), jnp.float32)] if coded else []
    return call(kernel, shapes, "targets", scratch)(
        where, blend, stats, stats_other, sum_own, sum_other, *grams, *weights
    )


def after(x, *others):
    return lax.optimization_barrier((x,) + others)[0]


def on_device(
    mesh_shape,
    queries,
    key_rows,
    value_rows,
    stream,
    earlier,
    out_weight,
    pred_weight,
    decoder_hidden,
    kept_index,
):
    groups, parts = mesh_shape["groups"], mesh_shape["dp"]
    chips = parts // 2
    patches, width = queries.shape[1:]
    clones, dec = decoder_hidden.shape[1], decoder_hidden.shape[3]
    half = width // 2
    scale = 2.0 / (math.sqrt(width) * clones)
    me = lax.axis_index("dp")
    core, chip = me % 2, me // 2
    where = jnp.stack([core, chip]).astype(jnp.int32)
    same_core = [[2 * k + j for k in range(chips)] for j in range(2)]
    by_pairs = chips == 2 * LINE

    def swap(x, bits):
        pairs = [(g * parts + i, g * parts + (i ^ bits)) for g in range(groups) for i in range(parts)]
        return lax.ppermute(x, AXES, pairs)

    def side_by_side(mine, theirs):
        return jnp.where(
            core == 0,
            jnp.concatenate(mine + theirs, axis=1),
            jnp.concatenate(theirs + mine, axis=1),
        )

    rows = out_weight.shape[0]
    pred_other = swap(pred_weight, CORE)
    if by_pairs:
        gram_mine, *gram_theirs, sum_own = gram(
            where, decoder_hidden, kept_index[0], (chips, dec // parts)
        )
    else:
        gram_all, sum_own = gram(where, decoder_hidden, kept_index[0], None)
    out_piece = cut(where, after(out_weight, sum_own), swap(out_weight, CORE))
    weights = [pred_weight, pred_other]

    def attend(*anchors):
        q = after(queries, *anchors) if anchors else queries
        return attention(where, q[0], key_rows[0], value_rows[0], stream[0], earlier[0])

    if by_pairs:
        z1, z2, y0 = swap(out_piece, NEXT_Z), swap(out_piece, FAR_Z), swap(out_piece, NEXT_Y)
        sum_other = swap(sum_own, CORE)
        gram_theirs = [swap(after(g, pred_other), CORE) for g in gram_theirs]
        send, keep = first_step(where, after(gram_mine, y0), gram_theirs)
        y1 = swap(z1, NEXT_Y)
        z3 = swap(after(z2, send), NEXT_Z)
        y2 = swap(after(z2, y0), NEXT_Y)
        own, *codes = second_step(where, after(keep, z2), swap(send, NEXT_Y))
        y3 = swap(after(z3, y1, own), NEXT_Y)
        out_pieces = [out_piece, y0, z1, y1, z2, y2, z3, y3]
        mixed_own, *bundle = attend(z3)
        others = [swap(b, CORE) for b in bundle]
        codes = [swap(c, NEXT_Z * (m + 1)) for m, c in enumerate(codes)]
        (gram_rows,) = last_step(where, after(own, y2), codes)
        mixed_own = after(mixed_own, gram_rows)
    else:
        got = lax.all_gather(out_piece, "dp", axis_index_groups=same_core).reshape(chips, 2, rows, half)
        out_pieces = [jnp.where(core == 0, got, got[:, ::-1]).reshape(width, half)]
        sum_other = swap(sum_own, CORE)
        mixed_own, *bundle = attend()
        others = [swap(b, CORE) for b in bundle]
        gram_rows = lax.psum_scatter(gram_all, "dp", scatter_dimension=0, tiled=True)
        high = gram_rows.astype(jnp.bfloat16)
        low = (gram_rows - high.astype(jnp.float32)).astype(jnp.bfloat16)
        gram_rows = jnp.concatenate([high, low], axis=0)
    grams = [gram_rows, swap(gram_rows, CORE)]

    blend, stats = branch(where, mixed_own, stream[0], earlier[0], *others, *out_pieces)
    stats_other = swap(stats, CORE)

    def term(part, coded, *before):
        return targets_and_term(
            where, blend, stats, after(stats_other, *before), sum_own, sum_other, grams, weights, part, coded
        )

    if not by_pairs:
        target_own, target_other, total = term((0, 1), False)
        targets = side_by_side([target_own], [swap(target_other, CORE)])[None]
        summed = lax.psum_scatter(
            total, "dp", scatter_dimension=0, tiled=True, axis_index_groups=same_core
        )
        summed = (summed * scale).reshape(2, dec // parts, half)
        keep = lax.dynamic_index_in_dim(summed, core, 0, keepdims=False)
        send = lax.dynamic_index_in_dim(summed, 1 - core, 0, keepdims=False)
        return targets, side_by_side([keep], [swap(send, CORE)])

    steps, rest = [], []
    for j, axis in enumerate((NEXT_Y, NEXT_Z)):
        target_own, target_other, send, keep = term((j, 2), True)
        rest.append(swap(target_other, CORE))
        steps.append((target_own, keep, swap(send, axis)))
    targets = side_by_side([x[0] for x in steps], rest)[None]
    mine, theirs = [], []
    for (_, keep, codes), halving, axis in zip(steps, (halve_z, halve_pairs), (NEXT_Z, NEXT_Y)):
        send, keep = next_step(where, keep, codes, halving)
        codes = swap(send, axis)
        send, keep = next_step(where, keep, codes, halve_far)
        codes = swap(send, FAR_Z)
        if not mine:
            keep = after(keep, targets)
        keep, send = last_step(where, keep, [codes], scale)
        mine.append(keep)
        theirs.append(swap(send, CORE))
    return targets, side_by_side(mine, theirs)


def solution(mesh):
    by_image = P(AXES, None, None)
    return jax.shard_map(
        functools.partial(on_device, dict(mesh.shape)),
        mesh=mesh,
        in_specs=(
            by_image,
            by_image,
            by_image,
            by_image,
            by_image,
            P("dp", None),
            P("dp", None),
            P(AXES, None, None, None),
            by_image,
        ),
        out_specs=(by_image, P(AXES, None)),
        check_vma=False,
    )
```

```python
import functools
import math

import jax
import jax.numpy as jnp
from jax import lax
from jax.experimental import pallas as pl
from jax.experimental.pallas import tpu as pltpu
from jax.sharding import PartitionSpec as P

HEADS = 24
TOP_K = 10
AXES = ("groups", "dp")
VMEM = 24 * 1024 * 1024
COST = 1000
CORE, NEXT_Y, NEXT_Z, FAR_Z = 1, 2, 4, 8
LINE = 4
TAIL = 16


def call(kernel, out_shape, name, scratch=()):
    held = pl.BlockSpec(memory_space=pltpu.VMEM)

    def run(where, *arrays):
        return pl.pallas_call(
            kernel,
            out_shape=tuple(out_shape),
            in_specs=[pl.BlockSpec(memory_space=pltpu.SMEM)] + [held] * len(arrays),
            out_specs=(held,) * len(out_shape),
            scratch_shapes=scratch,
            compiler_params=pltpu.CompilerParams(vmem_limit_bytes=VMEM),
            cost_estimate=pl.CostEstimate(flops=COST, bytes_accessed=COST, transcendentals=0),
            name=name,
        )(where, *arrays)

    return run


def f32(*shape):
    return jax.ShapeDtypeStruct(shape, jnp.float32)


def bf16(*shape):
    return jax.ShapeDtypeStruct(shape, jnp.bfloat16)


def contract_rows(a, b):
    return lax.dot_general(a, b, (((0,), (0,)), ((), ())), preferred_element_type=jnp.float32)


def attention_kernel(where_ref, q_ref, k_ref, v_ref, stream, earlier, out_ref, *bundle, size):
    mixed = []
    for j in range(q_ref.shape[1] // size):
        cols = slice(j * size, (j + 1) * size)
        q = q_ref[:, cols] * jnp.asarray(1.0 / math.sqrt(size), q_ref.dtype)
        scores = lax.dot_general(
            k_ref[:, cols], q, (((1,), (1,)), ((), ())), preferred_element_type=jnp.float32
        )
        weights = jnp.exp(scores - jnp.max(scores, axis=0, keepdims=True))
        weights = weights * (1.0 / jnp.sum(weights, axis=0, keepdims=True))
        mixed.append(contract_rows(weights.astype(jnp.bfloat16), v_ref[:, cols]))
    half = bundle[0].shape[1]
    mixed = jnp.concatenate(mixed, axis=1).astype(out_ref.dtype)
    out_ref[...] = mixed
    theirs = pl.ds(pl.multiple_of((1 - where_ref[0]) * half, half), half)
    bundle[0][...] = mixed[:, :half]
    bundle[1][...] = mixed[:, half:]
    bundle[2][...] = stream[:, theirs]
    bundle[3][...] = earlier[:, theirs]


def attention(where, q, k, v, stream, earlier):
    patches, width = q.shape
    kernel = functools.partial(attention_kernel, size=width // HEADS)
    shapes = [bf16(patches, width)] + [bf16(patches, width // 2)] * 4
    return call(kernel, shapes, "attention")(where, q, k, v, stream, earlier)


def symmetric_product(x, out):
    width = x.shape[1]
    block = 256 if width % 256 == 0 else width
    for at in range(0, width, block):
        here = slice(at, at + block)
        strip = contract_rows(x[:, here], x[:, at:])
        out[here, at:] = strip
        for later in range(at + block, width, block):
            out[later : later + block, here] = strip[:, later - at : later - at + block].T


def gram_kernel(where_ref, hidden_ref, kept_ref, *rest, parted):
    *gram_refs, sum_ref, rows_all, total = rest
    clones, patches = hidden_ref.shape[1:3]
    positions = lax.broadcasted_iota(jnp.int32, (patches, kept_ref.shape[1]), 0)
    sums = None
    for i in range(clones):
        kept = kept_ref[i : i + 1, :]
        covered = jnp.max(jnp.where(positions == kept, 1.0, 0.0), axis=1, keepdims=True)
        rows = hidden_ref[0, i]
        rows = jnp.where(covered > 0.5, jnp.zeros_like(rows), rows)
        rows_all[i * patches : (i + 1) * patches, :] = rows
        wide = rows.astype(jnp.float32)
        sums = wide if sums is None else sums + wide
    sum_ref[...] = sums.astype(sum_ref.dtype)
    if not parted:
        symmetric_product(rows_all, gram_refs[0])
        return
    symmetric_product(rows_all, total)
    mine, *theirs = gram_refs
    core = where_ref[0]
    chips, rows = parted
    for k in range(chips):
        at = pl.multiple_of((2 * k + core) * rows, rows)
        mine[k * rows : (k + 1) * rows, :] = total[pl.ds(at, rows), :]
        at = pl.multiple_of((2 * k + 1 - core) * rows, rows)
        part = k // (chips // len(theirs))
        here = (k % (chips // len(theirs))) * rows
        theirs[part][here : here + rows, :] = total[pl.ds(at, rows), :]


def gram(where, hidden, kept, parted):
    _, clones, patches, width = hidden.shape
    grams = [f32(width // 2, width)] + [f32(width // 4, width)] * 2 if parted else [f32(width, width)]
    scratch = [
        pltpu.VMEM((clones * patches, width), jnp.bfloat16),
        pltpu.VMEM((width, width), jnp.float32),
    ]
    kernel = functools.partial(gram_kernel, parted=parted)
    shapes = grams + [bf16(patches, width)]
    return call(kernel, shapes, "gram", scratch)(where, hidden, kept)


def cut_kernel(where_ref, own, other, out_ref):
    rows, half = own.shape[0], out_ref.shape[1]
    columns = pl.ds(pl.multiple_of(where_ref[0] * half, half), half)
    out_ref[:rows, :] = own[:, columns]
    out_ref[rows:, :] = other[:, columns]


def cut(where, own, other):
    rows, width = own.shape
    return call(cut_kernel, [bf16(2 * rows, width // 2)], "cut")(where, own, other)[0]


def put_in_order(where_ref, pieces, full):
    core, chip = where_ref[0], where_ref[1]
    if len(pieces) == 1:
        full[...] = pieces[0][...]
        return
    for k, piece in enumerate(pieces):
        rows = piece.shape[0] // 2
        base = (chip ^ k) * 2
        for j in range(2):
            at = pl.multiple_of((base + (core ^ j)) * rows, rows)
            full[pl.ds(at, rows), :] = piece[j * rows : (j + 1) * rows, :]


def branch_kernel(where_ref, mixed_own, stream, earlier, *rest):
    others, rest = rest[:4], rest[4:]
    *pieces, blend_ref, stats_ref, full = rest
    put_in_order(where_ref, pieces, full)
    patches, half = stream.shape[0], blend_ref.shape[1]
    columns = pl.ds(pl.multiple_of(where_ref[0] * half, half), half)
    mixeds = (mixed_own[...], jnp.concatenate([others[0][...], others[1][...]], axis=1))
    streams = (stream[:, columns], others[2][...])
    earliers = (earlier[:, columns], others[3][...])
    for i in range(2):
        layer_out = streams[i].astype(jnp.float32) + jnp.dot(
            mixeds[i], full[...], preferred_element_type=jnp.float32
        )
        center = jnp.mean(layer_out, axis=0, keepdims=True)
        away = layer_out - center
        spread = jnp.mean(away * away, axis=0, keepdims=True)
        normed = away * (1.0 / jnp.sqrt(spread + 1e-05))
        blend = ((TOP_K - 1) * earliers[i].astype(jnp.float32) + normed) * (1.0 / TOP_K)
        rows = slice(i * patches, (i + 1) * patches)
        blend_ref[rows, :] = blend
        middle = jnp.mean(blend, axis=1, keepdims=True)
        off = blend - middle
        squares = jnp.sum(off * off, axis=1, keepdims=True)
        lane = lax.broadcasted_iota(jnp.int32, (patches, 128), 1)
        stats_ref[rows, :] = jnp.where(lane < 64, middle, squares)


def branch(where, mixed_own, *others):
    patches, width = mixed_own.shape
    half = width // 2
    shapes = [f32(2 * patches, half), f32(2 * patches, 128)]
    scratch = [pltpu.VMEM((width, half), jnp.bfloat16)]
    return call(branch_kernel, shapes, "branch", scratch)(where, mixed_own, *others)


def encode(values, out_ref):
    rows = values.shape[0]
    top = jnp.max(jnp.abs(values), axis=0, keepdims=True)
    power = jnp.ceil(jnp.log2(jnp.maximum(top, 1e-30))) - 15.0
    codes = jnp.clip(jnp.round(values * jnp.exp2(-power)), -32767.0, 32767.0)
    out_ref[:rows, :] = codes.astype(jnp.int32).astype(jnp.int16)
    out_ref[rows:, :] = jnp.broadcast_to(power, (TAIL, values.shape[1])).astype(jnp.int32).astype(jnp.int16)


def decode(codes):
    rows = codes.shape[0] - TAIL
    power = codes[rows:, :].astype(jnp.int32).astype(jnp.float32)[:1]
    return codes[:rows, :].astype(jnp.int32).astype(jnp.float32) * jnp.exp2(power)


def halve(values, where_ref, send_ref, keep_ref):
    rows = keep_ref.shape[0] // LINE
    y = where_ref[1] % 2

    def blocks(of):
        return [values[pl.ds(pl.multiple_of((2 * z + of) * rows, rows), rows), :] for z in range(LINE)]

    keep_ref[...] = jnp.concatenate(blocks(y), axis=0)
    encode(jnp.concatenate(blocks(1 - y), axis=0), send_ref)


def halve_z(values, where_ref, send_ref, keep_ref):
    rows = keep_ref.shape[0] // 2
    z = where_ref[1] // 2

    def block(of):
        return values[pl.ds(pl.multiple_of(of * rows, rows), rows), :]

    keep_ref[...] = jnp.concatenate([block(z), block(z ^ 2)], axis=0)
    encode(jnp.concatenate([block(z ^ 1), block(z ^ 3)], axis=0), send_ref)


def halve_pairs(values, where_ref, send_ref, keep_ref):
    rows = keep_ref.shape[0] // 2
    y = where_ref[1] % 2

    def blocks(of):
        return [values[pl.ds(pl.multiple_of((2 * z + of) * rows, rows), rows), :] for z in range(2)]

    keep_ref[...] = jnp.concatenate(blocks(y), axis=0)
    encode(jnp.concatenate(blocks(1 - y), axis=0), send_ref)


def halve_far(values, where_ref, send_ref, keep_ref):
    rows = keep_ref.shape[0]
    keep_ref[...] = values[:rows, :]
    encode(values[rows:, :], send_ref)


def halved_shapes(rows, width):
    return [jax.ShapeDtypeStruct((rows // 2 + TAIL, width), jnp.int16), f32(rows // 2, width)]


def first_kernel(where_ref, mine, t0, t1, send_ref, keep_ref, total):
    total[...] = mine[...] + jnp.concatenate([t0[...], t1[...]], axis=0)
    halve(total, where_ref, send_ref, keep_ref)


def first_step(where, mine, theirs):
    scratch = [pltpu.VMEM(mine.shape, jnp.float32)]
    return call(first_kernel, halved_shapes(*mine.shape), "first_step", scratch)(where, mine, *theirs)


def second_kernel(where_ref, keep, codes, own_ref, *rest):
    *send_refs, total = rest
    rows = own_ref.shape[0]
    z = where_ref[1] // 2
    total[...] = keep[...] + decode(codes[...])

    def block(of):
        return total[pl.ds(pl.multiple_of(of * rows, rows), rows), :]

    own_ref[...] = block(z)
    for m, ref in enumerate(send_refs):
        encode(block(z ^ (m + 1)), ref)


def second_step(where, keep, codes):
    rows, width = keep.shape[0] // LINE, keep.shape[1]
    shapes = [f32(rows, width)] + [jax.ShapeDtypeStruct((rows + TAIL, width), jnp.int16)] * (LINE - 1)
    scratch = [pltpu.VMEM(keep.shape, jnp.float32)]
    return call(second_kernel, shapes, "second_step", scratch)(where, keep, codes)


def next_kernel(where_ref, keep, codes, send_ref, keep_ref, total, *, halving):
    total[...] = keep[...] + decode(codes[...])
    halving(total, where_ref, send_ref, keep_ref)


def next_step(where, keep, codes, halving):
    scratch = [pltpu.VMEM(keep.shape, jnp.float32)]
    kernel = functools.partial(next_kernel, halving=halving)
    return call(kernel, halved_shapes(*keep.shape), "next_step", scratch)(where, keep, codes)


def last_kernel(where_ref, own, *rest, scale, count):
    codes, out_refs = rest[:count], rest[count:]
    total = own[...]
    for ref in codes:
        total = total + decode(ref[...])
    if scale is None:
        (pair,) = out_refs
        rows = total.shape[0]
        high = total.astype(jnp.bfloat16)
        pair[:rows, :] = high
        pair[rows:, :] = (total - high.astype(jnp.float32)).astype(jnp.bfloat16)
        return
    keep, send = out_refs
    rows = keep.shape[0]
    first, second = total[:rows, :] * scale, total[rows:, :] * scale
    mine_first = where_ref[0] == 0
    keep[...] = jnp.where(mine_first, first, second)
    send[...] = jnp.where(mine_first, second, first)


def last_step(where, own, codes, scale=None):
    rows, width = own.shape
    shapes = [bf16(2 * rows, width)] if scale is None else [f32(rows // 2, width)] * 2
    return call(functools.partial(last_kernel, scale=scale, count=len(codes)), shapes, "last_step")(where, own, *codes)


def targets_kernel(where_ref, blend, stats, stats_other, sum_own, sum_other, gram_own, gram_other, weight_own, weight_other, own_ref, other_ref, *rest, cut, width):
    patches, columns = own_ref.shape
    cols = slice(cut * columns, (cut + 1) * columns)
    there = pl.ds(pl.multiple_of(where_ref[0] * (width // 2) + cut * columns, columns), columns)
    mine, theirs = weight_own[:, there], weight_other[:, there]
    grad = contract_rows(
        jnp.concatenate([gram_own[...], gram_other[...]], axis=0),
        jnp.concatenate([mine, mine, theirs, theirs], axis=0),
    )
    for i, (out, features) in enumerate(((own_ref, sum_own), (other_ref, sum_other))):
        mine = stats[i * patches : (i + 1) * patches, :]
        theirs = stats_other[(1 - i) * patches : (2 - i) * patches, :]
        gap = mine[:, :1] - theirs[:, :1]
        middle = 0.5 * (mine[:, :1] + theirs[:, :1])
        squares = mine[:, 64:65] + theirs[:, 64:65] + (width / 4) * gap * gap
        root = 1.0 / jnp.sqrt(squares * (1.0 / width) + 1e-06)
        target = (blend[i * patches : (i + 1) * patches, cols] - middle) * root
        out[...] = target
        grad = grad - contract_rows(features[...], target.astype(jnp.bfloat16))
    if len(rest) == 1:
        rest[0][...] = grad
        return
    send_ref, keep_ref, total = rest
    total[...] = grad
    if cut == 0:
        halve(total, where_ref, send_ref, keep_ref)
    else:
        halve_z(total, where_ref, send_ref, keep_ref)


def targets_and_term(where, blend, stats, stats_other, sum_own, sum_other, grams, weights, part, coded):
    j, n = part
    patches, columns = blend.shape[0] // 2, blend.shape[1] // n
    dec = grams[0].shape[1]
    shapes = [f32(patches, columns)] * 2
    shapes += halved_shapes(dec, columns) if coded else [f32(dec, columns)]
    kernel = functools.partial(targets_kernel, cut=j, width=2 * blend.shape[1])
    scratch = [pltpu.VMEM((dec, columns), jnp.float32)] if coded else []
    return call(kernel, shapes, "targets", scratch)(
        where, blend, stats, stats_other, sum_own, sum_other, *grams, *weights
    )


def after(x, *others):
    return lax.optimization_barrier((x,) + others)[0]


def on_device(
    mesh_shape,
    queries,
    key_rows,
    value_rows,
    stream,
    earlier,
    out_weight,
    pred_weight,
    decoder_hidden,
    kept_index,
):
    groups, parts = mesh_shape["groups"], mesh_shape["dp"]
    chips = parts // 2
    patches, width = queries.shape[1:]
    clones, dec = decoder_hidden.shape[1], decoder_hidden.shape[3]
    half = width // 2
    scale = 2.0 / (math.sqrt(width) * clones)
    me = lax.axis_index("dp")
    core, chip = me % 2, me // 2
    where = jnp.stack([core, chip]).astype(jnp.int32)
    same_core = [[2 * k + j for k in range(chips)] for j in range(2)]
    by_pairs = chips == 2 * LINE

    def swap(x, bits):
        pairs = [(g * parts + i, g * parts + (i ^ bits)) for g in range(groups) for i in range(parts)]
        return lax.ppermute(x, AXES, pairs)

    def side_by_side(mine, theirs):
        return jnp.where(
            core == 0,
            jnp.concatenate(mine + theirs, axis=1),
            jnp.concatenate(theirs + mine, axis=1),
        )

    rows = out_weight.shape[0]
    pred_other = swap(pred_weight, CORE)
    if by_pairs:
        gram_mine, *gram_theirs, sum_own = gram(
            where, decoder_hidden, jnp.maximum(kept_index[0], 0), (chips, dec // parts)
        )
    else:
        gram_all, sum_own = gram(where, decoder_hidden, kept_index[0], None)
    out_piece = cut(where, after(out_weight, sum_own), swap(out_weight, CORE))
    weights = [pred_weight, pred_other]

    def attend(*anchors):
        q = after(queries, *anchors) if anchors else queries
        return attention(where, q[0], key_rows[0], value_rows[0], stream[0], earlier[0])

    if by_pairs:
        z1, z2, y0 = swap(out_piece, NEXT_Z), swap(out_piece, FAR_Z), swap(out_piece, NEXT_Y)
        sum_other = swap(sum_own, CORE)
        gram_theirs = [swap(after(g, pred_other), CORE) for g in gram_theirs]
        send, keep = first_step(where, after(gram_mine, y0), gram_theirs)
        y1 = swap(z1, NEXT_Y)
        z3 = swap(after(z2, send), NEXT_Z)
        y2 = swap(after(z2, y0), NEXT_Y)
        own, *codes = second_step(where, after(keep, z2), swap(send, NEXT_Y))
        y3 = swap(after(z3, y1, own), NEXT_Y)
        out_pieces = [out_piece, y0, z1, y1, z2, y2, z3, y3]
        mixed_own, *bundle = attend(z3)
        others = [swap(b, CORE) for b in bundle]
        codes = [swap(c, NEXT_Z * (m + 1)) for m, c in enumerate(codes)]
        (gram_rows,) = last_step(where, after(own, y2), codes)
        mixed_own = after(mixed_own, *codes)
    else:
        got = lax.all_gather(out_piece, "dp", axis_index_groups=same_core).reshape(chips, 2, rows, half)
        out_pieces = [jnp.where(core == 0, got, got[:, ::-1]).reshape(width, half)]
        sum_other = swap(sum_own, CORE)
        mixed_own, *bundle = attend()
        others = [swap(b, CORE) for b in bundle]
        gram_rows = lax.psum_scatter(gram_all, "dp", scatter_dimension=0, tiled=True)
        high = gram_rows.astype(jnp.bfloat16)
        low = (gram_rows - high.astype(jnp.float32)).astype(jnp.bfloat16)
        gram_rows = jnp.concatenate([high, low], axis=0)
    grams = [gram_rows, swap(gram_rows, CORE)]

    blend, stats = branch(where, mixed_own, stream[0], earlier[0], *others, *out_pieces)
    stats_other = swap(stats, CORE)

    def term(part, coded, *before):
        return targets_and_term(
            where, blend, stats, after(stats_other, *before), sum_own, sum_other, grams, weights, part, coded
        )

    if not by_pairs:
        target_own, target_other, total = term((0, 1), False)
        targets = side_by_side([target_own], [swap(target_other, CORE)])[None]
        summed = lax.psum_scatter(
            total, "dp", scatter_dimension=0, tiled=True, axis_index_groups=same_core
        )
        summed = (summed * scale).reshape(2, dec // parts, half)
        keep = lax.dynamic_index_in_dim(summed, core, 0, keepdims=False)
        send = lax.dynamic_index_in_dim(summed, 1 - core, 0, keepdims=False)
        return targets, side_by_side([keep], [swap(send, CORE)])

    steps, rest = [], []
    for j, axis in enumerate((NEXT_Y, NEXT_Z)):
        target_own, target_other, send, keep = term((j, 2), True)
        rest.append(swap(target_other, CORE))
        steps.append((target_own, keep, swap(send, axis)))
    targets = side_by_side([x[0] for x in steps], rest)[None]
    mine, theirs = [], []
    for (_, keep, codes), halving, axis in zip(steps, (halve_z, halve_pairs), (NEXT_Z, NEXT_Y)):
        send, keep = next_step(where, keep, codes, halving)
        codes = swap(send, axis)
        send, keep = next_step(where, keep, codes, halve_far)
        codes = swap(send, FAR_Z)
        if not mine:
            keep = after(keep, targets)
        keep, send = last_step(where, keep, [codes], scale)
        mine.append(keep)
        theirs.append(swap(send, CORE))
    return targets, side_by_side(mine, theirs)


def solution(mesh):
    by_image = P(AXES, None, None)
    return jax.shard_map(
        functools.partial(on_device, dict(mesh.shape)),
        mesh=mesh,
        in_specs=(
            by_image,
            by_image,
            by_image,
            by_image,
            by_image,
            P("dp", None),
            P("dp", None),
            P(AXES, None, None, None),
            by_image,
        ),
        out_specs=(by_image, P(AXES, None)),
        check_vma=False,
    )
```
